32 devices in a mesh: dp: 8 (over z, y), mp: 4 (over x, core).
Axes of the slice: x: 2, y: 2, z: 4, core: 2. Of those that a mesh axis runs over, the one named last changes fastest.
Arguments:
- hidden_in: bfloat16 [8192, 1536], P(('dp', 'mp')), may hold values from -6 to 6
- out_grad: bfloat16 [8192, 1536], P(('dp', 'mp')), may hold values from -6 to 6
- seq_lengths: int32 [8, 8], P('dp'), may hold values from 1 to 896, as said below
- seq_grains: int32 [8, 8], P('dp'), may hold values from 0 to 3
- gain_attn: bfloat16 [1536], P(('dp', 'mp')), may hold values from 0.5 to 1.5
- w_qkv: bfloat16 [1536, 3, 1536], P('dp', None, 'mp'), may hold values from -0.15625 to 0.15625
- w_out: bfloat16 [1536, 1536], P('mp', 'dp'), may hold values from -1.25 to 1.25
- gain_ffn: bfloat16 [1536], P(('dp', 'mp')), may hold values from 0.5 to 1.5
- w_up: bfloat16 [1536, 6144], P('dp', 'mp'), may hold values from -0.15625 to 0.15625
- bias_up: bfloat16 [6144], P(('mp', 'dp')), may hold values from -3 to 3
- w_down: bfloat16 [6144, 1536], P('mp', 'dp'), may hold values from -0.078125 to 0.078125
- bias_down: bfloat16 [1536], P(('dp', 'mp')), may hold values from -3 to 3
Outputs:
- output: bfloat16 [8192, 1536], P(('dp', 'mp'))
- grad_in: float32 [8192, 1536], P(('dp', 'mp'))
- grad_gain_attn: float32 [1536], P(('dp', 'mp'))
- grad_w_qkv: float32 [1536, 3, 1536], P('dp', None, 'mp')
- grad_w_out: float32 [1536, 1536], P('mp', 'dp')
- grad_gain_ffn: float32 [1536], P(('dp', 'mp'))
- grad_w_up: float32 [1536, 6144], P('dp', 'mp')
- grad_bias_up: float32 [6144], P(('mp', 'dp'))
- grad_w_down: float32 [6144, 1536], P('mp', 'dp')
- grad_bias_down: float32 [1536], P(('dp', 'mp'))
The draws below stay inside these ranges and needn't reach their ends.
Inputs may be any that keep to these rules, and one draw needn't show every extreme that they name: `seq_lengths`: each row sums to 1024; exactly one entry of each row equals 896, the others sum to 128. `seq_grains`: granularity g uses the first 768 * 2 ** g hidden units.
All inputs are finite; a program needn't handle non-finite values.
Results may differ from the reference program's by a relative error of at most 0.015.
Values may be sent and summed in bfloat16 or wider, within the bound.
A program may use at most 192 MiB of HBM per device.

```python
import jax
import jax.numpy as jnp
from jax import lax

D = 1536
HEADS = 12
HEAD = 128
FF = 6144
TOK_DEV = 1024
SEQS = 8
GRAIN = 768
MAXLEN = 896
SHORT_TOTAL = 128
TOKENS = 8192
N_DP = 8


def one_group(key):
    slot_key, cut_key = jax.random.split(key)
    long_slot = jax.random.randint(slot_key, (), 0, SEQS)
    picked = jax.random.permutation(cut_key, SHORT_TOTAL - 1)[:SEQS - 2] + 1
    cut_points = jnp.sort(picked.astype(jnp.int32))
    boundaries = jnp.concatenate([jnp.zeros((1,), jnp.int32), cut_points, jnp.full((1,), SHORT_TOTAL, jnp.int32)])
    short_lengths = boundaries[1:] - boundaries[:-1]
    slot_index = jnp.arange(SEQS, dtype=jnp.int32)
    source_slot = jnp.clip(slot_index - (slot_index > long_slot).astype(jnp.int32), 0, SEQS - 2)
    return jnp.where(slot_index == long_slot, MAXLEN, short_lengths[source_slot]).astype(jnp.int32)


def draw_seq_lengths(key, part):
    key = jax.random.fold_in(key, 11)
    group_keys = jax.random.split(key, TOKENS // TOK_DEV)
    return jax.vmap(one_group)(group_keys)


def touch_ends(entries, key, least, largest):
    spot = [jax.random.randint(jax.random.fold_in(key, axis), (), 0, length) for axis, length in enumerate(entries.shape)]
    widest = entries.shape.index(max(entries.shape))
    neighbour = spot[:widest] + [(spot[widest] + 1) % entries.shape[widest]] + spot[widest + 1:]
    return entries.at[tuple(spot)].set(least).at[tuple(neighbour)].set(largest)


def block_scale(stream_key, dims, cuts, smallest, top_value):
    def one(axis_at, shards_of):
        steps = jax.random.uniform(jax.random.fold_in(jax.random.fold_in(stream_key, 6), axis_at), (shards_of,), jnp.float32, smallest / len(cuts), top_value / len(cuts))
        return jnp.repeat(jnp.exp(steps), dims[axis_at] // shards_of).reshape((-1,) + (1,) * (len(dims) - axis_at - 1))

    loudness = one(*cuts[0])
    for cut in cuts[1:]:
        loudness = loudness * one(*cut)
    return loudness


def normal_values(rng, extent, scale, most, cuts=(), kind=jnp.bfloat16):
    level = block_scale(rng, extent, cuts, -0.22, 0.18) if cuts else 1.0
    result = jax.random.normal(rng, extent, jnp.float32) * scale * level
    return jnp.minimum(jnp.maximum(result, -most), most).astype(kind)


def setup_inputs(seed: int = 0) -> dict:
    arg_keys = jax.random.split(jax.random.key(seed), 13)
    hidden_in = normal_values(arg_keys[0], (TOKENS, D), 1.0, 6.0, ((0, 32),))
    out_grad = normal_values(arg_keys[1], (TOKENS, D), 1.0, 6.0, ((0, 32),))
    seq_lengths = draw_seq_lengths(jax.random.fold_in(arg_keys[12], 71), 0)
    seq_grains = touch_ends(jax.random.randint(arg_keys[3], (N_DP, SEQS), 0, 4), jax.random.fold_in(arg_keys[3], 1), 0, 3).astype(jnp.int32)
    gain_attn = jnp.clip(1.0 + 0.1 * jax.random.normal(arg_keys[4], (D,), jnp.float32), 0.5, 1.5).astype(jnp.bfloat16)
    w_qkv = normal_values(arg_keys[5], (D, 3, D), D ** -0.5, 0.15625, ((0, 8), (2, 4)))
    w_out = normal_values(arg_keys[6], (D, D), (D // 64) ** -0.5, 1.25, ((0, 4), (1, 8)))
    gain_ffn = jnp.clip(1.0 + 0.1 * jax.random.normal(arg_keys[7], (D,), jnp.float32), 0.5, 1.5).astype(jnp.bfloat16)
    w_up = normal_values(arg_keys[8], (D, FF), D ** -0.5, 0.15625, ((0, 8), (1, 4)))
    bias_up = normal_values(arg_keys[9], (FF,), 0.5, 3.0, ((0, 32),))
    w_down = normal_values(arg_keys[10], (FF, D), FF ** -0.5, 0.078125, ((0, 4), (1, 8)))
    bias_down = normal_values(arg_keys[11], (D,), 0.5, 3.0, ((0, 32),))
    return {"hidden_in": hidden_in, "out_grad": out_grad, "seq_lengths": seq_lengths, "seq_grains": seq_grains, "gain_attn": gain_attn, "w_qkv": w_qkv, "w_out": w_out, "gain_ffn": gain_ffn, "w_up": w_up, "bias_up": bias_up, "w_down": w_down, "bias_down": bias_down}


norm_eps = 1e-06
rope_base = 10000.0
highest = lax.Precision.HIGHEST

@jax.custom_vjp
def low(v):
    return lax.optimization_barrier(v.astype(jnp.bfloat16)).astype(jnp.float32)

@jax.custom_vjp
def low_back(v):
    return v

def low_keep(v):
    return (low(v), None)

def low_pass(kept, grad):
    return (grad,)

def back_keep(v):
    return (v, None)

def back_low(kept, grad):
    return (low(grad),)
low.defvjp(low_keep, low_pass)
low_back.defvjp(back_keep, back_low)

def rope_tables(position, head_size):
    half_count = head_size // 2
    freq_index = jnp.arange(half_count, dtype=jnp.float32)
    inverse = rope_base ** (-2.0 * freq_index / head_size)
    angles = position.astype(jnp.float32)[:, None] * inverse[None, :]
    return (jnp.cos(angles)[:, None, :], jnp.sin(angles)[:, None, :])

def rotate(values, cosine_table, sine_table):
    front_half, back_half = jnp.split(values, 2, axis=-1)
    return jnp.concatenate([front_half * cosine_table - back_half * sine_table, back_half * cosine_table + front_half * sine_table], axis=-1)

def layout(lengths, grains, group_rows):
    seq_ends = jnp.cumsum(lengths).astype(jnp.int32)
    starts = (seq_ends - lengths).astype(jnp.int32)
    token_index = jnp.arange(group_rows, dtype=jnp.int32)
    member = ((token_index[:, None] >= starts[None, :]) & (token_index[:, None] < seq_ends[None, :])).astype(jnp.int32)
    seq_number = jnp.arange(lengths.shape[0], dtype=jnp.int32)
    seq_index = lax.optimization_barrier(jnp.sum(member * seq_number[None, :], axis=1)).astype(jnp.int32)
    position = (token_index - lax.optimization_barrier(jnp.sum(member * starts[None, :], axis=1))).astype(jnp.int32)
    unit_width = lax.optimization_barrier(jnp.sum(member * jnp.left_shift(jnp.int32(GRAIN), grains)[None, :], axis=1)).astype(jnp.int32)
    return (token_index, seq_index, position, unit_width)

def attend_block(pieces, keys_all, values_all, seq_index, token_index):
    query_block, query_seq, query_index = pieces
    scores = jnp.einsum('qhd,khd->hqk', query_block, keys_all, precision=highest) * HEAD ** (-0.5)
    scores = low_back(scores)
    allowed = (query_seq[:, None] == seq_index[None, :]) & (token_index[None, :] <= query_index[:, None])
    scores = jnp.where(allowed[None], scores, -1e+30)
    probabilities = low(jax.nn.softmax(scores, axis=-1))
    return jnp.einsum('hqk,khd->qhd', probabilities, values_all, precision=highest)

def group_forward(hidden, lengths, grains, gain_attn, w_qkv, w_out, gain_ffn, w_up, bias_up, w_down, bias_down):
    token_index, seq_index, position, unit_width = layout(lengths, grains, TOK_DEV)
    scale_one = lax.rsqrt(lax.optimization_barrier(jnp.mean(hidden * hidden, axis=-1, keepdims=True)) + norm_eps)
    normed_one = low(hidden * scale_one * gain_attn)
    mixed_all = low_back(jnp.dot(normed_one, w_qkv.reshape(D, 3 * D), precision=highest))
    mixed_all = mixed_all.reshape(TOK_DEV, 3, HEADS, HEAD)
    cosine_table, sine_table = rope_tables(position, HEAD)
    queries = low(rotate(mixed_all[:, 0], cosine_table, sine_table))
    keys_all = low(rotate(mixed_all[:, 1], cosine_table, sine_table))
    values_all = low(mixed_all[:, 2])
    block_rows = min(512, TOK_DEV)
    block_count = TOK_DEV // block_rows

    def one_block(pieces):
        return attend_block(pieces, keys_all, values_all, seq_index, token_index)
    attended = lax.map(jax.checkpoint(one_block), (queries.reshape(block_count, block_rows, HEADS, HEAD), seq_index.reshape(block_count, block_rows), token_index.reshape(block_count, block_rows)))
    heads_out = low(low_back(attended.reshape(TOK_DEV, D)))
    branch = low_back(jnp.dot(heads_out, w_out, precision=highest))
    middle = hidden + branch
    scale_two = lax.rsqrt(lax.optimization_barrier(jnp.mean(middle * middle, axis=-1, keepdims=True)) + norm_eps)
    normed_two = low(middle * scale_two * gain_ffn)
    pre_act = low_back(jnp.dot(normed_two, w_up, precision=highest) + bias_up)
    unit_mask = (jnp.arange(FF, dtype=jnp.int32)[None, :] < unit_width[:, None]).astype(jnp.float32)
    activated = low(jax.nn.gelu(pre_act) * unit_mask)
    return middle + jnp.dot(activated, w_down, precision=highest) + bias_down

def reference(hidden_in, out_grad, seq_lengths, seq_grains, gain_attn, w_qkv, w_out, gain_ffn, w_up, bias_up, w_down, bias_down):
    params = [one_array.astype(jnp.float32) for one_array in (gain_attn, w_qkv, w_out, gain_ffn, w_up, bias_up, w_down, bias_down)]
    hidden = hidden_in.astype(jnp.float32).reshape(N_DP, TOK_DEV, D)
    cotangent = out_grad.astype(jnp.float32).reshape(N_DP, TOK_DEV, D)
    group_step = jax.checkpoint(group_forward)

    def forward(hidden_all, *weights):

        def group_scan(carried, pieces):
            return (carried, group_step(pieces[0], pieces[1], pieces[2], *weights))
        unused, outputs = lax.scan(group_scan, jnp.zeros((), jnp.float32), (hidden_all, seq_lengths, seq_grains))
        return outputs
    outputs, pullback = jax.vjp(forward, hidden, *params)
    grads = pullback(cotangent)
    return (outputs.reshape(TOKENS, D).astype(jnp.bfloat16), grads[0].reshape(TOKENS, D), grads[1], grads[2], grads[3], grads[4], grads[5], grads[6], grads[7], grads[8])
```

```python
import functools

import jax
import jax.numpy as jnp
from jax import lax
from jax.experimental import pallas as pl
from jax.experimental.pallas import tpu as pltpu
from jax.sharding import PartitionSpec as P

HEAD = 128
GRAIN = 768
MESH = pl.DeviceIdType.MESH

norm_eps = 1e-06
rope_base = 10000.0
masked_score = -1e30
vmem_bytes = 56 * 2**20


def partners(size, step):
    return [(i, i ^ step) for i in range(size)]


def swap(value, axis, step):
    return lax.ppermute(value, axis, partners(lax.axis_size(axis), step))


def gather_dp(shard):
    size = lax.axis_size("dp")
    if size != 8:
        return lax.all_gather(shard, "dp", axis=0, tiled=True)
    me = lax.axis_index("dp")
    rows = shard.shape[0]
    pieces = [shard] + [swap(shard, "dp", 2 * step) for step in (1, 2, 3)]
    near = [swap(piece, "dp", 1) for piece in pieces]
    full = jnp.zeros((size * rows,) + shard.shape[1:], shard.dtype)
    for step in range(4):
        for side, piece in ((0, pieces[step]), (1, near[step])):
            place = jnp.bitwise_xor(me, 2 * step + side)
            full = lax.dynamic_update_slice_in_dim(full, piece, place * rows, 0)
    return full


def scatter_dp(partial):
    size = lax.axis_size("dp")
    rows = partial.shape[0] // size
    if size != 8:
        return lax.psum_scatter(
            partial.astype(jnp.float32), "dp", scatter_dimension=0, tiled=True
        )
    me = lax.axis_index("dp")
    z, y = me // 2, me % 2
    view = partial.reshape(4, 2, rows, partial.shape[1])
    sent = lax.dynamic_index_in_dim(view, 1 - y, 1, keepdims=False)
    kept = lax.dynamic_index_in_dim(view, y, 1, keepdims=False)
    both = kept.astype(jnp.float32) + swap(sent, "dp", 1).astype(jnp.float32)
    low = both.astype(jnp.bfloat16)
    total = lax.dynamic_index_in_dim(low, z, 0, keepdims=False).astype(jnp.float32)
    for step in (1, 2, 3):
        piece = lax.dynamic_index_in_dim(low, jnp.bitwise_xor(z, step), 0, keepdims=False)
        total = total + swap(piece, "dp", 2 * step).astype(jnp.float32)
    return total


def gather_mp(rows):
    core = swap(rows, "mp", 1)
    far = swap(rows, "mp", 2)
    far_core = swap(far, "mp", 1)
    return jnp.concatenate([rows, core, far, far_core], axis=0)


def scatter_mp(left, right):
    block = left.shape[0] // 4
    view = left.reshape(4, block, left.shape[1])

    def product(first, second):
        part = jnp.concatenate([view[first], view[second]], axis=0)
        return jnp.dot(part, right, preferred_element_type=jnp.float32).astype(jnp.bfloat16)

    sent = swap(product(1, 3), "mp", 1)
    both = product(0, 2).astype(jnp.float32) + sent.astype(jnp.float32)
    far = swap(both[block:].astype(jnp.bfloat16), "mp", 2)
    return both[:block] + far.astype(jnp.float32)


def greet(dp, mp, dp_size, mp_size):
    barrier = pltpu.get_barrier_semaphore()
    for step in range(1, mp_size):
        pl.semaphore_signal(barrier, inc=1, device_id=(dp, mp ^ step), device_id_type=MESH)
    for step in range(1, dp_size):
        pl.semaphore_signal(barrier, inc=1, device_id=(dp ^ step, mp), device_id_type=MESH)
    pl.semaphore_wait(barrier, mp_size + dp_size - 2)


def small_gather_kernel(dp_size, mp_size, mine, full, mp_send, mp_recv, dp_send, dp_recv):
    dp, mp = lax.axis_index("dp"), lax.axis_index("mp")
    greet(dp, mp, dp_size, mp_size)
    full[dp, mp] = mine[...]
    copies = []
    for step in range(1, mp_size):
        copy = pltpu.make_async_remote_copy(
            full.at[dp, mp],
            full.at[dp, mp],
            mp_send.at[step - 1],
            mp_recv.at[step - 1],
            device_id=(dp, mp ^ step),
            device_id_type=MESH,
        )
        copy.start()
        copies.append(copy)
    for copy in copies:
        copy.wait()
    copies = []
    for step in range(1, dp_size):
        copy = pltpu.make_async_remote_copy(
            full.at[dp],
            full.at[dp],
            dp_send.at[step - 1],
            dp_recv.at[step - 1],
            device_id=(dp ^ step, mp),
            device_id_type=MESH,
        )
        copy.start()
        copies.append(copy)
    for copy in copies:
        copy.wait()


def small_gather(mine):
    dp_size, mp_size = lax.axis_size("dp"), lax.axis_size("mp")
    return pl.pallas_call(
        functools.partial(small_gather_kernel, dp_size, mp_size),
        out_shape=jax.ShapeDtypeStruct((dp_size, mp_size) + mine.shape, mine.dtype),
        in_specs=[pl.BlockSpec(memory_space=pltpu.VMEM)],
        out_specs=pl.BlockSpec(memory_space=pltpu.VMEM),
        scratch_shapes=[pltpu.SemaphoreType.DMA((mp_size - 1,))] * 2
        + [pltpu.SemaphoreType.DMA((dp_size - 1,))] * 2,
        compiler_params=pltpu.CompilerParams(collective_id=0, has_side_effects=True),
        name="small_gather",
    )(mine)


def small_sum_kernel(
    dp_size, mp_size, mine, total, mp_got, sums, dp_got, mp_send, mp_recv, dp_send, dp_recv
):
    dp, mp = lax.axis_index("dp"), lax.axis_index("mp")
    greet(dp, mp, dp_size, mp_size)
    shared = mp_got.shape[1]
    copies = []
    for step in range(1, mp_size):
        copy = pltpu.make_async_remote_copy(
            mine.at[pl.ds(0, shared)],
            mp_got.at[step - 1],
            mp_send.at[step - 1],
            mp_recv.at[step - 1],
            device_id=(dp, mp ^ step),
            device_id_type=MESH,
        )
        copy.start()
        copies.append(copy)
    for copy in copies:
        copy.wait()
    part = mine[0:shared]
    for step in range(1, mp_size):
        part = part + mp_got[step - 1]
    sums[0:shared] = part
    sums[shared:] = mine[shared:]
    copies = []
    for step in range(1, dp_size):
        copy = pltpu.make_async_remote_copy(
            sums,
            dp_got.at[step - 1],
            dp_send.at[step - 1],
            dp_recv.at[step - 1],
            device_id=(dp ^ step, mp),
            device_id_type=MESH,
        )
        copy.start()
        copies.append(copy)
    for copy in copies:
        copy.wait()
    part = sums[...]
    for step in range(1, dp_size):
        part = part + dp_got[step - 1]
    total[...] = part


def small_sum(mine, shared):
    dp_size, mp_size = lax.axis_size("dp"), lax.axis_size("mp")
    return pl.pallas_call(
        functools.partial(small_sum_kernel, dp_size, mp_size),
        out_shape=jax.ShapeDtypeStruct(mine.shape, mine.dtype),
        in_specs=[pl.BlockSpec(memory_space=pltpu.VMEM)],
        out_specs=pl.BlockSpec(memory_space=pltpu.VMEM),
        scratch_shapes=[
            pltpu.VMEM((mp_size - 1, shared, 128), jnp.float32),
            pltpu.VMEM(mine.shape, jnp.float32),
            pltpu.VMEM((dp_size - 1,) + mine.shape, jnp.float32),
        ]
        + [pltpu.SemaphoreType.DMA((mp_size - 1,))] * 2
        + [pltpu.SemaphoreType.DMA((dp_size - 1,))] * 2,
        compiler_params=pltpu.CompilerParams(collective_id=1, has_side_effects=True),
        name="small_sum",
    )(mine)


def turn(values, cosine, sine):
    return values * cosine + pltpu.roll(values, HEAD // 2, 1) * sine


def scores_of(query, keys, starts, first, scale):
    scores = (
        lax.dot_general(
            query, keys, (((1,), (1,)), ((), ())), preferred_element_type=jnp.float32
        )
        * scale
    )
    key_index = lax.broadcasted_iota(jnp.int32, scores.shape, 1)
    row_index = first + lax.broadcasted_iota(jnp.int32, scores.shape, 0)
    allowed = (key_index >= starts) & (key_index <= row_index)
    return jnp.where(allowed, scores, masked_score)


def attend_kernel(heads, scale, mixed, cosine, sine, starts, out, queries, keys, values):
    group = mixed.shape[0]
    blocks = lax.axis_size("mp")
    rows = group // blocks
    mp = lax.axis_index("mp")

    def place(block):
        return pl.ds(pl.multiple_of((block ^ mp) * rows, rows), rows)

    width = heads * HEAD
    for block in range(blocks):
        here = pl.ds(block * rows, rows)
        there = place(block)
        cos, sin = cosine[there, :], sine[there, :]
        for head in range(heads):
            lanes = pl.ds(head * HEAD, HEAD)
            queries[here, lanes] = turn(mixed[there, lanes], cos, sin).astype(jnp.bfloat16)
            keys[here, lanes] = turn(
                mixed[there, pl.ds(width + head * HEAD, HEAD)], cos, sin
            ).astype(jnp.bfloat16)
            values[here, lanes] = mixed[there, pl.ds(2 * width + head * HEAD, HEAD)].astype(
                jnp.bfloat16
            )
    for block in range(blocks):
        here = pl.ds(block * rows, rows)
        seen = pl.ds(0, (block + 1) * rows)
        there = place(block)
        for head in range(heads):
            lanes = pl.ds(head * HEAD, HEAD)
            scores = scores_of(
                queries[here, lanes], keys[seen, lanes], starts[there, :], block * rows, scale
            )
            exponents = jnp.exp(scores - jnp.max(scores, axis=-1, keepdims=True))
            probs = exponents * (1.0 / jnp.sum(exponents, axis=-1, keepdims=True))
            out[there, lanes] = jnp.dot(
                probs.astype(jnp.bfloat16),
                values[seen, lanes],
                preferred_element_type=jnp.float32,
            ).astype(jnp.bfloat16)


def attend(mixed, cosine, sine, starts):
    group, width = mixed.shape[0], mixed.shape[1] // 3
    low = jax.ShapeDtypeStruct((group, width), jnp.bfloat16)
    return pl.pallas_call(
        functools.partial(attend_kernel, width // HEAD, HEAD ** (-0.5)),
        out_shape=[low] * 4,
        in_specs=[pl.BlockSpec(memory_space=pltpu.VMEM)] * 4,
        out_specs=[pl.BlockSpec(memory_space=pltpu.VMEM)] * 4,
        compiler_params=pltpu.CompilerParams(vmem_limit_bytes=vmem_bytes),
        cost_estimate=pl.CostEstimate(
            flops=3 * group * group * width, bytes_accessed=20 * group * width, transcendentals=0
        ),
        name="attend",
    )(mixed, cosine, sine, starts)


def attend_back_kernel(
    heads, scale, queries, keys, values, grads, cosine, sine, starts, out, keys_grad, values_grad
):
    group = queries.shape[0]
    blocks = lax.axis_size("mp")
    rows = group // blocks
    mp = lax.axis_index("mp")
    width = heads * HEAD

    def place(block):
        return pl.ds(pl.multiple_of((block ^ mp) * rows, rows), rows)

    def across(first, second):
        return lax.dot_general(
            first, second, (((0,), (0,)), ((), ())), preferred_element_type=jnp.float32
        )

    for head in range(heads):
        lanes = pl.ds(head * HEAD, HEAD)
        for block in reversed(range(blocks)):
            here = pl.ds(block * rows, rows)
            seen = pl.ds(0, (block + 1) * rows)
            there = place(block)
            query = queries[here, lanes]
            grad = grads[there, lanes]
            scores = scores_of(query, keys[seen, lanes], starts[there, :], block * rows, scale)
            exponents = jnp.exp(scores - jnp.max(scores, axis=-1, keepdims=True))
            probs = exponents * (1.0 / jnp.sum(exponents, axis=-1, keepdims=True))
            grad_probs = lax.dot_general(
                grad,
                values[seen, lanes],
                (((1,), (1,)), ((), ())),
                preferred_element_type=jnp.float32,
            )
            inner = jnp.sum(probs * grad_probs, axis=-1, keepdims=True)
            grad_scores = (probs * (grad_probs - inner)).astype(jnp.bfloat16)
            query_grad = (
                jnp.dot(grad_scores, keys[seen, lanes], preferred_element_type=jnp.float32)
                * scale
            )
            out[there, lanes] = turn(
                query_grad, cosine[there, :], -sine[there, :]
            ).astype(jnp.bfloat16)
            key_part = across(grad_scores, query)
            value_part = across(probs.astype(jnp.bfloat16), grad)
            if block == blocks - 1:
                keys_grad[...] = key_part
                values_grad[...] = value_part
            else:
                keys_grad[seen, :] += key_part
                values_grad[seen, :] += value_part
        for block in range(blocks):
            here = pl.ds(block * rows, rows)
            there = place(block)
            out[there, pl.ds(width + head * HEAD, HEAD)] = turn(
                keys_grad[here, :] * scale, cosine[there, :], -sine[there, :]
            ).astype(jnp.bfloat16)
            out[there, pl.ds(2 * width + head * HEAD, HEAD)] = values_grad[here, :].astype(
                jnp.bfloat16
            )


def attend_back(queries, keys, values, grads, cosine, sine, starts):
    group, width = queries.shape
    return pl.pallas_call(
        functools.partial(attend_back_kernel, width // HEAD, HEAD ** (-0.5)),
        out_shape=jax.ShapeDtypeStruct((group, 3 * width), jnp.bfloat16),
        in_specs=[pl.BlockSpec(memory_space=pltpu.VMEM)] * 7,
        out_specs=pl.BlockSpec(memory_space=pltpu.VMEM),
        scratch_shapes=[pltpu.VMEM((group, HEAD), jnp.float32)] * 2,
        compiler_params=pltpu.CompilerParams(vmem_limit_bytes=vmem_bytes),
        cost_estimate=pl.CostEstimate(
            flops=8 * group * group * width, bytes_accessed=20 * group * width, transcendentals=0
        ),
        name="attend_back",
    )(queries, keys, values, grads, cosine, sine, starts)


def token_layout(lengths, grains, token_index):
    seq_ends = jnp.cumsum(lengths)
    starts = seq_ends - lengths
    member = (
        (token_index[:, None] >= starts[None, :]) & (token_index[:, None] < seq_ends[None, :])
    ).astype(jnp.int32)
    first = jnp.sum(member * starts[None, :], axis=1)
    unit_width = jnp.sum(member * jnp.left_shift(jnp.int32(GRAIN), grains)[None, :], axis=1)
    return first, unit_width


def rope_tables(position):
    half_count = HEAD // 2
    freq_index = jnp.arange(half_count, dtype=jnp.float32)
    inverse = rope_base ** (-2.0 * freq_index / HEAD)
    angles = position.astype(jnp.float32)[:, None] * inverse[None, :]
    cosine, sine = jnp.cos(angles), jnp.sin(angles)
    return jnp.concatenate([cosine, cosine], axis=1), jnp.concatenate([-sine, sine], axis=1)


def norm_back(inputs, scale_rows, gain_full, grad_normed):
    weighted = grad_normed * gain_full
    return scale_rows * weighted - inputs * scale_rows**3 * jnp.mean(
        weighted * inputs, axis=-1, keepdims=True
    )


def gelu_both(value):
    root = (2.0 / jnp.pi) ** 0.5
    square = value * value
    bend = jnp.tanh(root * (value + 0.044715 * (value * square)))
    half = 0.5 * (1.0 + bend)
    slope = half + 0.5 * value * (1.0 - bend * bend) * root * (1.0 + 3 * 0.044715 * square)
    return value * half, slope


def across_tokens(first, second):
    return lax.dot_general(
        first, second, (((0,), (0,)), ((), ())), preferred_element_type=jnp.float32
    )


def times_transposed(first, second):
    return lax.dot_general(
        first, second, (((1,), (1,)), ((), ())), preferred_element_type=jnp.float32
    )


def shards(
    hidden_in,
    out_grad,
    seq_lengths,
    seq_grains,
    gain_attn,
    w_qkv,
    w_out,
    gain_ffn,
    w_up,
    bias_up,
    w_down,
    bias_down,
):
    local_rows, model_width = hidden_in.shape
    dp, mp = lax.axis_index("dp"), lax.axis_index("mp")
    dp_size, mp_size = lax.axis_size("dp"), lax.axis_size("mp")
    group_rows = local_rows * mp_size
    shard_rows = w_qkv.shape[0]
    local_width = w_qkv.shape[2]
    local_units = w_up.shape[1]

    qkv_full = gather_dp(w_qkv.reshape(shard_rows, 3 * local_width))
    out_full = gather_dp(w_out.T)
    up_full = gather_dp(w_up)
    down_full = gather_dp(w_down.T)
    hidden_all = gather_mp(hidden_in)
    grad_rows = gather_mp(out_grad)
    piece = gain_attn.shape[0]
    pieces = bias_up.shape[0]
    small = jnp.concatenate([gain_attn, gain_ffn, bias_down, bias_up]).astype(jnp.float32)
    pad = 1024 - small.shape[0]
    small = small_gather(jnp.pad(small, (0, pad)).reshape(8, 128))
    small = small.reshape(dp_size, mp_size, 1024)
    gain_one = small[:, :, :piece].reshape(1, model_width)
    gain_two = small[:, :, piece : 2 * piece].reshape(1, model_width)
    down_bias = small[:, :, 2 * piece : 3 * piece].reshape(1, model_width)
    up_bias = lax.dynamic_index_in_dim(small, mp, 1, keepdims=False)
    up_bias = up_bias[:, 3 * piece : 3 * piece + pieces].reshape(1, local_units)

    block = jnp.bitwise_xor(jnp.arange(mp_size, dtype=jnp.int32), mp)
    token_index = (
        block[:, None] * local_rows + jnp.arange(local_rows, dtype=jnp.int32)[None, :]
    ).reshape(group_rows)
    starts, unit_width = token_layout(seq_lengths[0], seq_grains[0], token_index)
    cosine, sine = rope_tables(token_index - starts)

    hidden_all = hidden_all.astype(jnp.float32)
    scales = lax.rsqrt(jnp.mean(hidden_all * hidden_all, axis=-1, keepdims=True) + norm_eps)
    normed_one = (hidden_all * scales * gain_one).astype(jnp.bfloat16)
    mixed = jnp.dot(normed_one, qkv_full, preferred_element_type=jnp.float32)
    heads_out, queries, keys, values = attend(mixed, cosine, sine, starts[:, None])
    branch = scatter_mp(heads_out, out_full.T)
    hidden = hidden_in.astype(jnp.float32)
    scale_one = scales[:local_rows]
    middle = hidden + branch
    scale_two = lax.rsqrt(jnp.mean(middle * middle, axis=-1, keepdims=True) + norm_eps)
    normed_two = gather_mp((middle * scale_two * gain_two).astype(jnp.bfloat16))

    pre_act = jnp.dot(normed_two, up_full, preferred_element_type=jnp.float32) + up_bias
    unit_index = mp * local_units + jnp.arange(local_units, dtype=jnp.int32)
    unit_mask = unit_index[None, :] < unit_width[:, None]
    activated, slope = gelu_both(pre_act)
    activated = jnp.where(unit_mask, activated, 0.0).astype(jnp.bfloat16)
    slope = jnp.where(unit_mask, slope, 0.0).astype(jnp.bfloat16)
    grad_down = across_tokens(grad_rows, activated).astype(jnp.bfloat16)
    summed_down = scatter_dp(grad_down)
    grad_act = jnp.dot(grad_rows, down_full, preferred_element_type=jnp.float32)
    grad_pre = (grad_act * slope.astype(jnp.float32)).astype(jnp.bfloat16)
    grad_up = across_tokens(normed_two, grad_pre).astype(jnp.bfloat16)
    summed_up = scatter_dp(grad_up)
    grad_up_bias = jnp.sum(grad_pre, axis=0, dtype=jnp.float32)
    grad_normed_two = scatter_mp(grad_pre, up_full.T)
    ffn_rows = scatter_mp(activated, down_full.T)
    output = (middle + ffn_rows + down_bias).astype(jnp.bfloat16)

    own_grad = out_grad.astype(jnp.float32)
    middle_back = own_grad + norm_back(middle, scale_two, gain_two, grad_normed_two)
    gain_two_grad = jnp.sum(grad_normed_two * middle * scale_two, axis=0)
    down_bias_grad = jnp.sum(own_grad, axis=0)
    branch_rows = gather_mp(middle_back.astype(jnp.bfloat16))
    grad_out = across_tokens(branch_rows, heads_out).astype(jnp.bfloat16)
    summed_out = scatter_dp(grad_out)
    grad_heads = jnp.dot(branch_rows, out_full, preferred_element_type=jnp.float32)
    grad_mixed = attend_back(
        queries, keys, values, grad_heads.astype(jnp.bfloat16), cosine, sine, starts[:, None]
    )
    grad_qkv = across_tokens(normed_one, grad_mixed).astype(jnp.bfloat16)
    summed_qkv = scatter_dp(grad_qkv).reshape(w_qkv.shape)
    grad_normed_one = scatter_mp(grad_mixed, qkv_full.T)
    grad_hidden = middle_back + norm_back(hidden, scale_one, gain_one, grad_normed_one)
    gain_one_grad = jnp.sum(grad_normed_one * hidden * scale_one, axis=0)

    shared = 3 * model_width // 128
    vectors = jnp.concatenate([gain_one_grad, gain_two_grad, down_bias_grad, grad_up_bias])
    pad = -vectors.shape[0] % 1024
    totals = small_sum(jnp.pad(vectors, (0, pad)).reshape(-1, 128), shared)
    totals = totals.reshape(-1)
    place = (dp * mp_size + mp) * piece

    def own(index):
        return lax.dynamic_slice_in_dim(
            totals[index * model_width : (index + 1) * model_width], place, piece
        )

    summed_upbias = lax.dynamic_slice_in_dim(totals, 3 * model_width + dp * pieces, pieces)
    return (
        output,
        grad_hidden,
        own(0),
        summed_qkv,
        summed_out.T,
        own(1),
        summed_up,
        summed_upbias,
        summed_down.T,
        own(2),
    )


def solution(mesh):
    return jax.shard_map(
        shards,
        mesh=mesh,
        in_specs=(
            P(("dp", "mp"), None),
            P(("dp", "mp"), None),
            P("dp", None),
            P("dp", None),
            P(("dp", "mp")),
            P("dp", None, "mp"),
            P("mp", "dp"),
            P(("dp", "mp")),
            P("dp", "mp"),
            P(("mp", "dp")),
            P("mp", "dp"),
            P(("dp", "mp")),
        ),
        out_specs=(
            P(("dp", "mp"), None),
            P(("dp", "mp"), None),
            P(("dp", "mp")),
            P("dp", None, "mp"),
            P("mp", "dp"),
            P(("dp", "mp")),
            P("dp", "mp"),
            P(("mp", "dp")),
            P("mp", "dp"),
            P(("dp", "mp")),
        ),
        check_vma=False,
    )
```

```python
import functools
import types
import typing

import jax
import jax.numpy as jnp
import numpy as np
from jax import lax
from jax.experimental import pallas as pl
from jax.experimental.pallas import tpu as pltpu
from jax.sharding import PartitionSpec as P

HEAD = 128
GRAIN = 768
MESH = pl.DeviceIdType.MESH
low = jnp.bfloat16
full = jnp.float32

norm_eps = 1e-06
rope_base = 10000.0
masked_score = -1e30
vmem_bytes = 62 * 2**20
root_half_pi = (2.0 / np.pi) ** 0.5
cubic = 0.044715

plain = (((1,), (0,)), ((), ()))
by_rows = (((1,), (1,)), ((), ()))
by_tokens = (((0,), (0,)), ((), ()))


def dot(first, second, dims=plain):
    return lax.dot_general(first, second, dims, preferred_element_type=jnp.float32)


def window(index, size):
    return pl.ds(pl.multiple_of(index * size, size), size)


class Wire:
    def __init__(self, sent, got, local):
        self.sent, self.got, self.local = sent, got, local
        self.used, self.used_local = 0, 0
        self.open = []

    def push(self, source, target, dp, mp):
        copy = pltpu.make_async_remote_copy(
            source,
            target,
            self.sent.at[self.used],
            self.got.at[self.used],
            device_id=(dp, mp),
            device_id_type=MESH,
        )
        self.used += 1
        copy.start()
        return copy

    def move(self, source, target):
        copy = pltpu.make_async_copy(source, target, self.local.at[self.used_local])
        self.used_local += 1
        copy.start()
        return copy

    def store(self, source, target):
        self.open.append(self.move(source, target))

    def close(self):
        for copy in self.open:
            copy.wait()
        self.open = []


def greet(dp, mp, dp_size, mp_size):
    barrier = pltpu.get_barrier_semaphore()
    for step in range(1, mp_size):
        pl.semaphore_signal(barrier, inc=1, device_id=(dp, mp ^ step), device_id_type=MESH)
    for step in range(1, dp_size):
        pl.semaphore_signal(barrier, inc=1, device_id=(dp ^ step, mp), device_id_type=MESH)
    pl.semaphore_wait(barrier, mp_size + dp_size - 2)


def cut(rows, *parts):
    edges = [16 * round(rows * part / 16) for part in parts]
    return [(a, b - a) for a, b in zip(edges[:-1], edges[1:]) if b > a]


def last_step(kind, k, dp_size):
    if k == 0:
        return 0
    if kind == "y":
        return (k & ~1) & -(k & ~1) if k > 1 else 1
    return k & -k


def onward(kind, k, dp_size):
    steps = []
    step = dp_size // 2
    while step:
        if step > 1:
            free = k < 2 or step < last_step(kind, k & ~1, dp_size)
        else:
            free = k == 0 or (kind == "z" and k > 1 and k % 2 == 0)
        if free:
            steps.append(step)
        step //= 2
    if kind == "z" and k % 2:
        return []
    if kind == "y" and k == 0:
        return [1] + steps[:-1]
    return steps


def turn(values, cosine, sine):
    return values * cosine + pltpu.roll(values, HEAD // 2, 1) * sine


def softmax_rows(query, keys, starts, first, scale):
    scores = dot(query, keys, by_rows) * scale
    key_index = lax.broadcasted_iota(jnp.int32, scores.shape, 1)
    row_index = first + lax.broadcasted_iota(jnp.int32, scores.shape, 0)
    allowed = (key_index >= starts) & (key_index <= row_index)
    scores = jnp.where(allowed, scores, masked_score)
    exponents = jnp.exp(scores - jnp.max(scores, axis=-1, keepdims=True))
    return exponents * (1.0 / jnp.sum(exponents, axis=-1, keepdims=True))


def gelu_both(value):
    square = value * value
    bend = jnp.tanh(value * (root_half_pi + (root_half_pi * cubic) * square))
    half = 0.5 + 0.5 * bend
    inner = root_half_pi + (3 * root_half_pi * cubic) * square
    return value * half, half + (0.5 * value) * (1.0 - bend * bend) * inner


class ForwardIn(typing.NamedTuple):
    hidden: object
    grad: object
    w_qkv: object
    w_out: object
    w_up: object
    w_down: object
    gain_attn: object
    gain_ffn: object
    bias_down: object
    bias_up: object
    spread: object
    spread_up: object
    targets: object
    inverse: object
    lengths: object
    grains: object


class ForwardOut(typing.NamedTuple):
    qkv_all: object
    out_all: object
    up_all: object
    down_all: object
    normed: object
    queries: object
    keys: object
    values: object
    heads: object
    middle: object
    normed_two: object
    activated: object
    slope: object
    grads: object
    grad_down: object
    cosine: object
    sine: object
    vectors: object


class ForwardScratch(typing.NamedTuple):
    s_hidden: object
    s_normed: object
    s_qkv: object
    s_out: object
    s_up: object
    s_q: object
    s_k: object
    s_v: object
    s_heads: object
    s_cos: object
    s_sin: object
    s_small: object
    s_starts: object
    s_widths: object
    s_core_out: object
    s_core_in: object
    s_x_out: object
    s_x_in: object
    s_part: object
    s_middle: object
    s_two: object
    s_act: object
    s_slope: object
    s_grads: object
    s_down: object
    sent: object
    got: object
    local: object


def forward_kernel(seqs, *refs):
    r = types.SimpleNamespace(
        **dict(zip(ForwardIn._fields + ForwardOut._fields + ForwardScratch._fields, refs, strict=True))
    )
    dp, mp = lax.axis_index("dp"), lax.axis_index("mp")
    dp_size, mp_size = lax.axis_size("dp"), lax.axis_size("mp")
    rings = dp_size // 2
    rows, width = r.hidden.shape
    group = rows * mp_size
    shard = r.w_up.shape[0]
    units = r.w_up.shape[1]
    lanes = r.w_out.shape[1]
    heads = lanes // HEAD
    scale = HEAD ** (-0.5)
    wire = Wire(r.sent, r.got, r.local)

    def block(index):
        return window(index, rows)

    mine, core, far, far_core = block(mp), block(mp ^ 1), block(mp ^ 2), block(mp ^ 3)
    greet(dp, mp, dp_size, mp_size)

    half = r.bias_up.shape[0] // 2
    pair = r.bias_up[...].astype(full).reshape(1, 2 * half)
    r.s_small[dp, mp] = jnp.zeros((8, 128), full)
    for line, value in enumerate((r.gain_attn, r.gain_ffn, r.bias_down)):
        count = value.shape[0]
        r.s_small[dp, mp, line : line + 1, 0:count] = value[...].astype(full).reshape(1, count)
    r.s_small[dp, mp, 3:4, 0:half] = pair[:, :half]
    r.s_small[dp, mp, 4:5, 0:half] = pair[:, half:]
    small = [
        wire.push(r.s_small.at[dp, mp], r.s_small.at[dp, mp], dp, mp ^ step)
        for step in range(1, mp_size)
    ]
    hidden_far = wire.push(r.hidden, r.s_hidden.at[mine], dp, mp ^ 2)
    hidden_core = wire.push(r.hidden, r.s_hidden.at[mine], dp, mp ^ 1)
    own_hidden = wire.move(r.hidden, r.s_hidden.at[mine])

    sources = [r.w_qkv, r.w_out, r.w_up, r.w_down]
    targets = [r.s_qkv, r.s_out, r.s_up, r.down_all]
    pieces = [(0, "z") + span for span in cut(shard, 0, 0.5, 1)]
    pieces += [(1, "z", 0, shard)]
    pieces += [(2, "z") + span for span in cut(shard, 0, 0.5, 1)]
    pieces += [(3, kind) + span for kind, span in zip("zy", cut(shard, 0, 0.5, 1), strict=True)]
    route, waited = {}, set()

    def rows_at(ref, span):
        return ref.at[:, span, :] if len(ref.shape) == 3 else ref.at[span, :]

    def spot(weight, k, first, count):
        start = pl.multiple_of((dp ^ k) * shard + first, 16)
        return rows_at(targets[weight], pl.ds(start, count))

    def pass_on(index, k, steps):
        weight, kind, first, count = pieces[index]
        place = spot(weight, k, first, count)
        part = place if k else rows_at(sources[weight], pl.ds(first, count))
        for step in steps:
            route[index, k ^ step] = wire.push(part, place, dp ^ step, mp)

    ticked = {}

    def launch(index, steps):
        pass_on(index, 0, [step for step in onward(pieces[index][1], 0, dp_size) if step in steps])

    def tick(index, part):
        kind = pieces[index][1]
        ks = [k for k in [0] + arrival[kind] if onward(kind, k, dp_size)]
        for k in ks[ticked.get(index, 1) : (part + 1) * len(ks) // 4]:
            if (index, k) not in route:
                break
            route[index, k].wait_recv()
            waited.add((index, k))
            pass_on(index, k, onward(kind, k, dp_size))
            ticked[index] = ticked.get(index, 1) + 1

    def arrived(weight):
        for index, piece in enumerate(pieces):
            if piece[0] == weight:
                for k in arrival[piece[1]]:
                    if (index, k) not in waited:
                        route[index, k].wait_recv()

    over_y = [1]
    over_z = [step for step in onward("z", 0, dp_size) if step > 1]
    arrival = {}
    for kind in "zy":
        found = [0]
        for k in found:
            found += [k ^ step for step in onward(kind, k, dp_size)]
        arrival[kind] = found[1:]

    flying, core_sent = types.SimpleNamespace(), {}

    def small_on():
        for copy in small:
            copy.wait_recv()
        small.extend(
            wire.push(r.s_small.at[dp], r.s_small.at[dp], dp ^ step, mp)
            for step in range(1, dp_size)
        )

    def make_positions():
        token = lax.broadcasted_iota(jnp.int32, (group, 1), 0)
        first = jnp.int32(0)
        starts = jnp.zeros((group, 1), jnp.int32)
        widths = jnp.zeros((group, 1), jnp.int32)
        for seq in range(seqs):
            starts = jnp.where(token >= first, first, starts)
            widths = jnp.where(token >= first, jnp.left_shift(GRAIN, r.grains[0, seq]), widths)
            first = first + r.lengths[0, seq]
        r.s_starts[...] = starts
        r.s_widths[...] = widths

    def make_tables():
        @pl.loop(0, group // 128)
        def _(index):
            here = window(index, 128)
            tokens = index * 128 + lax.broadcasted_iota(jnp.int32, (128, 1), 0)
            position = (tokens - r.s_starts[here, :]).astype(full)
            angles = position * r.inverse[0:1, :]
            r.s_cos[here, :] = jnp.cos(angles)
            r.s_sin[here, :] = jnp.sin(angles) * r.inverse[1:2, :]

        wire.store(r.s_cos, r.cosine)
        wire.store(r.s_sin, r.sine)

    def spread_vectors():
        for copy in small[mp_size - 1 :]:
            copy.wait_recv()
        devices = dp_size * mp_size * 8
        for start in range(0, width, 512):
            here = pl.ds(start, 512)
            packed = r.s_small[...].reshape(devices, 128).astype(low)
            spread = dot(packed, r.spread[:, here])
            row = lax.broadcasted_iota(jnp.int32, (devices, 1), 0)
            for line in range(3):
                chosen = row == r.targets[0:1, here] + line
                r.vectors[line : line + 1, here] = jnp.sum(
                    jnp.where(chosen, spread, 0.0), axis=0, keepdims=True
                )
        for start in range(0, units, 512):
            here = pl.ds(start, 512)
            packed = r.s_small[...].reshape(devices, 128).astype(low)
            spread = dot(packed, r.spread_up[:, here])
            row = lax.broadcasted_iota(jnp.int32, (devices, 1), 0)
            chosen = row == r.targets[1:2, here] + mp * 8
            r.vectors[3:4, here] = jnp.sum(jnp.where(chosen, spread, 0.0), axis=0, keepdims=True)

    def pass_hidden():
        hidden_far.wait_recv()
        flying.hidden_pass = wire.push(r.s_hidden.at[far], r.s_hidden.at[far], dp, mp ^ 1)
        flying.own_grad = wire.move(r.grad, r.s_grads.at[mine])
        flying.grad_far = wire.push(r.grad, r.s_grads.at[mine], dp, mp ^ 2)

    def norm_one():
        hidden_core.wait_recv()
        own_hidden.wait()
        flying.hidden_pass.wait_recv()
        flying.grad_core = wire.push(r.grad, r.s_grads.at[mine], dp, mp ^ 1)

        @pl.loop(0, group // 64)
        def _(index):
            here = window(index, 64)
            value = r.s_hidden[here, :].astype(full)
            ratio = lax.rsqrt(jnp.mean(value * value, axis=-1, keepdims=True) + norm_eps)
            r.s_normed[here, :] = (value * ratio * r.vectors[0:1, :]).astype(low)

        wire.store(r.s_normed, r.normed)

    def mix():
        for copy in flying.own_weights:
            copy.wait()
        arrived(0)
        wire.store(r.s_qkv, r.qkv_all)

        @pl.loop(0, mp_size)
        def _(index):
            here = block(index)
            value = r.s_normed[here, :]
            cos, sin = r.s_cos[here, :], r.s_sin[here, :]
            for part, place in enumerate((r.s_q, r.s_k, r.s_v)):
                mixed = dot(value, r.s_qkv[part, :, :])
                for head in range(heads):
                    span = slice(head * HEAD, (head + 1) * HEAD)
                    piece = mixed[:, span]
                    if part < 2:
                        piece = turn(piece, cos, sin)
                    place[here, span] = piece.astype(low)

        wire.store(r.s_q, r.queries)
        wire.store(r.s_k, r.keys)
        wire.store(r.s_v, r.values)

    def attend(index):
        here = pl.ds(index * rows, rows)
        seen = pl.ds(0, (index + 1) * rows)

        @pl.loop(0, heads)
        def _(head):
            span = window(head, HEAD)
            probs = softmax_rows(
                r.s_q[here, span], r.s_k[seen, span], r.s_starts[here, :], index * rows, scale
            )
            r.s_heads[here, span] = dot(probs.astype(low), r.s_v[seen, span]).astype(low)

    def branch(index, put):
        value = r.s_heads[index, :]

        @pl.loop(0, width // 512)
        def _(tile):
            span = window(tile, 512)
            put(span, dot(value, r.s_out[span, :], by_rows))

    def put_core(slot):
        def put(span, value):
            r.s_core_out[slot, :, span] = value.astype(low)

        return put

    def put_far(span, value):
        r.s_x_out[:, span] = (value + r.s_core_in[0, :, span].astype(full)).astype(low)

    def put_mine(span, value):
        r.s_part[:, span] = value + r.s_core_in[1, :, span].astype(full)

    def branch_core():
        wire.store(r.s_heads, r.heads)
        arrived(1)
        wire.store(r.s_out, r.out_all)
        for place, index in enumerate((far_core, core)):
            branch(index, put_core(place))
            core_sent[place] = wire.push(
                r.s_core_out.at[place], r.s_core_in.at[place], dp, mp ^ 1
            )

    def branch_far():
        core_sent[0].wait_recv()
        branch(far, put_far)
        flying.branch_far = wire.push(r.s_x_out, r.s_x_in, dp, mp ^ 2)

    def branch_mine():
        core_sent[1].wait_recv()
        branch(mine, put_mine)
        flying.grad_far.wait_recv()
        flying.grad_pass = wire.push(r.s_grads.at[far], r.s_grads.at[far], dp, mp ^ 1)

    def norm_two():
        flying.branch_far.wait_recv()

        @pl.loop(0, rows // 64)
        def _(index):
            here = window(index, 64)
            there = pl.ds(pl.multiple_of(mp * rows + index * 64, 64), 64)
            value = r.s_hidden[there, :].astype(full) + (
                r.s_part[here, :] + r.s_x_in[here, :].astype(full)
            )
            r.s_middle[here, :] = value
            ratio = lax.rsqrt(jnp.mean(value * value, axis=-1, keepdims=True) + norm_eps)
            r.s_two[there, :] = (value * ratio * r.vectors[1:2, :]).astype(low)

        flying.two_far = wire.push(r.s_two.at[mine], r.s_two.at[mine], dp, mp ^ 2)
        flying.two_core = wire.push(r.s_two.at[mine], r.s_two.at[mine], dp, mp ^ 1)
        wire.store(r.s_middle, r.middle)

    def units_of(index):
        value = r.s_two[index, :]
        limit = r.s_widths[index, :] - mp * units

        @pl.loop(0, units // 512)
        def _(tile):
            span = window(tile, 512)
            pre_act = dot(value, r.s_up[:, span]) + r.vectors[3:4, span]
            unit = tile * 512 + lax.broadcasted_iota(jnp.int32, (1, 512), 1)
            on = unit < limit
            activated, slope = gelu_both(pre_act)
            r.s_act[index, span] = jnp.where(on, activated, 0.0).astype(low)
            r.s_slope[index, span] = jnp.where(on, slope, 0.0).astype(low)

    def units_mine():
        arrived(2)
        wire.store(r.s_up, r.up_all)
        units_of(mine)

    def pass_two():
        flying.two_far.wait_recv()
        flying.two_pass = wire.push(r.s_two.at[far], r.s_two.at[far], dp, mp ^ 1)

    def units_core():
        flying.two_core.wait_recv()
        units_of(core)

    def units_far():
        units_of(far)

    def units_far_core():
        flying.two_pass.wait_recv()
        units_of(far_core)
        wire.store(r.s_two, r.normed_two)
        wire.store(r.s_act, r.activated)
        wire.store(r.s_slope, r.slope)

    def grad_down():
        flying.grad_core.wait_recv()
        flying.grad_pass.wait_recv()
        flying.own_grad.wait()
        wire.store(r.s_grads, r.grads)

        @pl.loop(0, width // 256)
        def _(tile):
            span = window(tile, 256)
            r.s_down[span, :] = dot(r.s_grads[:, span], r.s_act[...], by_tokens).astype(low)

        wire.store(r.s_down, r.grad_down)

    def load_own():
        flying.own_weights = [
            wire.move(sources[weight], rows_at(targets[weight], window(dp, shard)))
            for weight in range(4)
        ]

    order = [
        (launch, 1, over_y), (launch, 0, over_z), (load_own,), (launch, 3, over_y),
        (launch, 0, over_y), (launch, 1, over_z), (launch, 4, over_y), (launch, 2, over_y),
        (small_on,), (launch, 2, over_z), (tick, 0, 1), (tick, 1, 1), (tick, 2, 1), (tick, 0, 2),
        (spread_vectors,), (launch, 4, over_z), (make_positions,), (tick, 1, 2), (make_tables,),
        (tick, 0, 3), (pass_hidden,), (tick, 1, 3), (launch, 3, over_z), (tick, 2, 2),
        (norm_one,), (tick, 2, 3), (launch, 6, over_y), (launch, 5, over_z), (tick, 4, 1), (mix,),
        (tick, 3, 1), (attend, 0), (attend, 1), (tick, 4, 2), (tick, 5, 1), (tick, 3, 2),
        (attend, 2), (attend, 3), (branch_core,), (branch_far,), (tick, 3, 3), (branch_mine,),
        (tick, 4, 3), (launch, 6, over_z), (norm_two,), (launch, 5, over_y), (tick, 5, 2),
        (tick, 5, 3), (tick, 6, 1), (units_mine,), (tick, 6, 2), (units_core,), (pass_two,),
        (units_far,), (units_far_core,), (tick, 6, 3), (grad_down,),
    ]
    for step, *where in order:
        step(*where)
    for index in range(len(pieces)):
        tick(index, 3)
    arrived(3)
    wire.close()
    for copy in list(route.values()) + small + [hidden_far, hidden_core]:
        copy.wait_send()
    copies = list(core_sent.values())
    copies += [flying.branch_far, flying.grad_core, flying.grad_far, flying.grad_pass, flying.hidden_pass, flying.two_core, flying.two_far, flying.two_pass]
    for copy in copies:
        copy.wait_send()


def run_forward(inputs, seqs):
    hidden, w_up, w_out, w_qkv = inputs["hidden"], inputs["w_up"], inputs["w_out"], inputs["w_qkv"]
    dp_size, mp_size = lax.axis_size("dp"), lax.axis_size("mp")
    rows, width = hidden.shape
    group = rows * mp_size
    units, lanes = w_up.shape[1], w_out.shape[1]
    shapes = dict(
        qkv_all=((3, width, lanes), low),
        out_all=((width, lanes), low),
        up_all=((width, units), low),
        down_all=((width, units), low),
        normed=((group, width), low),
        queries=((group, lanes), low),
        keys=((group, lanes), low),
        values=((group, lanes), low),
        heads=((group, lanes), low),
        middle=((rows, width), full),
        normed_two=((group, width), low),
        activated=((group, units), low),
        slope=((group, units), low),
        grads=((group, width), low),
        grad_down=((width, units), low),
        cosine=((group, HEAD), full),
        sine=((group, HEAD), full),
        vectors=((8, width), full),
    )
    remote = mp_size - 1 + dp_size - 1 + 7 * (dp_size - 1) + 16
    scratch = [
        pltpu.VMEM(shape, kind)
        for shape, kind in (
            ((group, width), low),
            ((group, width), low),
            ((3, width, lanes), low),
            ((width, lanes), low),
            ((width, units), low),
            ((group, lanes), low),
            ((group, lanes), low),
            ((group, lanes), low),
            ((group, lanes), low),
            ((group, HEAD), full),
            ((group, HEAD), full),
            ((dp_size, mp_size, 8, 128), full),
            ((group, 1), jnp.int32),
            ((group, 1), jnp.int32),
            ((2, rows, width), low),
            ((2, rows, width), low),
            ((rows, width), low),
            ((rows, width), low),
            ((rows, width), full),
            ((rows, width), full),
            ((group, width), low),
            ((group, units), low),
            ((group, units), low),
            ((group, width), low),
            ((width, units), low),
        )
    ] + [
        pltpu.SemaphoreType.DMA((remote,)),
        pltpu.SemaphoreType.DMA((remote,)),
        pltpu.SemaphoreType.DMA((32,)),
    ]
    anywhere = pl.BlockSpec(memory_space=pl.ANY)
    vector = pl.BlockSpec(memory_space=pltpu.VMEM)
    scalar = pl.BlockSpec(memory_space=pltpu.SMEM)
    placed = dict(
        gain_attn=vector,
        gain_ffn=vector,
        bias_down=vector,
        bias_up=vector,
        spread=vector,
        spread_up=vector,
        targets=vector,
        inverse=vector,
        lengths=scalar,
        grains=scalar,
        vectors=vector,
    )
    outs = pl.pallas_call(
        functools.partial(forward_kernel, seqs),
        out_shape=[jax.ShapeDtypeStruct(*shapes[name]) for name in ForwardOut._fields],
        in_specs=[placed.get(name, anywhere) for name in ForwardIn._fields],
        out_specs=[placed.get(name, anywhere) for name in ForwardOut._fields],
        scratch_shapes=scratch,
        compiler_params=pltpu.CompilerParams(
            collective_id=0, has_side_effects=True, vmem_limit_bytes=vmem_bytes
        ),
        name="forward",
    )(*[inputs[name] for name in ForwardIn._fields])
    return dict(zip(ForwardOut._fields, outs))


def small_tables(width, units, dp_size, mp_size):
    piece = width // (dp_size * mp_size)
    half = units // dp_size // 2
    lane = np.arange(128)[:, None]
    column = np.arange(width)[None, :]
    unit = np.arange(units)[None, :]
    spread = (column % piece == lane).astype(np.float32)
    spread_up = (unit % half == lane).astype(np.float32)
    targets = np.zeros((8, max(width, units)), np.int32)
    targets[0, :width] = column[0] // piece * 8
    targets[1, :units] = unit[0] // (2 * half) * (8 * mp_size) + 3 + unit[0] % (2 * half) // half
    return jnp.asarray(spread, low), jnp.asarray(spread_up, low), jnp.asarray(targets)


def rope_rows():
    index = np.arange(HEAD // 2, dtype=np.float32)
    inverse = np.float32(rope_base) ** (np.float32(-2.0) * index / np.float32(HEAD))
    table = np.zeros((8, HEAD), np.float32)
    table[0] = np.concatenate([inverse, inverse])
    table[1] = np.concatenate([-np.ones(HEAD // 2), np.ones(HEAD // 2)])
    return jnp.asarray(table)


class BackwardIn(typing.NamedTuple):
    hidden: object
    lengths: object
    vectors: object
    cosine: object
    sine: object
    qkv_all: object
    out_all: object
    up_all: object
    down_all: object
    normed: object
    queries: object
    keys: object
    values: object
    heads: object
    middle: object
    normed_two: object
    activated: object
    slope: object
    grads: object
    grad_down: object


class BackwardOut(typing.NamedTuple):
    output: object
    grad_in: object
    own_qkv: object
    own_out: object
    own_up: object
    totals: object
    last_qkv: object
    last_out: object
    last_up: object
    last_down: object


class BackwardScratch(typing.NamedTuple):
    s_weights: object
    s_up: object
    s_slope: object
    s_grads: object
    s_two: object
    s_act: object
    s_pre: object
    s_own: object
    got_qkv: object
    got_out: object
    got_up: object
    got_down: object
    s_gqkv: object
    s_gout: object
    s_core_in: object
    s_x_in: object
    s_core_out: object
    s_x_out: object
    s_part: object
    s_middle: object
    s_back: object
    s_gheads: object
    s_gk: object
    s_gv: object
    s_cos: object
    s_sin: object
    s_sums: object
    s_vec: object
    s_vec_mp: object
    s_vec_y: object
    s_vec_z: object
    sent: object
    got: object
    local: object


def backward_kernel(seqs, *refs):
    r = types.SimpleNamespace(
        **dict(zip(BackwardIn._fields + BackwardOut._fields + BackwardScratch._fields, refs, strict=True))
    )
    dp, mp = lax.axis_index("dp"), lax.axis_index("mp")
    dp_size, mp_size = lax.axis_size("dp"), lax.axis_size("mp")
    rings = dp_size // 2
    rows, width = r.hidden.shape
    group = rows * mp_size
    shard = width // dp_size
    units = r.slope.shape[1]
    lanes = r.heads.shape[1]
    heads = lanes // HEAD
    scale = HEAD ** (-0.5)
    wire = Wire(r.sent, r.got, r.local)
    sends = []

    def block(index):
        return window(index, rows)

    def push(source, target, to_dp, to_mp):
        copy = wire.push(source, target, to_dp, to_mp)
        sends.append(copy)
        return copy

    def sent(*copies):
        for copy in copies:
            copy.wait_send()
            sends[:] = [other for other in sends if other is not copy]

    mine, core, far, far_core = block(mp), block(mp ^ 1), block(mp ^ 2), block(mp ^ 3)

    barrier = pltpu.get_barrier_semaphore()
    for step in range(1, mp_size):
        pl.semaphore_signal(barrier, inc=1, device_id=(dp, mp ^ step), device_id_type=MESH)
    pl.semaphore_signal(barrier, inc=1, device_id=(dp ^ 1, mp), device_id_type=MESH)
    for step in range(1, rings):
        pl.semaphore_signal(barrier, inc=1, device_id=(dp ^ (2 * step), mp), device_id_type=MESH)
    pl.semaphore_wait(barrier, mp_size + rings - 1)

    local = dict(down=r.grad_down, up=r.s_up, out=r.s_gout, qkv=r.s_gqkv)
    landing = dict(down=r.got_down, up=r.got_up, out=r.got_out, qkv=r.got_qkv)
    final = dict(down=r.last_down, up=r.last_up, out=r.last_out, qkv=r.last_qkv)
    pieces = [("down", kind) + span for kind, span in zip("yz", cut(shard, 0, 0.5, 1), strict=True)]
    pieces += [("up", "z") + span for span in cut(shard, 0, 0.5, 1)]
    pieces += [("out", "z", 0, shard)]
    pieces += [("qkv", "z") + span for span in cut(shard, 0, 0.5, 1)]
    inner, leaves, middle_slots, route, own = {}, {}, {}, {}, {}
    for kind in "zy":
        found = [0]
        for k in found:
            found += [k ^ step for step in onward(kind, k, dp_size)]
        inner[kind] = [k for k in found if onward(kind, k, dp_size)]
        leaves[kind] = [k for k in found[::-1] if not onward(kind, k, dp_size)]
        pairs = [(k, step) for k in inner[kind][1:] for step in onward(kind, k, dp_size)]
        middle_slots[kind] = {pair: place for place, pair in enumerate(pairs)}

    def rows_of(index, k):
        name, kind, first, count = pieces[index]
        return pl.ds(pl.multiple_of((dp ^ k) * shard + first, 16), count)

    def spot(index, k, step):
        name, kind, first, count = pieces[index]
        span = pl.ds(first, count)
        if k == 0:
            return final[name].at[onward(kind, 0, dp_size).index(step), span]
        return landing[name].at[middle_slots[kind][k, step], span]

    def climb(index, k, source):
        kind = pieces[index][1]
        step = last_step(kind, k, dp_size)
        route[index, k ^ step, step] = push(source, spot(index, k ^ step, step), dp ^ step, mp)

    launched, ticked = {}, {}

    def launch(index, part):
        ks = leaves[pieces[index][1]]
        for k in ks[launched.get(index, 0) : (part + 1) * len(ks) // 4]:
            climb(index, k, local[pieces[index][0]].at[rows_of(index, k)])
        launched[index] = (part + 1) * len(ks) // 4

    def tick(index, part):
        kind = pieces[index][1]
        ks = inner[kind][:0:-1]
        for k in ks[ticked.get(index, 0) : (part + 1) * len(inner[kind]) // 4]:
            if any((index, k, step) not in route for step in onward(kind, k, dp_size)):
                break
            add_up(index, k)
            ticked[index] = ticked.get(index, 0) + 1

    def own_load(index):
        name, kind, first, count = pieces[index]
        for place, k in enumerate(inner[kind][1:]):
            own[index, k] = wire.move(
                local[name].at[rows_of(index, k)], r.s_own.at[place, pl.ds(first, count)]
            )

    def own_part(index, k, start, count):
        name, kind, first, _ = pieces[index]
        if name == "down":
            return r.s_own[inner[kind].index(k) - 1, pl.ds(first + start, count), :].astype(full)
        place = pl.multiple_of((dp ^ k) * shard + first + start, 16)
        return local[name][pl.ds(place, count), :].astype(full)

    def add_up(index, k):
        name, kind, first, count = pieces[index]
        part = 48 if count % 48 == 0 else 16
        steps = onward(kind, k, dp_size)
        for step in steps:
            route[index, k, step].wait_recv()
        if name == "down":
            own[index, k].wait()

        @pl.loop(0, count // part)
        def _(turn_index):
            start = pl.multiple_of(turn_index * part, 16)
            here = pl.ds(pl.multiple_of(first + start, 16), part)
            total = own_part(index, k, start, part)
            for step in steps:
                slot_index = middle_slots[kind][k, step]
                total = total + landing[name][slot_index, here, :].astype(full)
            landing[name][middle_slots[kind][k, steps[0]], here, :] = total.astype(low)

        climb(index, k, spot(index, k, steps[0]))

    def finish(index):
        kind = pieces[index][1]
        for step in onward(kind, 0, dp_size):
            route[index, 0, step].wait_recv()

    def reduce_start(left, right, columns, slot_in):
        def product(index, put):
            value = left[index, columns]

            @pl.loop(0, width // 512)
            def _(tile):
                span = window(tile, 512)
                put(span, dot(value, right[span, columns], by_rows))

        def put_core(place):
            def put(span, value):
                r.s_core_out[place, :, span] = value.astype(low)

            return put

        def put_far(span, value):
            value = value + r.s_core_in[slot_in, 0, :, span].astype(full)
            r.s_x_out[slot_in, :, span] = value.astype(low)

        def put_mine(span, value):
            r.s_part[:, span] = value + r.s_core_in[slot_in, 1, :, span].astype(full)

        def first():
            product(far_core, put_core(0))
            one = push(r.s_core_out.at[0], r.s_core_in.at[slot_in, 0], dp, mp ^ 1)
            product(core, put_core(1))
            two = push(r.s_core_out.at[1], r.s_core_in.at[slot_in, 1], dp, mp ^ 1)
            return one, two

        def second(one):
            one.wait_recv()
            product(far, put_far)

        def third(two):
            two.wait_recv()
            product(mine, put_mine)

        return first, second, third

    tiles = [pl.ds(start, 512) for start in range(0, units, 512)]
    everything, mixed = pl.ds(0, units), pl.ds(0, 3 * lanes)
    to_heads = pl.ds(3 * lanes, lanes)
    load_grads = wire.move(r.grads, r.s_grads)
    load_tiles = [
        [
            wire.move(r.down_all.at[:, span], r.s_weights.at[:, span]),
            wire.move(r.slope.at[:, span], r.s_slope.at[:, span]),
        ]
        for span in tiles
    ]
    flying, loads = types.SimpleNamespace(), types.SimpleNamespace()

    def load():
        loads.up = wire.move(r.up_all, r.s_up)
        loads.two = wire.move(r.normed_two, r.s_two)
        loads.act = wire.move(r.activated, r.s_act)
        loads.middle = wire.move(r.middle, r.s_middle)
        own_load(1)
        own_load(0)
        loads.rest = [
            wire.move(r.cosine, r.s_cos),
            wire.move(r.sine, r.s_sin),
        ]
        r.s_sums[...] = jnp.zeros_like(r.s_sums)

    def unit_grads():
        load_grads.wait()
        for span, copies in zip(tiles, load_tiles):
            for copy in copies:
                copy.wait()
            value = dot(r.s_grads[...], r.s_weights[:, span]) * r.s_slope[:, span].astype(full)
            value = value.astype(low)
            r.s_pre[:, span] = value
            r.s_sums[3:4, span] = jnp.sum(value.astype(full), axis=0, keepdims=True)

    two_first, two_second, two_third = reduce_start(r.s_pre, r.s_up, everything, 0)
    ffn_first, ffn_second, ffn_third = reduce_start(r.s_act, r.s_weights, everything, 1)
    one_first, one_second, one_third = reduce_start(r.s_act, r.s_weights, mixed, 0)

    def two_core():
        loads.up.wait()
        flying.core = two_first()

    def two_far():
        two_second(flying.core[0])
        flying.two = push(r.s_x_out.at[0], r.s_x_in.at[0], dp, mp ^ 2)

    def two_mine():
        two_third(flying.core[1])

    def grad_up():
        loads.two.wait()

        @pl.loop(0, width // 256)
        def _(tile):
            span = window(tile, 256)
            r.s_up[span, :] = dot(r.s_two[:, span], r.s_pre[...], by_tokens).astype(low)

        loads.heads = [
            wire.move(place, r.s_two.at[:, pl.ds(index * lanes, lanes)])
            for index, place in enumerate((r.queries, r.keys, r.values, r.heads))
        ]

    def norm_two():
        loads.middle.wait()
        flying.two.wait_recv()

        @pl.loop(0, rows // 64)
        def _(index):
            here = window(index, 64)
            there = pl.ds(pl.multiple_of(mp * rows + index * 64, 64), 64)
            normed_grad = r.s_part[here, :] + r.s_x_in[0, here, :].astype(full)
            middle = r.s_middle[here, :]
            grad = r.s_grads[there, :].astype(full)
            ratio = lax.rsqrt(jnp.mean(middle * middle, axis=-1, keepdims=True) + norm_eps)
            weighted = normed_grad * r.vectors[1:2, :]
            back = (
                grad
                + ratio * weighted
                - middle * (ratio**3 * jnp.mean(weighted * middle, axis=-1, keepdims=True))
            )
            r.s_back[here, :] = back
            r.s_slope[there, :] = back.astype(low)
            r.s_sums[1:2, :] += jnp.sum(normed_grad * (middle * ratio), axis=0, keepdims=True)
            r.s_sums[2:3, :] += jnp.sum(grad, axis=0, keepdims=True)

        flying.branch_far = push(r.s_slope.at[mine], r.s_slope.at[mine], dp, mp ^ 2)
        flying.branch_core = push(r.s_slope.at[mine], r.s_slope.at[mine], dp, mp ^ 1)
        loads.normed = wire.move(r.normed, r.s_grads)

    def ffn_core():
        loads.act.wait()
        sent(*flying.core)
        flying.core = ffn_first()

    def ffn_far():
        ffn_second(flying.core[0])
        flying.ffn = push(r.s_x_out.at[1], r.s_x_in.at[1], dp, mp ^ 2)

    def ffn_mine():
        ffn_third(flying.core[1])
        loads.weights = [
            wire.move(r.qkv_all.at[part], r.s_weights.at[:, pl.ds(part * lanes, lanes)])
            for part in range(3)
        ]
        loads.weights.append(wire.move(r.out_all, r.s_weights.at[:, to_heads]))

    def branch():
        flying.branch_far.wait_recv()
        branch_pass = push(r.s_slope.at[far], r.s_slope.at[far], dp, mp ^ 1)
        flying.branch_core.wait_recv()
        for copy in loads.heads + loads.weights:
            copy.wait()
        branch_pass.wait_recv()

    def grad_out():
        @pl.loop(0, width // 512)
        def _(tile):
            span = window(tile, 512)
            r.s_gout[span, :] = dot(
                r.s_slope[:, span], r.s_two[:, to_heads], by_tokens
            ).astype(low)

    def grad_heads():
        @pl.loop(0, group // 512)
        def _(tile):
            here = window(tile, 512)
            r.s_gheads[here, :] = dot(r.s_slope[here, :], r.s_weights[:, to_heads]).astype(low)

        for copy in loads.rest:
            copy.wait()

    def starts_of(index):
        token = index * rows + lax.broadcasted_iota(jnp.int32, (rows, 1), 0)
        first_token = jnp.int32(0)
        starts = jnp.zeros((rows, 1), jnp.int32)
        for seq in range(seqs):
            starts = jnp.where(token >= first_token, first_token, starts)
            first_token = first_token + r.lengths[0, seq]
        return starts

    def attend_back(head):
        span = pl.ds(head * HEAD, HEAD)
        k_span = pl.ds(lanes + head * HEAD, HEAD)
        v_span = pl.ds(2 * lanes + head * HEAD, HEAD)
        for index in reversed(range(mp_size)):
            here = pl.ds(index * rows, rows)
            seen = pl.ds(0, (index + 1) * rows)
            query, grad = r.s_two[here, span], r.s_gheads[here, span]
            begin = starts_of(index)
            probs = softmax_rows(query, r.s_two[seen, k_span], begin, index * rows, scale)
            grad_probs = dot(grad, r.s_two[seen, v_span], by_rows)
            inner_sum = jnp.sum(probs * grad_probs, axis=-1, keepdims=True)
            grad_scores = (probs * (grad_probs - inner_sum)).astype(low)
            query_grad = dot(grad_scores, r.s_two[seen, k_span]) * scale
            r.s_act[here, span] = turn(
                query_grad, r.s_cos[here, :], -r.s_sin[here, :]
            ).astype(low)
            key_part = dot(grad_scores, query, by_tokens)
            value_part = dot(probs.astype(low), grad, by_tokens)
            if index == mp_size - 1:
                r.s_gk[...] = key_part
                r.s_gv[...] = value_part
            else:
                r.s_gk[seen, :] += key_part
                r.s_gv[seen, :] += value_part
        for index in range(mp_size):
            here = pl.ds(index * rows, rows)
            r.s_act[here, k_span] = turn(
                r.s_gk[here, :] * scale, r.s_cos[here, :], -r.s_sin[here, :]
            ).astype(low)
            r.s_act[here, v_span] = r.s_gv[here, :].astype(low)

    def output():
        flying.ffn.wait_recv()
        sent(flying.ffn)

        @pl.loop(0, rows // 64)
        def _(index):
            here = window(index, 64)
            value = r.s_part[here, :] + r.s_x_in[1, here, :].astype(full)
            r.s_x_out[1, here, :] = (r.s_middle[here, :] + value + r.vectors[2:3, :]).astype(low)

        wire.store(r.s_x_out.at[1], r.output)
        loads.hidden = wire.move(r.hidden, r.s_x_in.at[1])

    def one_core():
        sent(*flying.core, flying.two)
        flying.core = one_first()

    def one_far():
        one_second(flying.core[0])
        flying.one = push(r.s_x_out.at[0], r.s_x_in.at[0], dp, mp ^ 2)

    def one_mine():
        one_third(flying.core[1])

    def grad_qkv():
        loads.normed.wait()

        @pl.loop(0, width // 256)
        def _(tile):
            span = window(tile, 256)
            r.s_gqkv[span, :] = dot(r.s_grads[:, span], r.s_act[:, mixed], by_tokens).astype(low)

    def store_own():
        own_slot = window(dp, shard)
        wire.store(r.s_gqkv.at[own_slot], r.own_qkv)
        wire.store(r.s_gout.at[own_slot], r.own_out)
        wire.store(r.s_up.at[own_slot], r.own_up)

    def norm_one():
        flying.one.wait_recv()
        loads.hidden.wait()

        @pl.loop(0, rows // 64)
        def _(index):
            here = window(index, 64)
            normed_grad = r.s_part[here, :] + r.s_x_in[0, here, :].astype(full)
            hidden = r.s_x_in[1, here, :].astype(full)
            ratio = lax.rsqrt(jnp.mean(hidden * hidden, axis=-1, keepdims=True) + norm_eps)
            weighted = normed_grad * r.vectors[0:1, :]
            r.s_back[here, :] = (
                r.s_back[here, :]
                + ratio * weighted
                - hidden * (ratio**3 * jnp.mean(weighted * hidden, axis=-1, keepdims=True))
            )
            r.s_sums[0:1, :] += jnp.sum(normed_grad * (hidden * ratio), axis=0, keepdims=True)

        wire.store(r.s_back, r.grad_in)

    lines = width // 128
    shared = 3 * lines

    def vec_mp():
        for line in range(4):
            for index in range((units if line == 3 else width) // 128):
                r.s_vec[line * lines + index : line * lines + index + 1, :] = r.s_sums[
                    line : line + 1, index * 128 : (index + 1) * 128
                ]
        flying.vec = [
            push(r.s_vec.at[pl.ds(0, shared)], r.s_vec_mp.at[step - 1], dp, mp ^ step)
            for step in range(1, mp_size)
        ]

    def vec_y():
        for copy in flying.vec:
            copy.wait_recv()
        sent(*flying.vec)
        for step in range(1, mp_size):
            r.s_vec[0:shared, :] += r.s_vec_mp[step - 1]
        flying.vec = [push(r.s_vec, r.s_vec_y, dp ^ 1, mp)]

    def vec_z():
        for copy in flying.vec:
            copy.wait_recv()
        sent(*flying.vec)
        r.s_vec[...] += r.s_vec_y[...]
        flying.vec = [
            push(r.s_vec, r.s_vec_z.at[step - 1], dp ^ (2 * step), mp)
            for step in range(1, rings)
        ]

    def vec_done():
        for copy in flying.vec:
            copy.wait_recv()
        total = r.s_vec[...]
        for step in range(1, rings):
            total = total + r.s_vec_z[step - 1]
        r.totals[...] = total

    order = [
        (launch, 0, 0), (launch, 1, 0), (launch, 0, 1), (launch, 1, 1), (load,), (unit_grads,),
        (launch, 0, 2), (launch, 1, 2), (two_core,), (two_far,), (tick, 1, 0), (two_mine,),
        (tick, 0, 0), (launch, 1, 3), (grad_up,), (launch, 2, 0), (launch, 3, 0), (tick, 1, 1),
        (launch, 2, 1), (tick, 0, 1), (norm_two,), (launch, 3, 1), (tick, 2, 0), (launch, 2, 2),
        (ffn_core,), (ffn_far,), (tick, 0, 2), (tick, 3, 0), (launch, 2, 3), (tick, 1, 2),
        (launch, 3, 2), (tick, 3, 1), (ffn_mine,), (tick, 2, 1), (branch,), (grad_out,),
        (grad_heads,), (attend_back, 0), (launch, 4, 0), (tick, 2, 2), (attend_back, 1),
        (launch, 0, 3), (attend_back, 2), (launch, 4, 1), (grad_qkv,), (launch, 6, 0), (output,),
        (one_core,), (one_far,), (launch, 6, 1), (tick, 4, 0), (tick, 3, 2), (launch, 4, 2),
        (one_mine,), (tick, 6, 0), (launch, 5, 0), (launch, 6, 2), (launch, 3, 3), (tick, 4, 1),
        (tick, 5, 0), (tick, 4, 2), (norm_one,), (tick, 6, 1), (vec_mp,), (vec_y,),
        (launch, 5, 1), (tick, 6, 2), (launch, 5, 2), (launch, 6, 3), (vec_z,), (tick, 5, 1),
        (launch, 4, 3), (tick, 5, 2), (store_own,), (launch, 5, 3), (vec_done,),
    ]
    for step, *where in order:
        step(*where)
    for index in range(len(pieces)):
        tick(index, 3)
    for index in range(len(pieces)):
        finish(index)
    wire.close()
    for copy in sends:
        copy.wait_send()


def run_backward(inputs, seqs):
    dp_size, mp_size = lax.axis_size("dp"), lax.axis_size("mp")
    rings = dp_size // 2
    rows, width = inputs["hidden"].shape
    group, units = inputs["slope"].shape
    lanes = inputs["heads"].shape[1]
    shard = width // dp_size
    vec_rows = (3 * width + units) // 128
    steps = len(onward("z", 0, dp_size))
    between = dp_size - 1 - steps
    shapes = dict(
        output=((rows, width), low),
        grad_in=((rows, width), full),
        own_qkv=((shard, 3 * lanes), low),
        own_out=((shard, lanes), low),
        own_up=((shard, units), low),
        totals=((vec_rows, 128), full),
        last_qkv=((steps, shard, 3 * lanes), low),
        last_out=((steps, shard, lanes), low),
        last_up=((steps, shard, units), low),
        last_down=((steps, shard, units), low),
    )
    scratch = [
        pltpu.VMEM(shape, kind)
        for shape, kind in (
            ((width, max(units, 4 * lanes)), low),
            ((width, units), low),
            ((group, max(units, width)), low),
            ((group, width), low),
            ((group, max(width, 4 * lanes)), low),
            ((group, max(units, 3 * lanes)), low),
            ((group, units), low),
            ((rings - 1, shard, units), low),
            ((between, shard, 3 * lanes), low),
            ((between, shard, lanes), low),
            ((between, shard, units), low),
            ((between, shard, units), low),
            ((width, 3 * lanes), low),
            ((width, lanes), low),
            ((2, 2, rows, width), low),
            ((2, rows, width), low),
            ((2, rows, width), low),
            ((2, rows, width), low),
            ((rows, width), full),
            ((rows, width), full),
            ((rows, width), full),
            ((group, lanes), low),
            ((group, HEAD), full),
            ((group, HEAD), full),
            ((group, HEAD), full),
            ((group, HEAD), full),
            ((8, max(width, units)), full),
            ((vec_rows, 128), full),
            ((mp_size - 1, 3 * width // 128, 128), full),
            ((vec_rows, 128), full),
            ((rings - 1, vec_rows, 128), full),
        )
    ]
    remote = 7 * (dp_size - 1) + 9 + 3 + mp_size + rings
    scratch += [
        pltpu.SemaphoreType.DMA((remote,)),
        pltpu.SemaphoreType.DMA((remote,)),
        pltpu.SemaphoreType.DMA((40 + 2 * rings + 7 * steps,)),
    ]
    anywhere = pl.BlockSpec(memory_space=pl.ANY)
    vector = pl.BlockSpec(memory_space=pltpu.VMEM)
    placed = dict(
        lengths=pl.BlockSpec(memory_space=pltpu.SMEM), vectors=vector, totals=vector
    )
    outs = pl.pallas_call(
        functools.partial(backward_kernel, seqs),
        out_shape=[jax.ShapeDtypeStruct(*shapes[name]) for name in BackwardOut._fields],
        in_specs=[placed.get(name, anywhere) for name in BackwardIn._fields],
        out_specs=[placed.get(name, anywhere) for name in BackwardOut._fields],
        scratch_shapes=scratch,
        compiler_params=pltpu.CompilerParams(
            collective_id=1, has_side_effects=True, vmem_limit_bytes=vmem_bytes
        ),
        name="backward",
    )(*[inputs[name] for name in BackwardIn._fields])
    return dict(zip(BackwardOut._fields, outs))


class CollectIn(typing.NamedTuple):
    output: object
    grad_in: object
    grad_down: object
    own_qkv: object
    own_out: object
    own_up: object
    last_qkv: object
    last_out: object
    last_up: object
    last_down: object
    totals: object


class CollectOut(typing.NamedTuple):
    output: object
    grad_in: object
    sum_qkv: object
    sum_out: object
    sum_up: object
    sum_down: object
    gain_one: object
    gain_two: object
    down_bias: object
    up_bias: object


class CollectScratch(typing.NamedTuple):
    s_qkv: object
    s_out: object
    s_up: object
    s_down: object
    t_qkv: object
    t_out: object
    t_up: object
    t_down: object
    s_output: object
    s_grad_in: object
    local: object


def collect_kernel(piece, pieces, *refs):
    names = [name + "_in" for name in CollectIn._fields]
    names += CollectOut._fields + CollectScratch._fields
    r = types.SimpleNamespace(**dict(zip(names, refs, strict=True)))
    dp, mp = lax.axis_index("dp"), lax.axis_index("mp")
    shard = r.s_up.shape[1]
    wire = Wire(None, None, r.local)
    own = [r.grad_down_in.at[window(dp, shard)], r.own_up_in, r.own_qkv_in, r.own_out_in]
    last = [r.last_down_in, r.last_up_in, r.last_qkv_in, r.last_out_in]
    parts = [r.s_down, r.s_up, r.s_qkv, r.s_out]
    sums = [r.t_down, r.t_up, r.t_qkv, r.t_out]
    results = [r.sum_down, r.sum_up, r.sum_qkv, r.sum_out]
    loads = []
    for index in range(4):
        count = last[index].shape[0]
        loads.append(
            [
                wire.move(last[index], parts[index].at[pl.ds(0, count)]),
                wire.move(own[index], parts[index].at[count]),
            ]
        )
    through = [
        (wire.move(r.output_in, r.s_output), r.s_output, r.output),
        (wire.move(r.grad_in_in, r.s_grad_in), r.s_grad_in, r.grad_in),
    ]
    for line, place in enumerate((r.gain_one, r.gain_two, r.down_bias)):
        start = (dp * lax.axis_size("mp") + mp) * piece
        row = start // 128 + line * (r.output.shape[1] // 128)
        lane = start % 128
        pair = jnp.concatenate(
            [r.totals_in[pl.ds(row, 1), :], r.totals_in[pl.ds(row + 1, 1), :]], axis=1
        )
        pair = pltpu.roll(jnp.broadcast_to(pair, (8, 256)), (256 - lane) % 256, 1)
        place[...] = pair[0:1, :piece].reshape(piece)
    start = dp * pieces
    row = start // 128 + 3 * (r.output.shape[1] // 128)
    lane = start % 128
    last_row = r.totals_in.shape[0] - 1
    pair = jnp.concatenate(
        [
            r.totals_in[pl.ds(row, 1), :],
            r.totals_in[pl.ds(jnp.minimum(row + 1, last_row), 1), :],
        ],
        axis=1,
    )
    pair = pltpu.roll(jnp.broadcast_to(pair, (8, 256)), (256 - lane) % 256, 1)
    r.up_bias[...] = pair[0:1, :pieces].reshape(pieces)
    for copy, source, target in through:
        copy.wait()
        wire.store(source, target)
    for index in range(4):
        for copy in loads[index]:
            copy.wait()
        count = parts[index].shape[0]

        @pl.loop(0, shard // 16)
        def _(step):
            here = window(step, 16)
            total = parts[index][0, here, :].astype(full)
            for place in range(1, count):
                total = total + parts[index][place, here, :].astype(full)
            sums[index][here, :] = total

        if index == 2:
            lanes = results[index].shape[2]
            for part in range(3):
                wire.store(
                    sums[index].at[:, pl.ds(part * lanes, lanes)], results[index].at[part]
                )
        else:
            wire.store(sums[index], results[index])
    wire.close()


def collect(inputs, piece, pieces):
    rows, width = inputs["output"].shape
    steps, shard, units = inputs["last_up"].shape
    lanes = inputs["last_out"].shape[2]
    shapes = dict(
        output=((rows, width), low),
        grad_in=((rows, width), full),
        sum_qkv=((3, shard, lanes), full),
        sum_out=((shard, lanes), full),
        sum_up=((shard, units), full),
        sum_down=((shard, units), full),
        gain_one=((piece,), full),
        gain_two=((piece,), full),
        down_bias=((piece,), full),
        up_bias=((pieces,), full),
    )
    scratch = [
        pltpu.VMEM(shape, kind)
        for shape, kind in (
            ((steps + 1, shard, 3 * lanes), low),
            ((steps + 1, shard, lanes), low),
            ((steps + 1, shard, units), low),
            ((steps + 1, shard, units), low),
            ((shard, 3 * lanes), full),
            ((shard, lanes), full),
            ((shard, units), full),
            ((shard, units), full),
            ((rows, width), low),
            ((rows, width), full),
        )
    ] + [pltpu.SemaphoreType.DMA((20,))]
    anywhere = pl.BlockSpec(memory_space=pl.ANY)
    vector = pl.BlockSpec(memory_space=pltpu.VMEM)
    placed = dict(
        totals=vector, gain_one=vector, gain_two=vector, down_bias=vector, up_bias=vector
    )
    outs = pl.pallas_call(
        functools.partial(collect_kernel, piece, pieces),
        out_shape=[jax.ShapeDtypeStruct(*shapes[name]) for name in CollectOut._fields],
        in_specs=[placed.get(name, anywhere) for name in CollectIn._fields],
        out_specs=[placed.get(name, anywhere) for name in CollectOut._fields],
        scratch_shapes=scratch,
        compiler_params=pltpu.CompilerParams(vmem_limit_bytes=vmem_bytes),
        name="collect",
    )(*[inputs[name] for name in CollectIn._fields])
    return dict(zip(CollectOut._fields, outs))


def shards(
    hidden_in,
    out_grad,
    seq_lengths,
    seq_grains,
    gain_attn,
    w_qkv,
    w_out,
    gain_ffn,
    w_up,
    bias_up,
    w_down,
    bias_down,
):
    dp, mp = lax.axis_index("dp"), lax.axis_index("mp")
    dp_size, mp_size = lax.axis_size("dp"), lax.axis_size("mp")
    width = hidden_in.shape[1]
    units = w_up.shape[1]
    seqs = seq_lengths.shape[1]
    spread, spread_up, targets = small_tables(width, units, dp_size, mp_size)
    done = run_forward(
        dict(
            hidden=hidden_in,
            grad=out_grad,
            w_qkv=w_qkv.transpose(1, 0, 2),
            w_out=w_out.T,
            w_up=w_up,
            w_down=w_down.T,
            gain_attn=gain_attn,
            gain_ffn=gain_ffn,
            bias_down=bias_down,
            bias_up=bias_up,
            spread=spread,
            spread_up=spread_up,
            targets=targets,
            inverse=rope_rows(),
            lengths=seq_lengths,
            grains=seq_grains,
        ),
        seqs,
    )
    back = run_backward(dict(done, hidden=hidden_in, lengths=seq_lengths), seqs)
    piece, pieces = gain_attn.shape[0], bias_up.shape[0]
    ends = collect(dict(back, grad_down=done["grad_down"]), piece, pieces)
    return (
        ends["output"],
        ends["grad_in"],
        ends["gain_one"],
        ends["sum_qkv"].transpose(1, 0, 2),
        ends["sum_out"].T,
        ends["gain_two"],
        ends["sum_up"],
        ends["up_bias"],
        ends["sum_down"].T,
        ends["down_bias"],
    )


def solution(mesh):
    return jax.shard_map(
        shards,
        mesh=mesh,
        in_specs=(
            P(("dp", "mp"), None),
            P(("dp", "mp"), None),
            P("dp", None),
            P("dp", None),
            P(("dp", "mp")),
            P("dp", None, "mp"),
            P("mp", "dp"),
            P(("dp", "mp")),
            P("dp", "mp"),
            P(("mp", "dp")),
            P("mp", "dp"),
            P(("dp", "mp")),
        ),
        out_specs=(
            P(("dp", "mp"), None),
            P(("dp", "mp"), None),
            P(("dp", "mp")),
            P("dp", None, "mp"),
            P("mp", "dp"),
            P(("dp", "mp")),
            P("dp", "mp"),
            P(("mp", "dp")),
            P("mp", "dp"),
            P(("dp", "mp")),
        ),
        check_vma=False,
    )
```

```python
import functools
import types
import typing

import jax
import jax.numpy as jnp
import numpy as np
from jax import lax
from jax.experimental import pallas as pl
from jax.experimental.pallas import tpu as pltpu
from jax.sharding import PartitionSpec as P

HEAD = 128
GRAIN = 768
MESH = pl.DeviceIdType.MESH
low = jnp.bfloat16
full = jnp.float32

norm_eps = 1e-06
rope_base = 10000.0
masked_score = -1e30
vmem_bytes = 62 * 2**20
root_half_pi = (2.0 / np.pi) ** 0.5
cubic = 0.044715

plain = (((1,), (0,)), ((), ()))
by_rows = (((1,), (1,)), ((), ()))
by_tokens = (((0,), (0,)), ((), ()))


def dot(first, second, dims=plain):
    return lax.dot_general(first, second, dims, preferred_element_type=jnp.float32)


def window(index, size):
    return pl.ds(pl.multiple_of(index * size, size), size)


class Wire:
    def __init__(self, sent, got, local):
        self.sent, self.got, self.local = sent, got, local
        self.used, self.used_local = 0, 0
        self.open = []

    def push(self, source, target, dp, mp):
        copy = pltpu.make_async_remote_copy(
            source,
            target,
            self.sent.at[self.used],
            self.got.at[self.used],
            device_id=(dp, mp),
            device_id_type=MESH,
        )
        self.used += 1
        copy.start()
        return copy

    def move(self, source, target):
        copy = pltpu.make_async_copy(source, target, self.local.at[self.used_local])
        self.used_local += 1
        copy.start()
        return copy

    def store(self, source, target):
        self.open.append(self.move(source, target))

    def close(self):
        for copy in self.open:
            copy.wait()
        self.open = []


def greet(dp, mp, dp_size, mp_size):
    barrier = pltpu.get_barrier_semaphore()
    for step in range(1, mp_size):
        pl.semaphore_signal(barrier, inc=1, device_id=(dp, mp ^ step), device_id_type=MESH)
    for step in range(1, dp_size):
        pl.semaphore_signal(barrier, inc=1, device_id=(dp ^ step, mp), device_id_type=MESH)
    pl.semaphore_wait(barrier, mp_size + dp_size - 2)


def cut(rows, *parts):
    edges = [16 * round(rows * part / 16) for part in parts]
    return [(a, b - a) for a, b in zip(edges[:-1], edges[1:]) if b > a]


def last_step(kind, k, dp_size):
    if k == 0:
        return 0
    if kind == "y":
        return (k & ~1) & -(k & ~1) if k > 1 else 1
    return k & -k


def onward(kind, k, dp_size):
    steps = []
    step = dp_size // 2
    while step:
        if step > 1:
            free = k < 2 or step < last_step(kind, k & ~1, dp_size)
        else:
            free = k == 0 or (kind == "z" and k > 1 and k % 2 == 0)
        if free:
            steps.append(step)
        step //= 2
    if kind == "z" and k % 2:
        return []
    if kind == "y" and k == 0:
        return [1] + steps[:-1]
    return steps


def turn(values, cosine, sine):
    return values * cosine + pltpu.roll(values, HEAD // 2, 1) * sine


def softmax_rows(query, keys, starts, first, scale):
    scores = dot(query, keys, by_rows) * scale
    key_index = lax.broadcasted_iota(jnp.int32, scores.shape, 1)
    row_index = first + lax.broadcasted_iota(jnp.int32, scores.shape, 0)
    allowed = (key_index >= starts) & (key_index <= row_index)
    scores = jnp.where(allowed, scores, masked_score)
    exponents = jnp.exp(scores - jnp.max(scores, axis=-1, keepdims=True))
    return exponents * (1.0 / jnp.sum(exponents, axis=-1, keepdims=True))


def gelu_both(value):
    square = value * value
    bend = jnp.tanh(value * (root_half_pi + (root_half_pi * cubic) * square))
    half = 0.5 + 0.5 * bend
    inner = root_half_pi + (3 * root_half_pi * cubic) * square
    return value * half, half + (0.5 * value) * (1.0 - bend * bend) * inner


class ForwardInputs(typing.NamedTuple):
    hidden: object
    grad: object
    w_qkv: object
    w_out: object
    w_up: object
    w_down: object
    pack: object
    spread: object
    spread_up: object
    targets: object
    inverse: object
    lengths: object
    grains: object


class ForwardOutputs(typing.NamedTuple):
    qkv_all: object
    out_all: object
    up_all: object
    down_all: object
    normed: object
    queries: object
    keys: object
    values: object
    heads: object
    middle: object
    normed_two: object
    activated: object
    slope: object
    grads: object
    grad_down: object
    cosine: object
    sine: object
    vectors: object


class ForwardScratch(typing.NamedTuple):
    s_hidden: object
    s_normed: object
    s_qkv: object
    s_out: object
    s_up: object
    s_q: object
    s_k: object
    s_v: object
    s_heads: object
    s_cos: object
    s_sin: object
    s_small: object
    s_starts: object
    s_widths: object
    s_core_out: object
    s_core_in: object
    s_x_out: object
    s_x_in: object
    s_part: object
    s_middle: object
    s_two: object
    s_act: object
    s_slope: object
    s_grads: object
    s_down: object
    sent: object
    got: object
    local: object


def forward_kernel(seqs, *refs):
    r = types.SimpleNamespace(
        **dict(zip(ForwardInputs._fields + ForwardOutputs._fields + ForwardScratch._fields, refs, strict=True))
    )
    dp, mp = lax.axis_index("dp"), lax.axis_index("mp")
    dp_size, mp_size = lax.axis_size("dp"), lax.axis_size("mp")
    rings = dp_size // 2
    rows, width = r.hidden.shape
    group = rows * mp_size
    shard = r.w_up.shape[0]
    units = r.w_up.shape[1]
    lanes = r.w_out.shape[1]
    heads = lanes // HEAD
    scale = HEAD ** (-0.5)
    wire = Wire(r.sent, r.got, r.local)

    def block(index):
        return window(index, rows)

    mine, core, far, far_core = block(mp), block(mp ^ 1), block(mp ^ 2), block(mp ^ 3)
    greet(dp, mp, dp_size, mp_size)

    r.s_small[dp, mp] = r.pack[...]
    small = [
        wire.push(r.s_small.at[dp, mp], r.s_small.at[dp, mp], dp, mp ^ step)
        for step in range(1, mp_size)
    ]
    hidden_far = wire.push(r.hidden, r.s_hidden.at[mine], dp, mp ^ 2)
    hidden_core = wire.push(r.hidden, r.s_hidden.at[mine], dp, mp ^ 1)
    own_hidden = wire.move(r.hidden, r.s_hidden.at[mine])

    sources = [r.w_qkv, r.w_out, r.w_up, r.w_down]
    targets = [r.s_qkv, r.s_out, r.s_up, r.down_all]
    pieces = [(0, "z") + span for span in cut(shard, 0, 0.5, 1)]
    pieces += [(1, "z", 0, shard)]
    pieces += [(2, "z") + span for span in cut(shard, 0, 0.5, 1)]
    pieces += [(3, kind) + span for kind, span in zip("zy", cut(shard, 0, 0.5, 1), strict=True)]
    route, waited = {}, set()

    def spot(weight, k, first, count):
        start = pl.multiple_of((dp ^ k) * shard + first, 16)
        return targets[weight].at[pl.ds(start, count)]

    def pass_on(index, k, steps):
        weight, kind, first, count = pieces[index]
        place = spot(weight, k, first, count)
        part = place if k else sources[weight].at[pl.ds(first, count)]
        for step in steps:
            route[index, k ^ step] = wire.push(part, place, dp ^ step, mp)

    def launch(index, steps=None):
        pass_on(index, 0, onward(pieces[index][1], 0, dp_size) if steps is None else steps)

    def tick(index, *ks):
        for k in ks:
            route[index, k].wait_recv()
            waited.add((index, k))
            pass_on(index, k, onward(pieces[index][1], k, dp_size))

    def ticks(index, part):
        kind = pieces[index][1]
        ks = [k for k in arrival[kind] if onward(kind, k, dp_size)]
        early = [k for k in ks if (k & -k if kind == "z" else k) > 1 and (k & (k - 1)) == 0]
        if kind == "y":
            early = [1]
        tick(index, *(early if part == 0 else [k for k in ks if k not in early]))

    def arrived(weight):
        for index, piece in enumerate(pieces):
            if piece[0] == weight:
                for k in arrival[piece[1]]:
                    if (index, k) not in waited:
                        route[index, k].wait_recv()

    arrival = {}
    for kind in "zy":
        found = [0]
        for k in found:
            found += [k ^ step for step in onward(kind, k, dp_size)]
        arrival[kind] = found[1:]

    launch(0)
    for copy in small:
        copy.wait_recv()
    small += [
        wire.push(r.s_small.at[dp], r.s_small.at[dp], dp ^ step, mp) for step in range(1, dp_size)
    ]
    launch(1)
    own_weights = [
        wire.move(sources[weight], targets[weight].at[window(dp, shard)]) for weight in range(4)
    ]

    token = lax.broadcasted_iota(jnp.int32, (group, 1), 0)
    first = jnp.int32(0)
    starts = jnp.zeros((group, 1), jnp.int32)
    widths = jnp.zeros((group, 1), jnp.int32)
    for seq in range(seqs):
        starts = jnp.where(token >= first, first, starts)
        widths = jnp.where(token >= first, jnp.left_shift(GRAIN, r.grains[0, seq]), widths)
        first = first + r.lengths[0, seq]
    r.s_starts[...] = starts
    r.s_widths[...] = widths
    ticks(0, 0)

    @pl.loop(0, group // 128)
    def _(index):
        here = window(index, 128)
        tokens = index * 128 + lax.broadcasted_iota(jnp.int32, (128, 1), 0)
        position = (tokens - r.s_starts[here, :]).astype(full)
        angles = position * r.inverse[0:1, :]
        r.s_cos[here, :] = jnp.cos(angles)
        r.s_sin[here, :] = jnp.sin(angles) * r.inverse[1:2, :]

    wire.store(r.s_cos, r.cosine)
    wire.store(r.s_sin, r.sine)
    ticks(1, 0)
    launch(2)

    for copy in small[mp_size - 1 :]:
        copy.wait_recv()
    devices = dp_size * mp_size * 8
    for start in range(0, width, 512):
        here = pl.ds(start, 512)
        packed = r.s_small[...].reshape(devices, 128).astype(low)
        spread = dot(packed, r.spread[:, here])
        row = lax.broadcasted_iota(jnp.int32, (devices, 1), 0)
        for line in range(3):
            chosen = row == r.targets[0:1, here] + line
            r.vectors[line : line + 1, here] = jnp.sum(
                jnp.where(chosen, spread, 0.0), axis=0, keepdims=True
            )
    for start in range(0, units, 512):
        here = pl.ds(start, 512)
        packed = r.s_small[...].reshape(devices, 128).astype(low)
        spread = dot(packed, r.spread_up[:, here])
        row = lax.broadcasted_iota(jnp.int32, (devices, 1), 0)
        chosen = row == r.targets[1:2, here] + mp * 8
        r.vectors[3:4, here] = jnp.sum(jnp.where(chosen, spread, 0.0), axis=0, keepdims=True)

    hidden_far.wait_recv()
    hidden_pass = wire.push(r.s_hidden.at[far], r.s_hidden.at[far], dp, mp ^ 1)
    own_grad = wire.move(r.grad, r.s_grads.at[mine])
    grad_far = wire.push(r.grad, r.s_grads.at[mine], dp, mp ^ 2)
    ticks(0, 1)
    launch(3)
    hidden_core.wait_recv()
    own_hidden.wait()
    hidden_pass.wait_recv()
    grad_core = wire.push(r.grad, r.s_grads.at[mine], dp, mp ^ 1)

    @pl.loop(0, group // 64)
    def _(index):
        here = window(index, 64)
        value = r.s_hidden[here, :].astype(full)
        ratio = lax.rsqrt(jnp.mean(value * value, axis=-1, keepdims=True) + norm_eps)
        r.s_normed[here, :] = (value * ratio * r.vectors[0:1, :]).astype(low)

    wire.store(r.s_normed, r.normed)
    ticks(1, 1)
    ticks(2, 0)
    for copy in own_weights:
        copy.wait()
    arrived(0)
    wire.store(r.s_qkv, r.qkv_all)

    @pl.loop(0, mp_size)
    def _(index):
        here = block(index)
        value = r.s_normed[here, :]
        cos, sin = r.s_cos[here, :], r.s_sin[here, :]
        for part, place in enumerate((r.s_q, r.s_k, r.s_v)):
            mixed = dot(value, r.s_qkv[:, pl.ds(part * lanes, lanes)])
            for head in range(heads):
                span = slice(head * HEAD, (head + 1) * HEAD)
                piece = mixed[:, span]
                if part < 2:
                    piece = turn(piece, cos, sin)
                place[here, span] = piece.astype(low)

    ticks(2, 1)
    launch(4)
    ticks(3, 0)
    wire.store(r.s_q, r.queries)
    wire.store(r.s_k, r.keys)
    wire.store(r.s_v, r.values)
    for index in range(mp_size):
        here = pl.ds(index * rows, rows)
        seen = pl.ds(0, (index + 1) * rows)

        @pl.loop(0, heads)
        def _(head):
            span = window(head, HEAD)
            probs = softmax_rows(
                r.s_q[here, span], r.s_k[seen, span], r.s_starts[here, :], index * rows, scale
            )
            r.s_heads[here, span] = dot(probs.astype(low), r.s_v[seen, span]).astype(low)

    wire.store(r.s_heads, r.heads)
    ticks(3, 1)
    launch(5)
    launch(6, [1])
    arrived(1)
    wire.store(r.s_out, r.out_all)

    def branch(index, put):
        value = r.s_heads[index, :]

        @pl.loop(0, width // 512)
        def _(tile):
            span = window(tile, 512)
            put(span, dot(value, r.s_out[span, :], by_rows))

    def put_core(slot):
        def put(span, value):
            r.s_core_out[slot, :, span] = value.astype(low)

        return put

    def put_far(span, value):
        r.s_x_out[:, span] = (value + r.s_core_in[0, :, span].astype(full)).astype(low)

    def put_mine(span, value):
        r.s_part[:, span] = value + r.s_core_in[1, :, span].astype(full)

    branch(far_core, put_core(0))
    core_first = wire.push(r.s_core_out.at[0], r.s_core_in.at[0], dp, mp ^ 1)
    branch(core, put_core(1))
    core_second = wire.push(r.s_core_out.at[1], r.s_core_in.at[1], dp, mp ^ 1)
    core_first.wait_recv()
    branch(far, put_far)
    branch_far = wire.push(r.s_x_out, r.s_x_in, dp, mp ^ 2)
    core_second.wait_recv()
    branch(mine, put_mine)
    ticks(4, 0)
    launch(6, [step for step in onward("y", 0, dp_size) if step > 1])
    ticks(6, 0)
    grad_far.wait_recv()
    grad_pass = wire.push(r.s_grads.at[far], r.s_grads.at[far], dp, mp ^ 1)
    branch_far.wait_recv()

    @pl.loop(0, rows // 64)
    def _(index):
        here = window(index, 64)
        there = pl.ds(pl.multiple_of(mp * rows + index * 64, 64), 64)
        value = r.s_hidden[there, :].astype(full) + (
            r.s_part[here, :] + r.s_x_in[here, :].astype(full)
        )
        r.s_middle[here, :] = value
        ratio = lax.rsqrt(jnp.mean(value * value, axis=-1, keepdims=True) + norm_eps)
        r.s_two[there, :] = (value * ratio * r.vectors[1:2, :]).astype(low)

    two_far = wire.push(r.s_two.at[mine], r.s_two.at[mine], dp, mp ^ 2)
    two_core = wire.push(r.s_two.at[mine], r.s_two.at[mine], dp, mp ^ 1)
    wire.store(r.s_middle, r.middle)
    ticks(4, 1)
    ticks(5, 0)
    ticks(5, 1)
    arrived(2)
    wire.store(r.s_up, r.up_all)

    def units_of(index):
        value = r.s_two[index, :]
        limit = r.s_widths[index, :] - mp * units

        @pl.loop(0, units // 512)
        def _(tile):
            span = window(tile, 512)
            pre_act = dot(value, r.s_up[:, span]) + r.vectors[3:4, span]
            unit = tile * 512 + lax.broadcasted_iota(jnp.int32, (1, 512), 1)
            on = unit < limit
            activated, slope = gelu_both(pre_act)
            r.s_act[index, span] = jnp.where(on, activated, 0.0).astype(low)
            r.s_slope[index, span] = jnp.where(on, slope, 0.0).astype(low)

    units_of(mine)
    two_far.wait_recv()
    two_pass = wire.push(r.s_two.at[far], r.s_two.at[far], dp, mp ^ 1)
    two_core.wait_recv()
    units_of(core)
    ticks(6, 1)
    units_of(far)
    two_pass.wait_recv()
    units_of(far_core)
    wire.store(r.s_two, r.normed_two)
    wire.store(r.s_act, r.activated)
    wire.store(r.s_slope, r.slope)
    grad_core.wait_recv()
    grad_pass.wait_recv()
    own_grad.wait()
    wire.store(r.s_grads, r.grads)

    @pl.loop(0, width // 256)
    def _(tile):
        span = window(tile, 256)
        r.s_down[span, :] = dot(r.s_grads[:, span], r.s_act[...], by_tokens).astype(low)

    wire.store(r.s_down, r.grad_down)
    arrived(3)
    wire.close()
    for copy in route.values():
        copy.wait_send()
    for copy in small:
        copy.wait_send()
    for copy in (
        hidden_far,
        hidden_core,
        hidden_pass,
        grad_far,
        grad_core,
        grad_pass,
        core_first,
        core_second,
        branch_far,
        two_far,
        two_core,
        two_pass,
    ):
        copy.wait_send()


def run_forward(inputs, seqs):
    hidden, w_up, w_out, w_qkv = inputs["hidden"], inputs["w_up"], inputs["w_out"], inputs["w_qkv"]
    dp_size, mp_size = lax.axis_size("dp"), lax.axis_size("mp")
    rows, width = hidden.shape
    group = rows * mp_size
    units, lanes = w_up.shape[1], w_out.shape[1]
    shapes = dict(
        qkv_all=((width, 3 * lanes), low),
        out_all=((width, lanes), low),
        up_all=((width, units), low),
        down_all=((width, units), low),
        normed=((group, width), low),
        queries=((group, lanes), low),
        keys=((group, lanes), low),
        values=((group, lanes), low),
        heads=((group, lanes), low),
        middle=((rows, width), full),
        normed_two=((group, width), low),
        activated=((group, units), low),
        slope=((group, units), low),
        grads=((group, width), low),
        grad_down=((width, units), low),
        cosine=((group, HEAD), full),
        sine=((group, HEAD), full),
        vectors=((8, width), full),
    )
    remote = mp_size - 1 + dp_size - 1 + 7 * (dp_size - 1) + 16
    scratch = [
        pltpu.VMEM(shape, kind)
        for shape, kind in (
            ((group, width), low),
            ((group, width), low),
            ((width, 3 * lanes), low),
            ((width, lanes), low),
            ((width, units), low),
            ((group, lanes), low),
            ((group, lanes), low),
            ((group, lanes), low),
            ((group, lanes), low),
            ((group, HEAD), full),
            ((group, HEAD), full),
            ((dp_size, mp_size, 8, 128), full),
            ((group, 1), jnp.int32),
            ((group, 1), jnp.int32),
            ((2, rows, width), low),
            ((2, rows, width), low),
            ((rows, width), low),
            ((rows, width), low),
            ((rows, width), full),
            ((rows, width), full),
            ((group, width), low),
            ((group, units), low),
            ((group, units), low),
            ((group, width), low),
            ((width, units), low),
        )
    ] + [
        pltpu.SemaphoreType.DMA((remote,)),
        pltpu.SemaphoreType.DMA((remote,)),
        pltpu.SemaphoreType.DMA((32,)),
    ]
    anywhere = pl.BlockSpec(memory_space=pl.ANY)
    vector = pl.BlockSpec(memory_space=pltpu.VMEM)
    scalar = pl.BlockSpec(memory_space=pltpu.SMEM)
    placed = dict(
        pack=vector,
        spread=vector,
        spread_up=vector,
        targets=vector,
        inverse=vector,
        lengths=scalar,
        grains=scalar,
        vectors=vector,
    )
    outs = pl.pallas_call(
        functools.partial(forward_kernel, seqs),
        out_shape=[jax.ShapeDtypeStruct(*shapes[name]) for name in ForwardOutputs._fields],
        in_specs=[placed.get(name, anywhere) for name in ForwardInputs._fields],
        out_specs=[placed.get(name, anywhere) for name in ForwardOutputs._fields],
        scratch_shapes=scratch,
        compiler_params=pltpu.CompilerParams(
            collective_id=0, has_side_effects=True, vmem_limit_bytes=vmem_bytes
        ),
        name="forward",
    )(*[inputs[name] for name in ForwardInputs._fields])
    return dict(zip(ForwardOutputs._fields, outs))


def small_tables(width, units, dp_size, mp_size):
    piece = width // (dp_size * mp_size)
    half = units // dp_size // 2
    lane = np.arange(128)[:, None]
    column = np.arange(width)[None, :]
    unit = np.arange(units)[None, :]
    spread = (column % piece == lane).astype(np.float32)
    spread_up = (unit % half == lane).astype(np.float32)
    targets = np.zeros((8, max(width, units)), np.int32)
    targets[0, :width] = column[0] // piece * 8
    targets[1, :units] = unit[0] // (2 * half) * (8 * mp_size) + 3 + unit[0] % (2 * half) // half
    return jnp.asarray(spread, low), jnp.asarray(spread_up, low), jnp.asarray(targets)


def rope_rows():
    index = np.arange(HEAD // 2, dtype=np.float32)
    inverse = np.float32(rope_base) ** (np.float32(-2.0) * index / np.float32(HEAD))
    table = np.zeros((8, HEAD), np.float32)
    table[0] = np.concatenate([inverse, inverse])
    table[1] = np.concatenate([-np.ones(HEAD // 2), np.ones(HEAD // 2)])
    return jnp.asarray(table)


def small_pack(gain_attn, gain_ffn, bias_down, bias_up):
    half = bias_up.shape[0] // 2
    lines = [gain_attn, gain_ffn, bias_down, bias_up[:half], bias_up[half:]]
    lines = [jnp.pad(line.astype(full), (0, 128 - line.shape[0])) for line in lines]
    return jnp.stack(lines + [jnp.zeros((128,), full)] * 3)


class BackwardInputs(typing.NamedTuple):
    hidden: object
    lengths: object
    vectors: object
    cosine: object
    sine: object
    qkv_all: object
    out_all: object
    up_all: object
    down_all: object
    normed: object
    queries: object
    keys: object
    values: object
    heads: object
    middle: object
    normed_two: object
    activated: object
    slope: object
    grads: object
    grad_down: object


class BackwardOutputs(typing.NamedTuple):
    output: object
    grad_in: object
    sum_qkv: object
    sum_out: object
    sum_up: object
    sum_down: object
    totals: object
    last_qkv: object
    last_out: object
    last_up: object
    last_down: object


class BackwardScratch(typing.NamedTuple):
    s_weights: object
    s_up: object
    s_slope: object
    s_grads: object
    s_two: object
    s_act: object
    s_pre: object
    s_own: object
    got_qkv: object
    got_out: object
    got_up: object
    got_down: object
    s_gqkv: object
    s_gout: object
    s_core_in: object
    s_x_in: object
    s_core_out: object
    s_x_out: object
    s_part: object
    s_middle: object
    s_back: object
    s_gheads: object
    s_gk: object
    s_gv: object
    s_cos: object
    s_sin: object
    s_hidden: object
    s_output: object
    s_sums: object
    s_vec: object
    s_vec_mp: object
    s_vec_y: object
    s_vec_z: object
    sent: object
    got: object
    local: object


def backward_kernel(seqs, *refs):
    r = types.SimpleNamespace(
        **dict(zip(BackwardInputs._fields + BackwardOutputs._fields + BackwardScratch._fields, refs, strict=True))
    )
    dp, mp = lax.axis_index("dp"), lax.axis_index("mp")
    dp_size, mp_size = lax.axis_size("dp"), lax.axis_size("mp")
    rings = dp_size // 2
    rows, width = r.hidden.shape
    group = rows * mp_size
    shard = width // dp_size
    units = r.slope.shape[1]
    lanes = r.heads.shape[1]
    heads = lanes // HEAD
    scale = HEAD ** (-0.5)
    wire = Wire(r.sent, r.got, r.local)
    sends = []

    def block(index):
        return window(index, rows)

    def push(source, target, to_dp, to_mp):
        copy = wire.push(source, target, to_dp, to_mp)
        sends.append(copy)
        return copy

    def sent(*copies):
        for copy in copies:
            copy.wait_send()
            sends[:] = [other for other in sends if other is not copy]

    mine, core, far, far_core = block(mp), block(mp ^ 1), block(mp ^ 2), block(mp ^ 3)

    barrier = pltpu.get_barrier_semaphore()
    for step in range(1, mp_size):
        pl.semaphore_signal(barrier, inc=1, device_id=(dp, mp ^ step), device_id_type=MESH)
    pl.semaphore_signal(barrier, inc=1, device_id=(dp ^ 1, mp), device_id_type=MESH)
    for step in range(1, rings):
        pl.semaphore_signal(barrier, inc=1, device_id=(dp ^ (2 * step), mp), device_id_type=MESH)
    pl.semaphore_wait(barrier, mp_size + rings - 1)

    local = dict(down=r.grad_down, up=r.s_up, out=r.s_gout, qkv=r.s_gqkv)
    landing = dict(down=r.got_down, up=r.got_up, out=r.got_out, qkv=r.got_qkv)
    final = dict(down=r.last_down, up=r.last_up, out=r.last_out, qkv=r.last_qkv)
    sum_of = dict(down=r.sum_down, up=r.sum_up, out=r.sum_out, qkv=r.sum_qkv)
    pieces = [("down", kind) + span for kind, span in zip("yz", cut(shard, 0, 0.5, 1), strict=True)]
    pieces += [("up", "z") + span for span in cut(shard, 0, 0.5, 1)]
    pieces += [("out", "z", 0, shard)]
    pieces += [("qkv", "z") + span for span in cut(shard, 0, 0.5, 1)]
    inner, leaves, middle_slots, route, own = {}, {}, {}, {}, {}
    for kind in "zy":
        found = [0]
        for k in found:
            found += [k ^ step for step in onward(kind, k, dp_size)]
        inner[kind] = [k for k in found if onward(kind, k, dp_size)]
        leaves[kind] = [k for k in found[::-1] if not onward(kind, k, dp_size)]
        pairs = [(k, step) for k in inner[kind][1:] for step in onward(kind, k, dp_size)]
        middle_slots[kind] = {pair: place for place, pair in enumerate(pairs)}

    def rows_of(index, k):
        name, kind, first, count = pieces[index]
        return pl.ds(pl.multiple_of((dp ^ k) * shard + first, 16), count)

    def spot(index, k, step):
        name, kind, first, count = pieces[index]
        span = pl.ds(first, count)
        if k == 0:
            return final[name].at[onward(kind, 0, dp_size).index(step), span]
        return landing[name].at[middle_slots[kind][k, step], span]

    def climb(index, k, source):
        kind = pieces[index][1]
        step = last_step(kind, k, dp_size)
        route[index, k ^ step, step] = push(source, spot(index, k ^ step, step), dp ^ step, mp)

    def launch(index, *ks):
        for k in ks:
            climb(index, k, local[pieces[index][0]].at[rows_of(index, k)])

    def launch_both(first, second, ks):
        for k in ks:
            launch(first, k)
            launch(second, k)

    def own_load(index):
        name, kind, first, count = pieces[index]
        for place, k in enumerate(inner[kind]):
            own[index, k] = wire.move(
                local[name].at[rows_of(index, k)], r.s_own.at[place, pl.ds(first, count)]
            )

    def own_part(index, k, start, count):
        name, kind, first, _ = pieces[index]
        if name == "down":
            return r.s_own[inner[kind].index(k), pl.ds(first + start, count), :].astype(full)
        place = pl.multiple_of((dp ^ k) * shard + first + start, 16)
        return local[name][pl.ds(place, count), :].astype(full)

    def tick(index, *ks):
        name, kind, first, count = pieces[index]
        part = 48 if count % 48 == 0 else 16
        for k in ks:
            steps = onward(kind, k, dp_size)
            for step in steps:
                route[index, k, step].wait_recv()
            if name == "down":
                own[index, k].wait()

            @pl.loop(0, count // part)
            def _(turn_index):
                start = pl.multiple_of(turn_index * part, 16)
                here = pl.ds(pl.multiple_of(first + start, 16), part)
                total = own_part(index, k, start, part)
                for step in steps:
                    slot_index = middle_slots[kind][k, step]
                    total = total + landing[name][slot_index, here, :].astype(full)
                landing[name][middle_slots[kind][k, steps[0]], here, :] = total.astype(low)

            climb(index, k, spot(index, k, steps[0]))

    def finish(index, stage):
        name, kind, first, count = pieces[index]
        columns = final[name].shape[2]
        span = pl.ds(0, columns)
        steps = onward(kind, 0, dp_size)
        base = index % 2 * (group // 2)
        loads = []
        for place, step in enumerate(steps):
            route[index, 0, step].wait_recv()
            loads.append(
                wire.move(
                    spot(index, 0, step), r.s_pre.at[pl.ds(base + place * count, count), span]
                )
            )
        if name == "down":
            own[index, 0].wait()
        for copy in loads:
            copy.wait()
        part = 48 if count % 48 == 0 else 16

        @pl.loop(0, count // part)
        def _(turn_index):
            start = pl.multiple_of(turn_index * part, 16)
            total = own_part(index, 0, start, part)
            for place in range(len(steps)):
                there = pl.multiple_of(base + place * count + start, 16)
                total = total + r.s_pre[pl.ds(there, part), span].astype(full)
            stage[pl.ds(pl.multiple_of(first + start, 16), part), span] = total

        here = pl.ds(first, count)
        return wire.move(stage.at[here, span], sum_of[name].at[here])

    def reduce_start(left, right, columns, slot_in):
        def product(index, put):
            value = left[index, columns]

            @pl.loop(0, width // 512)
            def _(tile):
                span = window(tile, 512)
                put(span, dot(value, right[span, columns], by_rows))

        def put_core(place):
            def put(span, value):
                r.s_core_out[place, :, span] = value.astype(low)

            return put

        def put_far(span, value):
            value = value + r.s_core_in[slot_in, 0, :, span].astype(full)
            r.s_x_out[slot_in, :, span] = value.astype(low)

        def put_mine(span, value):
            r.s_part[:, span] = value + r.s_core_in[slot_in, 1, :, span].astype(full)

        def first():
            product(far_core, put_core(0))
            one = push(r.s_core_out.at[0], r.s_core_in.at[slot_in, 0], dp, mp ^ 1)
            product(core, put_core(1))
            two = push(r.s_core_out.at[1], r.s_core_in.at[slot_in, 1], dp, mp ^ 1)
            return one, two

        def second(one):
            one.wait_recv()
            product(far, put_far)

        def third(two):
            two.wait_recv()
            product(mine, put_mine)

        return first, second, third

    load_grads = wire.move(r.grads, r.s_grads)
    load_down = wire.move(r.down_all, r.s_weights)
    load_slope = wire.move(r.slope, r.s_slope)
    for one, two in zip(leaves["y"], leaves["z"], strict=True):
        launch(0, one)
        launch(1, two)
    load_up = wire.move(r.up_all, r.s_up)
    load_two = wire.move(r.normed_two, r.s_two)
    load_act = wire.move(r.activated, r.s_act)
    load_middle = wire.move(r.middle, r.s_middle)
    own_load(1)
    own_load(0)
    load_rest = [
        wire.move(r.cosine, r.s_cos),
        wire.move(r.sine, r.s_sin),
        wire.move(r.hidden, r.s_hidden),
    ]
    r.s_sums[...] = jnp.zeros_like(r.s_sums)
    load_grads.wait()
    load_down.wait()
    load_slope.wait()

    @pl.loop(0, units // 512)
    def _(tile):
        span = window(tile, 512)
        value = dot(r.s_grads[...], r.s_weights[:, span]) * r.s_slope[:, span].astype(full)
        value = value.astype(low)
        r.s_pre[:, span] = value
        r.s_sums[3:4, span] = jnp.sum(value.astype(full), axis=0, keepdims=True)

    early = [k for k in inner["z"][:0:-1] if len(onward("z", k, dp_size)) == 1]
    late = [k for k in inner["z"][:0:-1] if k not in early]
    early_y = [k for k in inner["y"][:0:-1] if len(onward("y", k, dp_size)) == 1]
    late_y = [k for k in inner["y"][:0:-1] if k not in early_y]
    load_up.wait()
    everything = pl.ds(0, units)
    first, second, third = reduce_start(r.s_pre, r.s_up, everything, 0)
    one, two = first()
    second(one)
    two_far = push(r.s_x_out.at[0], r.s_x_in.at[0], dp, mp ^ 2)
    third(two)
    tick(1, *early)
    load_two.wait()

    @pl.loop(0, width // 256)
    def _(tile):
        span = window(tile, 256)
        r.s_up[span, :] = dot(r.s_two[:, span], r.s_pre[...], by_tokens).astype(low)

    launch_both(2, 3, leaves["z"])
    tick(0, *early_y)
    load_heads = [
        wire.move(place, r.s_two.at[:, pl.ds(index * lanes, lanes)])
        for index, place in enumerate((r.queries, r.keys, r.values, r.heads))
    ]
    load_middle.wait()
    two_far.wait_recv()

    @pl.loop(0, rows // 64)
    def _(index):
        here = window(index, 64)
        there = pl.ds(pl.multiple_of(mp * rows + index * 64, 64), 64)
        normed_grad = r.s_part[here, :] + r.s_x_in[0, here, :].astype(full)
        middle = r.s_middle[here, :]
        grad = r.s_grads[there, :].astype(full)
        ratio = lax.rsqrt(jnp.mean(middle * middle, axis=-1, keepdims=True) + norm_eps)
        weighted = normed_grad * r.vectors[1:2, :]
        back = (
            grad
            + ratio * weighted
            - middle * (ratio**3 * jnp.mean(weighted * middle, axis=-1, keepdims=True))
        )
        r.s_back[here, :] = back
        r.s_slope[there, :] = back.astype(low)
        r.s_sums[1:2, :] += jnp.sum(normed_grad * (middle * ratio), axis=0, keepdims=True)
        r.s_sums[2:3, :] += jnp.sum(grad, axis=0, keepdims=True)

    branch_far = push(r.s_slope.at[mine], r.s_slope.at[mine], dp, mp ^ 2)
    branch_core = push(r.s_slope.at[mine], r.s_slope.at[mine], dp, mp ^ 1)
    load_normed = wire.move(r.normed, r.s_grads)

    load_act.wait()
    first, second, third = reduce_start(r.s_act, r.s_weights, everything, 1)
    sent(one, two)
    one, two = first()
    second(one)
    ffn_far = push(r.s_x_out.at[1], r.s_x_in.at[1], dp, mp ^ 2)
    third(two)
    load_weights = [
        wire.move(r.qkv_all, r.s_weights.at[:, pl.ds(0, 3 * lanes)]),
        wire.move(r.out_all, r.s_weights.at[:, pl.ds(3 * lanes, lanes)]),
    ]
    tick(1, *late)
    tick(2, *early)
    tick(0, *late_y)
    tick(3, *early)
    branch_far.wait_recv()
    branch_pass = push(r.s_slope.at[far], r.s_slope.at[far], dp, mp ^ 1)
    branch_core.wait_recv()
    for copy in load_heads + load_weights:
        copy.wait()
    branch_pass.wait_recv()
    to_heads = pl.ds(3 * lanes, lanes)

    @pl.loop(0, width // 512)
    def _(tile):
        span = window(tile, 512)
        r.s_gout[span, :] = dot(r.s_slope[:, span], r.s_two[:, to_heads], by_tokens).astype(low)

    launch(4, *leaves["z"])

    @pl.loop(0, group // 512)
    def _(tile):
        here = window(tile, 512)
        r.s_gheads[here, :] = dot(r.s_slope[here, :], r.s_weights[:, to_heads]).astype(low)


    for copy in load_rest:
        copy.wait()
    token = lax.broadcasted_iota(jnp.int32, (group, 1), 0)
    first_token = jnp.int32(0)
    starts = jnp.zeros((group, 1), jnp.int32)
    for seq in range(seqs):
        starts = jnp.where(token >= first_token, first_token, starts)
        first_token = first_token + r.lengths[0, seq]

    @pl.loop(0, heads)
    def _(head):
        span = window(head, HEAD)
        k_span = pl.ds(pl.multiple_of(lanes + head * HEAD, HEAD), HEAD)
        v_span = pl.ds(pl.multiple_of(2 * lanes + head * HEAD, HEAD), HEAD)
        for index in reversed(range(mp_size)):
            here = pl.ds(index * rows, rows)
            seen = pl.ds(0, (index + 1) * rows)
            query, grad = r.s_two[here, span], r.s_gheads[here, span]
            begin = starts[index * rows : (index + 1) * rows]
            probs = softmax_rows(query, r.s_two[seen, k_span], begin, index * rows, scale)
            grad_probs = dot(grad, r.s_two[seen, v_span], by_rows)
            inner = jnp.sum(probs * grad_probs, axis=-1, keepdims=True)
            grad_scores = (probs * (grad_probs - inner)).astype(low)
            query_grad = dot(grad_scores, r.s_two[seen, k_span]) * scale
            r.s_act[here, span] = turn(
                query_grad, r.s_cos[here, :], -r.s_sin[here, :]
            ).astype(low)
            key_part = dot(grad_scores, query, by_tokens)
            value_part = dot(probs.astype(low), grad, by_tokens)
            if index == mp_size - 1:
                r.s_gk[...] = key_part
                r.s_gv[...] = value_part
            else:
                r.s_gk[seen, :] += key_part
                r.s_gv[seen, :] += value_part
        for index in range(mp_size):
            here = pl.ds(index * rows, rows)
            r.s_act[here, k_span] = turn(
                r.s_gk[here, :] * scale, r.s_cos[here, :], -r.s_sin[here, :]
            ).astype(low)
            r.s_act[here, v_span] = r.s_gv[here, :].astype(low)

    tick(2, *late)
    tick(3, *late)

    mixed = pl.ds(0, 3 * lanes)
    first, second, third = reduce_start(r.s_act, r.s_weights, mixed, 0)
    sent(one, two, two_far)
    ffn_far.wait_recv()

    @pl.loop(0, rows // 64)
    def _(index):
        here = window(index, 64)
        value = r.s_part[here, :] + r.s_x_in[1, here, :].astype(full)
        r.s_output[here, :] = (r.s_middle[here, :] + value + r.vectors[2:3, :]).astype(low)

    wire.store(r.s_output, r.output)
    one, two = first()
    second(one)
    one_far = push(r.s_x_out.at[0], r.s_x_in.at[0], dp, mp ^ 2)
    third(two)
    load_normed.wait()

    @pl.loop(0, width // 256)
    def _(tile):
        span = window(tile, 256)
        r.s_gqkv[span, :] = dot(r.s_grads[:, span], r.s_act[:, mixed], by_tokens).astype(low)

    launch_both(5, 6, leaves["z"][:-1])
    tick(4, *early)
    done = [finish(0, r.s_middle), finish(1, r.s_middle)]
    tick(4, *late)
    one_far.wait_recv()

    @pl.loop(0, rows // 64)
    def _(index):
        here = window(index, 64)
        normed_grad = r.s_part[here, :] + r.s_x_in[0, here, :].astype(full)
        hidden = r.s_hidden[here, :].astype(full)
        ratio = lax.rsqrt(jnp.mean(hidden * hidden, axis=-1, keepdims=True) + norm_eps)
        weighted = normed_grad * r.vectors[0:1, :]
        r.s_back[here, :] = (
            r.s_back[here, :]
            + ratio * weighted
            - hidden * (ratio**3 * jnp.mean(weighted * hidden, axis=-1, keepdims=True))
        )
        r.s_sums[0:1, :] += jnp.sum(normed_grad * (hidden * ratio), axis=0, keepdims=True)

    wire.store(r.s_back, r.grad_in)

    lines = width // 128
    for line in range(4):
        for index in range((units if line == 3 else width) // 128):
            r.s_vec[line * lines + index : line * lines + index + 1, :] = r.s_sums[
                line : line + 1, index * 128 : (index + 1) * 128
            ]
    shared = 3 * lines
    vec_mp = [
        push(r.s_vec.at[pl.ds(0, shared)], r.s_vec_mp.at[step - 1], dp, mp ^ step)
        for step in range(1, mp_size)
    ]
    tick(5, *early)
    for copy in vec_mp:
        copy.wait_recv()
    sent(*vec_mp)
    for step in range(1, mp_size):
        r.s_vec[0:shared, :] += r.s_vec_mp[step - 1]
    vec_y = push(r.s_vec, r.s_vec_y, dp ^ 1, mp)
    launch_both(5, 6, leaves["z"][-1:])
    tick(6, *early)
    done += [finish(2, r.s_part), finish(3, r.s_part)]
    vec_y.wait_recv()
    sent(vec_y)
    r.s_vec[...] += r.s_vec_y[...]
    vec_z = [
        push(r.s_vec, r.s_vec_z.at[step - 1], dp ^ (2 * step), mp) for step in range(1, rings)
    ]
    tick(5, *late)
    tick(6, *late)
    for copy in done[2:4]:
        copy.wait()
    done += [finish(4, r.s_part)]
    for copy in vec_z:
        copy.wait_recv()
    total = r.s_vec[...]
    for step in range(1, rings):
        total = total + r.s_vec_z[step - 1]
    r.totals[...] = total
    for copy in done[:2]:
        copy.wait()
    done += [finish(5, r.s_middle), finish(6, r.s_middle)]
    for copy in done[4:]:
        copy.wait()
    wire.close()
    for copy in sends:
        copy.wait_send()


def run_backward(inputs, seqs):
    dp_size, mp_size = lax.axis_size("dp"), lax.axis_size("mp")
    rings = dp_size // 2
    rows, width = inputs["hidden"].shape
    group, units = inputs["slope"].shape
    lanes = inputs["heads"].shape[1]
    shard = width // dp_size
    vec_rows = (3 * width + units) // 128
    steps = len(onward("z", 0, dp_size))
    between = dp_size - 1 - steps
    shapes = dict(
        output=((rows, width), low),
        grad_in=((rows, width), full),
        sum_qkv=((shard, 3 * lanes), full),
        sum_out=((shard, lanes), full),
        sum_up=((shard, units), full),
        sum_down=((shard, units), full),
        totals=((vec_rows, 128), full),
        last_qkv=((steps, shard, 3 * lanes), low),
        last_out=((steps, shard, lanes), low),
        last_up=((steps, shard, units), low),
        last_down=((steps, shard, units), low),
    )
    scratch = [
        pltpu.VMEM(shape, kind)
        for shape, kind in (
            ((width, max(units, 4 * lanes)), low),
            ((width, units), low),
            ((group, max(units, width)), low),
            ((group, width), low),
            ((group, max(width, 4 * lanes)), low),
            ((group, max(units, 3 * lanes)), low),
            ((group, units), low),
            ((rings, shard, units), low),
            ((between, shard, 3 * lanes), low),
            ((between, shard, lanes), low),
            ((between, shard, units), low),
            ((between, shard, units), low),
            ((width, 3 * lanes), low),
            ((width, lanes), low),
            ((2, 2, rows, width), low),
            ((2, rows, width), low),
            ((2, rows, width), low),
            ((2, rows, width), low),
            ((rows, width), full),
            ((rows, width), full),
            ((rows, width), full),
            ((group, lanes), low),
            ((group, HEAD), full),
            ((group, HEAD), full),
            ((group, HEAD), full),
            ((group, HEAD), full),
            ((rows, width), low),
            ((rows, width), low),
            ((8, max(width, units)), full),
            ((vec_rows, 128), full),
            ((mp_size - 1, 3 * width // 128, 128), full),
            ((vec_rows, 128), full),
            ((rings - 1, vec_rows, 128), full),
        )
    ]
    remote = 7 * (dp_size - 1) + 9 + 3 + mp_size + rings
    scratch += [
        pltpu.SemaphoreType.DMA((remote,)),
        pltpu.SemaphoreType.DMA((remote,)),
        pltpu.SemaphoreType.DMA((40 + 2 * rings + 7 * steps,)),
    ]
    anywhere = pl.BlockSpec(memory_space=pl.ANY)
    vector = pl.BlockSpec(memory_space=pltpu.VMEM)
    placed = dict(
        lengths=pl.BlockSpec(memory_space=pltpu.SMEM), vectors=vector, totals=vector
    )
    outs = pl.pallas_call(
        functools.partial(backward_kernel, seqs),
        out_shape=[jax.ShapeDtypeStruct(*shapes[name]) for name in BackwardOutputs._fields],
        in_specs=[placed.get(name, anywhere) for name in BackwardInputs._fields],
        out_specs=[placed.get(name, anywhere) for name in BackwardOutputs._fields],
        scratch_shapes=scratch,
        compiler_params=pltpu.CompilerParams(
            collective_id=1, has_side_effects=True, vmem_limit_bytes=vmem_bytes
        ),
        name="backward",
    )(*[inputs[name] for name in BackwardInputs._fields])
    return dict(zip(BackwardOutputs._fields, outs))


def shards(
    hidden_in,
    out_grad,
    seq_lengths,
    seq_grains,
    gain_attn,
    w_qkv,
    w_out,
    gain_ffn,
    w_up,
    bias_up,
    w_down,
    bias_down,
):
    dp, mp = lax.axis_index("dp"), lax.axis_index("mp")
    dp_size, mp_size = lax.axis_size("dp"), lax.axis_size("mp")
    width = hidden_in.shape[1]
    units = w_up.shape[1]
    seqs = seq_lengths.shape[1]
    spread, spread_up, targets = small_tables(width, units, dp_size, mp_size)
    done = run_forward(
        dict(
            hidden=hidden_in,
            grad=out_grad,
            w_qkv=w_qkv.reshape(w_qkv.shape[0], -1),
            w_out=w_out.T,
            w_up=w_up,
            w_down=w_down.T,
            pack=small_pack(gain_attn, gain_ffn, bias_down, bias_up),
            spread=spread,
            spread_up=spread_up,
            targets=targets,
            inverse=rope_rows(),
            lengths=seq_lengths,
            grains=seq_grains,
        ),
        seqs,
    )
    back = run_backward(dict(done, hidden=hidden_in, lengths=seq_lengths), seqs)
    totals = back["totals"].reshape(-1)
    piece, pieces = gain_attn.shape[0], bias_up.shape[0]

    def own(line):
        return lax.dynamic_slice_in_dim(
            totals[line * width : (line + 1) * width], (dp * mp_size + mp) * piece, piece
        )

    return (
        back["output"],
        back["grad_in"],
        own(0),
        back["sum_qkv"].reshape(w_qkv.shape),
        back["sum_out"].T,
        own(1),
        back["sum_up"],
        lax.dynamic_slice_in_dim(totals[3 * width :], dp * pieces, pieces),
        back["sum_down"].T,
        own(2),
    )


def solution(mesh):
    return jax.shard_map(
        shards,
        mesh=mesh,
        in_specs=(
            P(("dp", "mp"), None),
            P(("dp", "mp"), None),
            P("dp", None),
            P("dp", None),
            P(("dp", "mp")),
            P("dp", None, "mp"),
            P("mp", "dp"),
            P(("dp", "mp")),
            P("dp", "mp"),
            P(("mp", "dp")),
            P("mp", "dp"),
            P(("dp", "mp")),
        ),
        out_specs=(
            P(("dp", "mp"), None),
            P(("dp", "mp"), None),
            P(("dp", "mp")),
            P("dp", None, "mp"),
            P("mp", "dp"),
            P(("dp", "mp")),
            P("dp", "mp"),
            P(("mp", "dp")),
            P("mp", "dp"),
            P(("dp", "mp")),
        ),
        check_vma=False,
    )
```

```python
import functools
import types
import typing

import jax
import jax.numpy as jnp
import numpy as np
from jax import lax
from jax.experimental import pallas as pl
from jax.experimental.pallas import tpu as pltpu
from jax.sharding import PartitionSpec as P

HEAD = 128
GRAIN = 768
MESH = pl.DeviceIdType.MESH
low = jnp.bfloat16
full = jnp.float32

norm_eps = 1e-06
rope_base = 10000.0
masked_score = -1e30
vmem_bytes = 62 * 2**20
root_half_pi = (2.0 / np.pi) ** 0.5
cubic = 0.044715

plain = (((1,), (0,)), ((), ()))
by_rows = (((1,), (1,)), ((), ()))
by_tokens = (((0,), (0,)), ((), ()))


def dot(first, second, dims=plain):
    return lax.dot_general(first, second, dims, preferred_element_type=jnp.float32)


def window(index, size):
    return pl.ds(pl.multiple_of(index * size, size), size)


class Wire:
    def __init__(self, sent, got, local):
        self.sent, self.got, self.local = sent, got, local
        self.used, self.used_local = 0, 0
        self.open = []

    def push(self, source, target, dp, mp):
        copy = pltpu.make_async_remote_copy(
            source,
            target,
            self.sent.at[self.used],
            self.got.at[self.used],
            device_id=(dp, mp),
            device_id_type=MESH,
        )
        self.used += 1
        copy.start()
        return copy

    def move(self, source, target):
        copy = pltpu.make_async_copy(source, target, self.local.at[self.used_local])
        self.used_local += 1
        copy.start()
        return copy

    def store(self, source, target):
        self.open.append(self.move(source, target))

    def close(self):
        for copy in self.open:
            copy.wait()
        self.open = []


def greet(dp, mp, dp_size, mp_size):
    barrier = pltpu.get_barrier_semaphore()
    for step in range(1, mp_size):
        pl.semaphore_signal(barrier, inc=1, device_id=(dp, mp ^ step), device_id_type=MESH)
    for step in range(1, dp_size):
        pl.semaphore_signal(barrier, inc=1, device_id=(dp ^ step, mp), device_id_type=MESH)
    pl.semaphore_wait(barrier, mp_size + dp_size - 2)


def split_rows(rows, first, parts):
    edges = [first + 16 * round(rows * part / 16) for part in parts]
    return [(a, b - a) for a, b in zip(edges[:-1], edges[1:]) if b > a]


def turn(values, cosine, sine):
    return values * cosine + pltpu.roll(values, HEAD // 2, 1) * sine


def softmax_rows(query, keys, starts, first, scale):
    scores = dot(query, keys, by_rows) * scale
    key_index = lax.broadcasted_iota(jnp.int32, scores.shape, 1)
    row_index = first + lax.broadcasted_iota(jnp.int32, scores.shape, 0)
    allowed = (key_index >= starts) & (key_index <= row_index)
    scores = jnp.where(allowed, scores, masked_score)
    exponents = jnp.exp(scores - jnp.max(scores, axis=-1, keepdims=True))
    return exponents * (1.0 / jnp.sum(exponents, axis=-1, keepdims=True))


def gelu_both(value):
    square = value * value
    bend = jnp.tanh(value * (root_half_pi + (root_half_pi * cubic) * square))
    half = 0.5 + 0.5 * bend
    inner = root_half_pi + (3 * root_half_pi * cubic) * square
    return value * half, half + (0.5 * value) * (1.0 - bend * bend) * inner


class ForwardInputs(typing.NamedTuple):
    hidden: object
    grad: object
    w_qkv: object
    w_out: object
    w_up: object
    w_down: object
    pack: object
    spread: object
    spread_up: object
    targets: object
    inverse: object
    lengths: object
    grains: object


class ForwardOutputs(typing.NamedTuple):
    qkv_all: object
    out_all: object
    up_all: object
    down_all: object
    normed: object
    queries: object
    keys: object
    values: object
    heads: object
    middle: object
    normed_two: object
    activated: object
    slope: object
    grads: object
    grad_down: object
    cosine: object
    sine: object
    vectors: object


class ForwardScratch(typing.NamedTuple):
    s_hidden: object
    s_normed: object
    s_qkv: object
    s_out: object
    s_up: object
    s_q: object
    s_k: object
    s_v: object
    s_heads: object
    s_cos: object
    s_sin: object
    s_small: object
    s_starts: object
    s_widths: object
    s_core_out: object
    s_core_in: object
    s_x_out: object
    s_x_in: object
    s_part: object
    s_middle: object
    s_two: object
    s_act: object
    s_slope: object
    s_grads: object
    s_down: object
    sent: object
    got: object
    local: object


def forward_kernel(seqs, *refs):
    r = types.SimpleNamespace(
        **dict(zip(ForwardInputs._fields + ForwardOutputs._fields + ForwardScratch._fields, refs, strict=True))
    )
    dp, mp = lax.axis_index("dp"), lax.axis_index("mp")
    dp_size, mp_size = lax.axis_size("dp"), lax.axis_size("mp")
    rings = dp_size // 2
    rows, width = r.hidden.shape
    group = rows * mp_size
    shard = r.w_up.shape[0]
    units = r.w_up.shape[1]
    lanes = r.w_out.shape[1]
    heads = lanes // HEAD
    scale = HEAD ** (-0.5)
    wire = Wire(r.sent, r.got, r.local)

    def block(index):
        return window(index, rows)

    mine, core, far, far_core = block(mp), block(mp ^ 1), block(mp ^ 2), block(mp ^ 3)
    greet(dp, mp, dp_size, mp_size)

    own_hidden = wire.move(r.hidden, r.s_hidden.at[mine])
    hidden_far = wire.push(r.hidden, r.s_hidden.at[mine], dp, mp ^ 2)
    r.s_small[dp, mp] = r.pack[...]
    small = [
        wire.push(r.s_small.at[dp, mp], r.s_small.at[dp, mp], dp, mp ^ step)
        for step in range(1, mp_size)
    ]
    hidden_core = wire.push(r.hidden, r.s_hidden.at[mine], dp, mp ^ 1)

    sources = [r.w_qkv, r.w_out, r.w_up, r.w_down]
    targets = [r.s_qkv, r.s_out, r.s_up, r.down_all]
    pieces = [(0, a, n) for a, n in split_rows(shard, 0, (0, 0.5, 1))]
    pieces += [(1, 0, shard)]
    pieces += [(2, a, n) for a, n in split_rows(shard, 0, (0, 0.5, 1))]
    pieces += [(3, a, n) for a, n in split_rows(shard, 0, (0, 0.5, 0.75, 1))]
    along, across = {}, {}

    def spot(weight, step, first, count):
        start = pl.multiple_of((dp ^ (2 * step)) * shard + first, 16)
        return targets[weight].at[pl.ds(start, count)]

    def launch(index):
        if index >= len(pieces):
            return
        weight, first, count = pieces[index]
        part = sources[weight].at[pl.ds(first, count)]
        for step in range(1, rings):
            along[index, step] = wire.push(
                part, spot(weight, 0, first, count), dp ^ (2 * step), mp
            )
        across[index, 0] = wire.push(part, spot(weight, 0, first, count), dp ^ 1, mp)

    def tick(index):
        if index >= len(pieces):
            return
        weight, first, count = pieces[index]
        for step in range(1, rings):
            along[index, step].wait_recv()
            place = spot(weight, step, first, count)
            across[index, step] = wire.push(place, place, dp ^ 1, mp)

    def arrived(weight):
        for index, piece in enumerate(pieces):
            if piece[0] == weight:
                for step in range(rings):
                    across[index, step].wait_recv()

    for copy in small:
        copy.wait_recv()
    small += [
        wire.push(r.s_small.at[dp], r.s_small.at[dp], dp ^ step, mp) for step in range(1, dp_size)
    ]
    launch(0)
    launch(1)
    launch(2)
    own_weights = [
        wire.move(sources[weight], targets[weight].at[window(dp, shard)]) for weight in range(4)
    ]
    launch(3)

    token = lax.broadcasted_iota(jnp.int32, (group, 1), 0)
    first = jnp.int32(0)
    starts = jnp.zeros((group, 1), jnp.int32)
    widths = jnp.zeros((group, 1), jnp.int32)
    for seq in range(seqs):
        starts = jnp.where(token >= first, first, starts)
        widths = jnp.where(token >= first, jnp.left_shift(GRAIN, r.grains[0, seq]), widths)
        first = first + r.lengths[0, seq]
    r.s_starts[...] = starts
    r.s_widths[...] = widths

    @pl.loop(0, group // 128)
    def _(index):
        here = window(index, 128)
        tokens = index * 128 + lax.broadcasted_iota(jnp.int32, (128, 1), 0)
        position = (tokens - r.s_starts[here, :]).astype(full)
        angles = position * r.inverse[0:1, :]
        r.s_cos[here, :] = jnp.cos(angles)
        r.s_sin[here, :] = jnp.sin(angles) * r.inverse[1:2, :]

    wire.store(r.s_cos, r.cosine)
    wire.store(r.s_sin, r.sine)

    for copy in small[mp_size - 1 :]:
        copy.wait_recv()
    devices = dp_size * mp_size * 8
    for start in range(0, width, 512):
        here = pl.ds(start, 512)
        packed = r.s_small[...].reshape(devices, 128).astype(low)
        spread = dot(packed, r.spread[:, here])
        row = lax.broadcasted_iota(jnp.int32, (devices, 1), 0)
        for line in range(3):
            chosen = row == r.targets[0:1, here] + line
            r.vectors[line : line + 1, here] = jnp.sum(
                jnp.where(chosen, spread, 0.0), axis=0, keepdims=True
            )
    for start in range(0, units, 512):
        here = pl.ds(start, 512)
        packed = r.s_small[...].reshape(devices, 128).astype(low)
        spread = dot(packed, r.spread_up[:, here])
        row = lax.broadcasted_iota(jnp.int32, (devices, 1), 0)
        chosen = row == r.targets[1:2, here] + mp * 8
        r.vectors[3:4, here] = jnp.sum(jnp.where(chosen, spread, 0.0), axis=0, keepdims=True)

    hidden_far.wait_recv()
    hidden_pass = wire.push(r.s_hidden.at[far], r.s_hidden.at[far], dp, mp ^ 1)
    own_grad = wire.move(r.grad, r.s_grads.at[mine])
    grad_far = wire.push(r.grad, r.s_grads.at[mine], dp, mp ^ 2)
    tick(0)
    launch(4)
    hidden_core.wait_recv()
    own_hidden.wait()
    hidden_pass.wait_recv()
    grad_core = wire.push(r.grad, r.s_grads.at[mine], dp, mp ^ 1)

    @pl.loop(0, group // 64)
    def _(index):
        here = window(index, 64)
        value = r.s_hidden[here, :].astype(full)
        ratio = lax.rsqrt(jnp.mean(value * value, axis=-1, keepdims=True) + norm_eps)
        r.s_normed[here, :] = (value * ratio * r.vectors[0:1, :]).astype(low)

    wire.store(r.s_normed, r.normed)
    tick(1)
    launch(5)
    tick(2)
    launch(6)
    for copy in own_weights:
        copy.wait()
    arrived(0)
    wire.store(r.s_qkv, r.qkv_all)

    @pl.loop(0, mp_size)
    def _(index):
        here = block(index)
        value = r.s_normed[here, :]
        cos, sin = r.s_cos[here, :], r.s_sin[here, :]
        for part, place in enumerate((r.s_q, r.s_k, r.s_v)):
            mixed = dot(value, r.s_qkv[:, pl.ds(part * lanes, lanes)])
            for head in range(heads):
                span = slice(head * HEAD, (head + 1) * HEAD)
                piece = mixed[:, span]
                if part < 2:
                    piece = turn(piece, cos, sin)
                place[here, span] = piece.astype(low)

    wire.store(r.s_q, r.queries)
    wire.store(r.s_k, r.keys)
    wire.store(r.s_v, r.values)
    for index in range(mp_size):
        here = pl.ds(index * rows, rows)
        seen = pl.ds(0, (index + 1) * rows)

        @pl.loop(0, heads)
        def _(head):
            span = window(head, HEAD)
            probs = softmax_rows(
                r.s_q[here, span], r.s_k[seen, span], r.s_starts[here, :], index * rows, scale
            )
            r.s_heads[here, span] = dot(probs.astype(low), r.s_v[seen, span]).astype(low)

    wire.store(r.s_heads, r.heads)
    arrived(1)
    wire.store(r.s_out, r.out_all)

    def branch(index, put):
        value = r.s_heads[index, :]

        @pl.loop(0, width // 512)
        def _(tile):
            span = window(tile, 512)
            put(span, dot(value, r.s_out[span, :], by_rows))

    def put_core(slot):
        def put(span, value):
            r.s_core_out[slot, :, span] = value.astype(low)

        return put

    def put_far(span, value):
        r.s_x_out[:, span] = (value + r.s_core_in[0, :, span].astype(full)).astype(low)

    def put_mine(span, value):
        r.s_part[:, span] = value + r.s_core_in[1, :, span].astype(full)

    branch(far_core, put_core(0))
    core_first = wire.push(r.s_core_out.at[0], r.s_core_in.at[0], dp, mp ^ 1)
    branch(core, put_core(1))
    core_second = wire.push(r.s_core_out.at[1], r.s_core_in.at[1], dp, mp ^ 1)
    core_first.wait_recv()
    branch(far, put_far)
    branch_far = wire.push(r.s_x_out, r.s_x_in, dp, mp ^ 2)
    tick(3)
    launch(7)
    core_second.wait_recv()
    branch(mine, put_mine)
    grad_far.wait_recv()
    grad_pass = wire.push(r.s_grads.at[far], r.s_grads.at[far], dp, mp ^ 1)
    branch_far.wait_recv()

    @pl.loop(0, rows // 64)
    def _(index):
        here = window(index, 64)
        there = pl.ds(pl.multiple_of(mp * rows + index * 64, 64), 64)
        value = r.s_hidden[there, :].astype(full) + (
            r.s_part[here, :] + r.s_x_in[here, :].astype(full)
        )
        r.s_middle[here, :] = value
        ratio = lax.rsqrt(jnp.mean(value * value, axis=-1, keepdims=True) + norm_eps)
        r.s_two[there, :] = (value * ratio * r.vectors[1:2, :]).astype(low)

    two_far = wire.push(r.s_two.at[mine], r.s_two.at[mine], dp, mp ^ 2)
    two_core = wire.push(r.s_two.at[mine], r.s_two.at[mine], dp, mp ^ 1)
    wire.store(r.s_middle, r.middle)
    tick(4)
    arrived(2)
    wire.store(r.s_up, r.up_all)

    def units_of(index):
        value = r.s_two[index, :]
        limit = r.s_widths[index, :] - mp * units

        @pl.loop(0, units // 512)
        def _(tile):
            span = window(tile, 512)
            pre_act = dot(value, r.s_up[:, span]) + r.vectors[3:4, span]
            unit = tile * 512 + lax.broadcasted_iota(jnp.int32, (1, 512), 1)
            on = unit < limit
            activated, slope = gelu_both(pre_act)
            r.s_act[index, span] = jnp.where(on, activated, 0.0).astype(low)
            r.s_slope[index, span] = jnp.where(on, slope, 0.0).astype(low)

    units_of(mine)
    two_far.wait_recv()
    two_pass = wire.push(r.s_two.at[far], r.s_two.at[far], dp, mp ^ 1)
    two_core.wait_recv()
    units_of(core)
    tick(5)
    units_of(far)
    two_pass.wait_recv()
    units_of(far_core)
    wire.store(r.s_two, r.normed_two)
    wire.store(r.s_act, r.activated)
    wire.store(r.s_slope, r.slope)
    grad_core.wait_recv()
    grad_pass.wait_recv()
    own_grad.wait()
    wire.store(r.s_grads, r.grads)
    tick(6)

    @pl.loop(0, width // 256)
    def _(tile):
        span = window(tile, 256)
        r.s_down[span, :] = dot(r.s_grads[:, span], r.s_act[...], by_tokens).astype(low)

    wire.store(r.s_down, r.grad_down)
    tick(7)
    arrived(3)
    wire.close()
    for copy in along.values():
        copy.wait_send()
    for copy in across.values():
        copy.wait_send()
    for copy in small:
        copy.wait_send()
    for copy in (
        hidden_far,
        hidden_core,
        hidden_pass,
        grad_far,
        grad_core,
        grad_pass,
        core_first,
        core_second,
        branch_far,
        two_far,
        two_core,
        two_pass,
    ):
        copy.wait_send()


def run_forward(inputs, seqs):
    hidden, w_up, w_out, w_qkv = inputs["hidden"], inputs["w_up"], inputs["w_out"], inputs["w_qkv"]
    dp_size, mp_size = lax.axis_size("dp"), lax.axis_size("mp")
    rows, width = hidden.shape
    group = rows * mp_size
    units, lanes = w_up.shape[1], w_out.shape[1]
    shapes = dict(
        qkv_all=((width, 3 * lanes), low),
        out_all=((width, lanes), low),
        up_all=((width, units), low),
        down_all=((width, units), low),
        normed=((group, width), low),
        queries=((group, lanes), low),
        keys=((group, lanes), low),
        values=((group, lanes), low),
        heads=((group, lanes), low),
        middle=((rows, width), full),
        normed_two=((group, width), low),
        activated=((group, units), low),
        slope=((group, units), low),
        grads=((group, width), low),
        grad_down=((width, units), low),
        cosine=((group, HEAD), full),
        sine=((group, HEAD), full),
        vectors=((8, width), full),
    )
    rings = dp_size // 2
    remote = mp_size - 1 + dp_size - 1 + 8 * (2 * rings - 1) + 16
    scratch = [
        pltpu.VMEM(shape, kind)
        for shape, kind in (
            ((group, width), low),
            ((group, width), low),
            ((width, 3 * lanes), low),
            ((width, lanes), low),
            ((width, units), low),
            ((group, lanes), low),
            ((group, lanes), low),
            ((group, lanes), low),
            ((group, lanes), low),
            ((group, HEAD), full),
            ((group, HEAD), full),
            ((dp_size, mp_size, 8, 128), full),
            ((group, 1), jnp.int32),
            ((group, 1), jnp.int32),
            ((2, rows, width), low),
            ((2, rows, width), low),
            ((rows, width), low),
            ((rows, width), low),
            ((rows, width), full),
            ((rows, width), full),
            ((group, width), low),
            ((group, units), low),
            ((group, units), low),
            ((group, width), low),
            ((width, units), low),
        )
    ] + [
        pltpu.SemaphoreType.DMA((remote,)),
        pltpu.SemaphoreType.DMA((remote,)),
        pltpu.SemaphoreType.DMA((32,)),
    ]
    anywhere = pl.BlockSpec(memory_space=pl.ANY)
    vector = pl.BlockSpec(memory_space=pltpu.VMEM)
    scalar = pl.BlockSpec(memory_space=pltpu.SMEM)
    placed = dict(
        pack=vector,
        spread=vector,
        spread_up=vector,
        targets=vector,
        inverse=vector,
        lengths=scalar,
        grains=scalar,
        vectors=vector,
    )
    outs = pl.pallas_call(
        functools.partial(forward_kernel, seqs),
        out_shape=[jax.ShapeDtypeStruct(*shapes[name]) for name in ForwardOutputs._fields],
        in_specs=[placed.get(name, anywhere) for name in ForwardInputs._fields],
        out_specs=[placed.get(name, anywhere) for name in ForwardOutputs._fields],
        scratch_shapes=scratch,
        compiler_params=pltpu.CompilerParams(
            collective_id=0, has_side_effects=True, vmem_limit_bytes=vmem_bytes
        ),
        name="forward",
    )(*[inputs[name] for name in ForwardInputs._fields])
    return dict(zip(ForwardOutputs._fields, outs))


def small_tables(width, units, dp_size, mp_size):
    piece = width // (dp_size * mp_size)
    half = units // dp_size // 2
    lane = np.arange(128)[:, None]
    column = np.arange(width)[None, :]
    unit = np.arange(units)[None, :]
    spread = (column % piece == lane).astype(np.float32)
    spread_up = (unit % half == lane).astype(np.float32)
    targets = np.zeros((8, max(width, units)), np.int32)
    targets[0, :width] = column[0] // piece * 8
    targets[1, :units] = unit[0] // (2 * half) * (8 * mp_size) + 3 + unit[0] % (2 * half) // half
    return jnp.asarray(spread, low), jnp.asarray(spread_up, low), jnp.asarray(targets)


def rope_rows():
    index = np.arange(HEAD // 2, dtype=np.float32)
    inverse = np.float32(rope_base) ** (np.float32(-2.0) * index / np.float32(HEAD))
    table = np.zeros((8, HEAD), np.float32)
    table[0] = np.concatenate([inverse, inverse])
    table[1] = np.concatenate([-np.ones(HEAD // 2), np.ones(HEAD // 2)])
    return jnp.asarray(table)


def small_pack(gain_attn, gain_ffn, bias_down, bias_up):
    half = bias_up.shape[0] // 2
    lines = [gain_attn, gain_ffn, bias_down, bias_up[:half], bias_up[half:]]
    lines = [jnp.pad(line.astype(full), (0, 128 - line.shape[0])) for line in lines]
    return jnp.stack(lines + [jnp.zeros((128,), full)] * 3)


class BackwardInputs(typing.NamedTuple):
    hidden: object
    lengths: object
    vectors: object
    cosine: object
    sine: object
    qkv_all: object
    out_all: object
    up_all: object
    down_all: object
    normed: object
    queries: object
    keys: object
    values: object
    heads: object
    middle: object
    normed_two: object
    activated: object
    slope: object
    grads: object
    grad_down: object


class BackwardOutputs(typing.NamedTuple):
    output: object
    grad_in: object
    sum_qkv: object
    sum_out: object
    sum_up: object
    sum_down: object
    totals: object
    z_qkv: object
    z_out: object
    z_up: object
    z_down: object


class BackwardScratch(typing.NamedTuple):
    s_weights: object
    s_up: object
    s_slope: object
    s_grads: object
    s_two: object
    s_act: object
    s_pre: object
    s_own: object
    y_qkv: object
    y_out: object
    y_up: object
    y_down: object
    s_gqkv: object
    s_gout: object
    s_core_in: object
    s_x_in: object
    s_core_out: object
    s_x_out: object
    s_part: object
    s_middle: object
    s_back: object
    s_gheads: object
    s_gk: object
    s_gv: object
    s_cos: object
    s_sin: object
    s_hidden: object
    s_output: object
    s_sums: object
    s_vec: object
    s_vec_mp: object
    s_vec_y: object
    s_vec_z: object
    sent: object
    got: object
    local: object


def backward_kernel(seqs, *refs):
    r = types.SimpleNamespace(
        **dict(zip(BackwardInputs._fields + BackwardOutputs._fields + BackwardScratch._fields, refs, strict=True))
    )
    dp, mp = lax.axis_index("dp"), lax.axis_index("mp")
    dp_size, mp_size = lax.axis_size("dp"), lax.axis_size("mp")
    rings = dp_size // 2
    rows, width = r.hidden.shape
    group = rows * mp_size
    shard = width // dp_size
    units = r.slope.shape[1]
    lanes = r.heads.shape[1]
    heads = lanes // HEAD
    scale = HEAD ** (-0.5)
    wire = Wire(r.sent, r.got, r.local)
    sends = []

    def block(index):
        return window(index, rows)

    def slot(index):
        return window(index, shard)

    def push(source, target, to_dp, to_mp):
        copy = wire.push(source, target, to_dp, to_mp)
        sends.append(copy)
        return copy

    def sent(*copies):
        for copy in copies:
            copy.wait_send()
            sends[:] = [other for other in sends if other is not copy]

    mine, core, far, far_core = block(mp), block(mp ^ 1), block(mp ^ 2), block(mp ^ 3)

    barrier = pltpu.get_barrier_semaphore()
    for step in range(1, mp_size):
        pl.semaphore_signal(barrier, inc=1, device_id=(dp, mp ^ step), device_id_type=MESH)
    pl.semaphore_signal(barrier, inc=1, device_id=(dp ^ 1, mp), device_id_type=MESH)
    for step in range(1, rings):
        pl.semaphore_signal(barrier, inc=1, device_id=(dp ^ (2 * step), mp), device_id_type=MESH)
    pl.semaphore_wait(barrier, mp_size + rings - 1)

    order = list(range(rings - 1, -1, -1))
    locals_of = dict(down=r.grad_down, up=r.s_up, out=r.s_gout, qkv=r.s_gqkv)
    y_of = dict(down=r.y_down, up=r.y_up, out=r.y_out, qkv=r.y_qkv)
    z_of = dict(down=r.z_down, up=r.z_up, out=r.z_out, qkv=r.z_qkv)
    sum_of = dict(down=r.sum_down, up=r.sum_up, out=r.sum_out, qkv=r.sum_qkv)
    across, along, own = {}, {}, {}

    def y_launch(name):
        for step in order:
            across[name, step] = push(
                locals_of[name].at[slot(dp ^ 1 ^ (2 * step))], y_of[name].at[step], dp ^ 1, mp
            )

    def own_load(place):
        if place < rings:
            step = order[place]
            own[step] = wire.move(
                r.grad_down.at[slot(dp ^ (2 * step))], r.s_own.at[place % 2]
            )

    def y_tick(name, place):
        if place >= rings:
            return
        step = order[place]
        across[name, step].wait_recv()
        if name == "down":
            own[step].wait()
        part = 16 if shard % 64 else 64

        @pl.loop(0, shard // part)
        def _(index):
            here = window(index, part)
            if name == "down":
                value = r.s_own[place % 2, here, :]
            else:
                start = pl.multiple_of((dp ^ (2 * step)) * shard + index * part, part)
                value = locals_of[name][pl.ds(start, part), :]
            total = y_of[name][step, here, :].astype(full) + value.astype(full)
            y_of[name][step, here, :] = total.astype(low)

        if step:
            along[name, step] = push(
                y_of[name].at[step], z_of[name].at[step - 1], dp ^ (2 * step), mp
            )
        if name == "down":
            own_load(place + 2)

    def z_finish(name, stage):
        columns = z_of[name].shape[2]
        span = pl.ds(0, columns)
        loads = []
        for step in order[:-1]:
            along[name, step].wait_recv()
            loads.append(
                wire.move(
                    z_of[name].at[step - 1], r.s_pre.at[pl.ds((step - 1) * shard, shard), span]
                )
            )
        for copy in loads:
            copy.wait()

        @pl.loop(0, shard // 16)
        def _(index):
            here = window(index, 16)
            total = y_of[name][0, here, :].astype(full)
            for step in range(1, rings):
                start = pl.multiple_of((step - 1) * shard + index * 16, 16)
                total = total + r.s_pre[pl.ds(start, 16), span].astype(full)
            stage[here, span] = total

        return wire.move(stage.at[pl.ds(0, shard), span], sum_of[name])

    def reduce_start(left, right, columns, slot_in):
        def product(index, put):
            value = left[index, columns]

            @pl.loop(0, width // 512)
            def _(tile):
                span = window(tile, 512)
                put(span, dot(value, right[span, columns], by_rows))

        def put_core(place):
            def put(span, value):
                r.s_core_out[place, :, span] = value.astype(low)

            return put

        def put_far(span, value):
            value = value + r.s_core_in[slot_in, 0, :, span].astype(full)
            r.s_x_out[slot_in, :, span] = value.astype(low)

        def put_mine(span, value):
            r.s_part[:, span] = value + r.s_core_in[slot_in, 1, :, span].astype(full)

        def first():
            product(far_core, put_core(0))
            one = push(r.s_core_out.at[0], r.s_core_in.at[slot_in, 0], dp, mp ^ 1)
            product(core, put_core(1))
            two = push(r.s_core_out.at[1], r.s_core_in.at[slot_in, 1], dp, mp ^ 1)
            return one, two

        def second(one):
            one.wait_recv()
            product(far, put_far)

        def third(two):
            two.wait_recv()
            product(mine, put_mine)

        return first, second, third

    load_grads = wire.move(r.grads, r.s_grads)
    load_down = wire.move(r.down_all, r.s_weights)
    load_slope = wire.move(r.slope, r.s_slope)
    y_launch("down")
    load_up = wire.move(r.up_all, r.s_up)
    load_two = wire.move(r.normed_two, r.s_two)
    load_act = wire.move(r.activated, r.s_act)
    load_middle = wire.move(r.middle, r.s_middle)
    own_load(0)
    own_load(1)
    load_rest = [
        wire.move(r.cosine, r.s_cos),
        wire.move(r.sine, r.s_sin),
        wire.move(r.hidden, r.s_hidden),
    ]
    r.s_sums[...] = jnp.zeros_like(r.s_sums)
    load_grads.wait()
    load_down.wait()
    load_slope.wait()

    @pl.loop(0, units // 512)
    def _(tile):
        span = window(tile, 512)
        value = dot(r.s_grads[...], r.s_weights[:, span]) * r.s_slope[:, span].astype(full)
        value = value.astype(low)
        r.s_pre[:, span] = value
        r.s_sums[3:4, span] = jnp.sum(value.astype(full), axis=0, keepdims=True)

    load_up.wait()
    everything = pl.ds(0, units)
    first, second, third = reduce_start(r.s_pre, r.s_up, everything, 0)
    one, two = first()
    second(one)
    two_far = push(r.s_x_out.at[0], r.s_x_in.at[0], dp, mp ^ 2)
    third(two)
    y_tick("down", 0)
    load_two.wait()

    @pl.loop(0, width // 256)
    def _(tile):
        span = window(tile, 256)
        r.s_up[span, :] = dot(r.s_two[:, span], r.s_pre[...], by_tokens).astype(low)

    y_launch("up")
    load_heads = [
        wire.move(place, r.s_two.at[:, pl.ds(index * lanes, lanes)])
        for index, place in enumerate((r.queries, r.keys, r.values, r.heads))
    ]
    y_tick("down", 1)
    load_middle.wait()
    two_far.wait_recv()

    @pl.loop(0, rows // 64)
    def _(index):
        here = window(index, 64)
        there = pl.ds(pl.multiple_of(mp * rows + index * 64, 64), 64)
        normed_grad = r.s_part[here, :] + r.s_x_in[0, here, :].astype(full)
        middle = r.s_middle[here, :]
        grad = r.s_grads[there, :].astype(full)
        ratio = lax.rsqrt(jnp.mean(middle * middle, axis=-1, keepdims=True) + norm_eps)
        weighted = normed_grad * r.vectors[1:2, :]
        back = (
            grad
            + ratio * weighted
            - middle * (ratio**3 * jnp.mean(weighted * middle, axis=-1, keepdims=True))
        )
        r.s_back[here, :] = back
        r.s_slope[there, :] = back.astype(low)
        r.s_sums[1:2, :] += jnp.sum(normed_grad * (middle * ratio), axis=0, keepdims=True)
        r.s_sums[2:3, :] += jnp.sum(grad, axis=0, keepdims=True)

    branch_far = push(r.s_slope.at[mine], r.s_slope.at[mine], dp, mp ^ 2)
    branch_core = push(r.s_slope.at[mine], r.s_slope.at[mine], dp, mp ^ 1)
    load_normed = wire.move(r.normed, r.s_grads)

    load_act.wait()
    first, second, third = reduce_start(r.s_act, r.s_weights, everything, 1)
    sent(one, two)
    one, two = first()
    second(one)
    ffn_far = push(r.s_x_out.at[1], r.s_x_in.at[1], dp, mp ^ 2)
    third(two)
    load_weights = [
        wire.move(r.qkv_all, r.s_weights.at[:, pl.ds(0, 3 * lanes)]),
        wire.move(r.out_all, r.s_weights.at[:, pl.ds(3 * lanes, lanes)]),
    ]
    y_tick("down", 2)
    branch_far.wait_recv()
    branch_pass = push(r.s_slope.at[far], r.s_slope.at[far], dp, mp ^ 1)
    branch_core.wait_recv()
    for copy in load_heads + load_weights:
        copy.wait()
    branch_pass.wait_recv()
    to_heads = pl.ds(3 * lanes, lanes)

    @pl.loop(0, width // 512)
    def _(tile):
        span = window(tile, 512)
        r.s_gout[span, :] = dot(r.s_slope[:, span], r.s_two[:, to_heads], by_tokens).astype(low)

    y_launch("out")

    @pl.loop(0, group // 512)
    def _(tile):
        here = window(tile, 512)
        r.s_gheads[here, :] = dot(r.s_slope[here, :], r.s_weights[:, to_heads]).astype(low)

    y_tick("down", 3)

    for copy in load_rest:
        copy.wait()
    token = lax.broadcasted_iota(jnp.int32, (group, 1), 0)
    first_token = jnp.int32(0)
    starts = jnp.zeros((group, 1), jnp.int32)
    for seq in range(seqs):
        starts = jnp.where(token >= first_token, first_token, starts)
        first_token = first_token + r.lengths[0, seq]

    @pl.loop(0, heads)
    def _(head):
        span = window(head, HEAD)
        k_span = pl.ds(pl.multiple_of(lanes + head * HEAD, HEAD), HEAD)
        v_span = pl.ds(pl.multiple_of(2 * lanes + head * HEAD, HEAD), HEAD)
        for index in reversed(range(mp_size)):
            here = pl.ds(index * rows, rows)
            seen = pl.ds(0, (index + 1) * rows)
            query, grad = r.s_two[here, span], r.s_gheads[here, span]
            begin = starts[index * rows : (index + 1) * rows]
            probs = softmax_rows(query, r.s_two[seen, k_span], begin, index * rows, scale)
            grad_probs = dot(grad, r.s_two[seen, v_span], by_rows)
            inner = jnp.sum(probs * grad_probs, axis=-1, keepdims=True)
            grad_scores = (probs * (grad_probs - inner)).astype(low)
            query_grad = dot(grad_scores, r.s_two[seen, k_span]) * scale
            r.s_act[here, span] = turn(
                query_grad, r.s_cos[here, :], -r.s_sin[here, :]
            ).astype(low)
            key_part = dot(grad_scores, query, by_tokens)
            value_part = dot(probs.astype(low), grad, by_tokens)
            if index == mp_size - 1:
                r.s_gk[...] = key_part
                r.s_gv[...] = value_part
            else:
                r.s_gk[seen, :] += key_part
                r.s_gv[seen, :] += value_part
        for index in range(mp_size):
            here = pl.ds(index * rows, rows)
            r.s_act[here, k_span] = turn(
                r.s_gk[here, :] * scale, r.s_cos[here, :], -r.s_sin[here, :]
            ).astype(low)
            r.s_act[here, v_span] = r.s_gv[here, :].astype(low)

    y_tick("up", 0)

    mixed = pl.ds(0, 3 * lanes)
    first, second, third = reduce_start(r.s_act, r.s_weights, mixed, 0)
    sent(one, two, two_far)
    ffn_far.wait_recv()

    @pl.loop(0, rows // 64)
    def _(index):
        here = window(index, 64)
        value = r.s_part[here, :] + r.s_x_in[1, here, :].astype(full)
        r.s_output[here, :] = (r.s_middle[here, :] + value + r.vectors[2:3, :]).astype(low)

    wire.store(r.s_output, r.output)
    one, two = first()
    y_tick("up", 1)
    second(one)
    one_far = push(r.s_x_out.at[0], r.s_x_in.at[0], dp, mp ^ 2)
    third(two)
    load_normed.wait()

    @pl.loop(0, width // 256)
    def _(tile):
        span = window(tile, 256)
        r.s_gqkv[span, :] = dot(r.s_grads[:, span], r.s_act[:, mixed], by_tokens).astype(low)

    y_launch("qkv")
    y_tick("up", 2)
    one_far.wait_recv()

    @pl.loop(0, rows // 64)
    def _(index):
        here = window(index, 64)
        normed_grad = r.s_part[here, :] + r.s_x_in[0, here, :].astype(full)
        hidden = r.s_hidden[here, :].astype(full)
        ratio = lax.rsqrt(jnp.mean(hidden * hidden, axis=-1, keepdims=True) + norm_eps)
        weighted = normed_grad * r.vectors[0:1, :]
        r.s_back[here, :] = (
            r.s_back[here, :]
            + ratio * weighted
            - hidden * (ratio**3 * jnp.mean(weighted * hidden, axis=-1, keepdims=True))
        )
        r.s_sums[0:1, :] += jnp.sum(normed_grad * (hidden * ratio), axis=0, keepdims=True)

    wire.store(r.s_back, r.grad_in)

    lines = width // 128
    for line in range(4):
        for index in range((units if line == 3 else width) // 128):
            r.s_vec[line * lines + index : line * lines + index + 1, :] = r.s_sums[
                line : line + 1, index * 128 : (index + 1) * 128
            ]
    shared = 3 * lines
    vec_mp = [
        push(r.s_vec.at[pl.ds(0, shared)], r.s_vec_mp.at[step - 1], dp, mp ^ step)
        for step in range(1, mp_size)
    ]
    y_tick("up", 3)
    for copy in vec_mp:
        copy.wait_recv()
    sent(*vec_mp)
    for step in range(1, mp_size):
        r.s_vec[0:shared, :] += r.s_vec_mp[step - 1]
    vec_y = push(r.s_vec, r.s_vec_y, dp ^ 1, mp)
    for place in range(4):
        y_tick("out", place)
    vec_y.wait_recv()
    sent(vec_y)
    r.s_vec[...] += r.s_vec_y[...]
    vec_z = [
        push(r.s_vec, r.s_vec_z.at[step - 1], dp ^ (2 * step), mp) for step in range(1, rings)
    ]
    for place in range(4, rings):
        for name in ("down", "up", "out"):
            y_tick(name, place)
    done_down = z_finish("down", r.s_part)
    y_tick("qkv", 0)
    y_tick("qkv", 1)
    done_up = z_finish("up", r.s_middle)
    y_tick("qkv", 2)
    for place in range(3, rings):
        y_tick("qkv", place)
    for copy in vec_z:
        copy.wait_recv()
    total = r.s_vec[...]
    for step in range(1, rings):
        total = total + r.s_vec_z[step - 1]
    r.totals[...] = total
    done_down.wait()
    done_out = z_finish("out", r.s_part)
    done_up.wait()
    done_qkv = z_finish("qkv", r.s_middle)
    done_out.wait()
    done_qkv.wait()
    wire.close()
    for copy in sends:
        copy.wait_send()


def run_backward(inputs, seqs):
    dp_size, mp_size = lax.axis_size("dp"), lax.axis_size("mp")
    rings = dp_size // 2
    rows, width = inputs["hidden"].shape
    group, units = inputs["slope"].shape
    lanes = inputs["heads"].shape[1]
    shard = width // dp_size
    vec_rows = (3 * width + units) // 128
    shapes = dict(
        output=((rows, width), low),
        grad_in=((rows, width), full),
        sum_qkv=((shard, 3 * lanes), full),
        sum_out=((shard, lanes), full),
        sum_up=((shard, units), full),
        sum_down=((shard, units), full),
        totals=((vec_rows, 128), full),
        z_qkv=((rings - 1, shard, 3 * lanes), low),
        z_out=((rings - 1, shard, lanes), low),
        z_up=((rings - 1, shard, units), low),
        z_down=((rings - 1, shard, units), low),
    )
    scratch = [
        pltpu.VMEM(shape, kind)
        for shape, kind in (
            ((width, max(units, 4 * lanes)), low),
            ((width, units), low),
            ((group, max(units, width)), low),
            ((group, width), low),
            ((group, max(width, 4 * lanes)), low),
            ((group, max(units, 3 * lanes)), low),
            ((group, units), low),
            ((2, shard, units), low),
            ((rings, shard, 3 * lanes), low),
            ((rings, shard, lanes), low),
            ((rings, shard, units), low),
            ((rings, shard, units), low),
            ((width, 3 * lanes), low),
            ((width, lanes), low),
            ((2, 2, rows, width), low),
            ((2, rows, width), low),
            ((2, rows, width), low),
            ((2, rows, width), low),
            ((rows, width), full),
            ((rows, width), full),
            ((rows, width), full),
            ((group, lanes), low),
            ((group, HEAD), full),
            ((group, HEAD), full),
            ((group, HEAD), full),
            ((group, HEAD), full),
            ((rows, width), low),
            ((rows, width), low),
            ((8, max(width, units)), full),
            ((vec_rows, 128), full),
            ((mp_size - 1, 3 * width // 128, 128), full),
            ((vec_rows, 128), full),
            ((rings - 1, vec_rows, 128), full),
        )
    ]
    remote = 4 * (2 * rings - 1) + 9 + 3 + mp_size + rings
    scratch += [
        pltpu.SemaphoreType.DMA((remote,)),
        pltpu.SemaphoreType.DMA((remote,)),
        pltpu.SemaphoreType.DMA((32 + 5 * rings,)),
    ]
    anywhere = pl.BlockSpec(memory_space=pl.ANY)
    vector = pl.BlockSpec(memory_space=pltpu.VMEM)
    placed = dict(
        lengths=pl.BlockSpec(memory_space=pltpu.SMEM), vectors=vector, totals=vector
    )
    outs = pl.pallas_call(
        functools.partial(backward_kernel, seqs),
        out_shape=[jax.ShapeDtypeStruct(*shapes[name]) for name in BackwardOutputs._fields],
        in_specs=[placed.get(name, anywhere) for name in BackwardInputs._fields],
        out_specs=[placed.get(name, anywhere) for name in BackwardOutputs._fields],
        scratch_shapes=scratch,
        compiler_params=pltpu.CompilerParams(
            collective_id=1, has_side_effects=True, vmem_limit_bytes=vmem_bytes
        ),
        name="backward",
    )(*[inputs[name] for name in BackwardInputs._fields])
    return dict(zip(BackwardOutputs._fields, outs))


def shards(
    hidden_in,
    out_grad,
    seq_lengths,
    seq_grains,
    gain_attn,
    w_qkv,
    w_out,
    gain_ffn,
    w_up,
    bias_up,
    w_down,
    bias_down,
):
    dp, mp = lax.axis_index("dp"), lax.axis_index("mp")
    dp_size, mp_size = lax.axis_size("dp"), lax.axis_size("mp")
    width = hidden_in.shape[1]
    units = w_up.shape[1]
    seqs = seq_lengths.shape[1]
    spread, spread_up, targets = small_tables(width, units, dp_size, mp_size)
    done = run_forward(
        dict(
            hidden=hidden_in,
            grad=out_grad,
            w_qkv=w_qkv.reshape(w_qkv.shape[0], -1),
            w_out=w_out.T,
            w_up=w_up,
            w_down=w_down.T,
            pack=small_pack(gain_attn, gain_ffn, bias_down, bias_up),
            spread=spread,
            spread_up=spread_up,
            targets=targets,
            inverse=rope_rows(),
            lengths=seq_lengths,
            grains=seq_grains,
        ),
        seqs,
    )
    back = run_backward(dict(done, hidden=hidden_in, lengths=seq_lengths), seqs)
    totals = back["totals"].reshape(-1)
    piece, pieces = gain_attn.shape[0], bias_up.shape[0]

    def own(line):
        return lax.dynamic_slice_in_dim(
            totals[line * width : (line + 1) * width], (dp * mp_size + mp) * piece, piece
        )

    return (
        back["output"],
        back["grad_in"],
        own(0),
        back["sum_qkv"].reshape(w_qkv.shape),
        back["sum_out"].T,
        own(1),
        back["sum_up"],
        lax.dynamic_slice_in_dim(totals[3 * width :], dp * pieces, pieces),
        back["sum_down"].T,
        own(2),
    )


def solution(mesh):
    return jax.shard_map(
        shards,
        mesh=mesh,
        in_specs=(
            P(("dp", "mp"), None),
            P(("dp", "mp"), None),
            P("dp", None),
            P("dp", None),
            P(("dp", "mp")),
            P("dp", None, "mp"),
            P("mp", "dp"),
            P(("dp", "mp")),
            P("dp", "mp"),
            P(("mp", "dp")),
            P("mp", "dp"),
            P(("dp", "mp")),
        ),
        out_specs=(
            P(("dp", "mp"), None),
            P(("dp", "mp"), None),
            P(("dp", "mp")),
            P("dp", None, "mp"),
            P("mp", "dp"),
            P(("dp", "mp")),
            P("dp", "mp"),
            P(("mp", "dp")),
            P("mp", "dp"),
            P(("dp", "mp")),
        ),
        check_vma=False,
    )
```

```python
import functools
import types
import typing

import jax
import jax.numpy as jnp
import numpy as np
from jax import lax
from jax.experimental import pallas as pl
from jax.experimental.pallas import tpu as pltpu
from jax.sharding import PartitionSpec as P

HEAD = 128
GRAIN = 768
MESH = pl.DeviceIdType.MESH
low = jnp.bfloat16
full = jnp.float32

norm_eps = 1e-06
rope_base = 10000.0
masked_score = -1e30
vmem_bytes = 62 * 2**20
root_half_pi = (2.0 / np.pi) ** 0.5
cubic = 0.044715

plain = (((1,), (0,)), ((), ()))
by_rows = (((1,), (1,)), ((), ()))
by_tokens = (((0,), (0,)), ((), ()))


def dot(first, second, dims=plain):
    return lax.dot_general(first, second, dims, preferred_element_type=jnp.float32)


def window(index, size):
    return pl.ds(pl.multiple_of(index * size, size), size)


class Wire:
    def __init__(self, sent, got, local):
        self.sent, self.got, self.local = sent, got, local
        self.used, self.used_local = 0, 0
        self.open = []

    def push(self, source, target, dp, mp):
        copy = pltpu.make_async_remote_copy(
            source,
            target,
            self.sent.at[self.used],
            self.got.at[self.used],
            device_id=(dp, mp),
            device_id_type=MESH,
        )
        self.used += 1
        copy.start()
        return copy

    def move(self, source, target):
        copy = pltpu.make_async_copy(source, target, self.local.at[self.used_local])
        self.used_local += 1
        copy.start()
        return copy

    def store(self, source, target):
        self.open.append(self.move(source, target))

    def close(self):
        for copy in self.open:
            copy.wait()
        self.open = []


def greet(dp, mp, dp_size, mp_size):
    barrier = pltpu.get_barrier_semaphore()
    for step in range(1, mp_size):
        pl.semaphore_signal(barrier, inc=1, device_id=(dp, mp ^ step), device_id_type=MESH)
    for step in range(1, dp_size):
        pl.semaphore_signal(barrier, inc=1, device_id=(dp ^ step, mp), device_id_type=MESH)
    pl.semaphore_wait(barrier, mp_size + dp_size - 2)


def cut(rows, *parts):
    edges = [16 * round(rows * part / 16) for part in parts]
    return [(a, b - a) for a, b in zip(edges[:-1], edges[1:]) if b > a]


def last_step(kind, k, dp_size):
    if k == 0:
        return 0
    if kind == "y":
        return (k & ~1) & -(k & ~1) if k > 1 else 1
    return k & -k


def onward(kind, k, dp_size):
    steps = []
    step = dp_size // 2
    while step:
        if step > 1:
            free = k < 2 or step < last_step(kind, k & ~1, dp_size)
        else:
            free = k == 0 or (kind == "z" and k > 1 and k % 2 == 0)
        if free:
            steps.append(step)
        step //= 2
    if kind == "z" and k % 2:
        return []
    if kind == "y" and k == 0:
        return [1] + steps[:-1]
    return steps


def turn(values, cosine, sine):
    return values * cosine + pltpu.roll(values, HEAD // 2, 1) * sine


def softmax_rows(query, keys, starts, first, scale):
    scores = dot(query, keys, by_rows) * scale
    key_index = lax.broadcasted_iota(jnp.int32, scores.shape, 1)
    row_index = first + lax.broadcasted_iota(jnp.int32, scores.shape, 0)
    allowed = (key_index >= starts) & (key_index <= row_index)
    scores = jnp.where(allowed, scores, masked_score)
    exponents = jnp.exp(scores - jnp.max(scores, axis=-1, keepdims=True))
    return exponents * (1.0 / jnp.sum(exponents, axis=-1, keepdims=True))


def gelu_both(value):
    square = value * value
    bend = jnp.tanh(value * (root_half_pi + (root_half_pi * cubic) * square))
    half = 0.5 + 0.5 * bend
    inner = root_half_pi + (3 * root_half_pi * cubic) * square
    return value * half, half + (0.5 * value) * (1.0 - bend * bend) * inner


class ForwardInputs(typing.NamedTuple):
    hidden: object
    grad: object
    w_qkv: object
    w_out: object
    w_up: object
    w_down: object
    gain_attn: object
    gain_ffn: object
    bias_down: object
    bias_up: object
    spread: object
    spread_up: object
    targets: object
    inverse: object
    lengths: object
    grains: object


class ForwardOutputs(typing.NamedTuple):
    qkv_all: object
    out_all: object
    up_all: object
    down_all: object
    normed: object
    queries: object
    keys: object
    values: object
    heads: object
    middle: object
    normed_two: object
    activated: object
    slope: object
    grads: object
    grad_down: object
    cosine: object
    sine: object
    vectors: object


class ForwardScratch(typing.NamedTuple):
    s_hidden: object
    s_normed: object
    s_qkv: object
    s_out: object
    s_up: object
    s_q: object
    s_k: object
    s_v: object
    s_heads: object
    s_cos: object
    s_sin: object
    s_small: object
    s_starts: object
    s_widths: object
    s_core_out: object
    s_core_in: object
    s_x_out: object
    s_x_in: object
    s_part: object
    s_middle: object
    s_two: object
    s_act: object
    s_slope: object
    s_grads: object
    s_down: object
    sent: object
    got: object
    local: object


def forward_kernel(seqs, *refs):
    r = types.SimpleNamespace(
        **dict(zip(ForwardInputs._fields + ForwardOutputs._fields + ForwardScratch._fields, refs, strict=True))
    )
    dp, mp = lax.axis_index("dp"), lax.axis_index("mp")
    dp_size, mp_size = lax.axis_size("dp"), lax.axis_size("mp")
    rings = dp_size // 2
    rows, width = r.hidden.shape
    group = rows * mp_size
    shard = r.w_up.shape[0]
    units = r.w_up.shape[1]
    lanes = r.w_out.shape[1]
    heads = lanes // HEAD
    scale = HEAD ** (-0.5)
    wire = Wire(r.sent, r.got, r.local)

    def block(index):
        return window(index, rows)

    mine, core, far, far_core = block(mp), block(mp ^ 1), block(mp ^ 2), block(mp ^ 3)
    greet(dp, mp, dp_size, mp_size)

    half = r.bias_up.shape[0] // 2
    pair = r.bias_up[...].astype(full).reshape(1, 2 * half)
    r.s_small[dp, mp] = jnp.zeros((8, 128), full)
    for line, value in enumerate((r.gain_attn, r.gain_ffn, r.bias_down)):
        count = value.shape[0]
        r.s_small[dp, mp, line : line + 1, 0:count] = value[...].astype(full).reshape(1, count)
    r.s_small[dp, mp, 3:4, 0:half] = pair[:, :half]
    r.s_small[dp, mp, 4:5, 0:half] = pair[:, half:]
    small = [
        wire.push(r.s_small.at[dp, mp], r.s_small.at[dp, mp], dp, mp ^ step)
        for step in range(1, mp_size)
    ]
    hidden_far = wire.push(r.hidden, r.s_hidden.at[mine], dp, mp ^ 2)
    hidden_core = wire.push(r.hidden, r.s_hidden.at[mine], dp, mp ^ 1)
    own_hidden = wire.move(r.hidden, r.s_hidden.at[mine])

    sources = [r.w_qkv, r.w_out, r.w_up, r.w_down]
    targets = [r.s_qkv, r.s_out, r.s_up, r.down_all]
    pieces = [(0, "z") + span for span in cut(shard, 0, 0.5, 1)]
    pieces += [(1, "z", 0, shard)]
    pieces += [(2, "z") + span for span in cut(shard, 0, 0.5, 1)]
    pieces += [(3, kind) + span for kind, span in zip("zy", cut(shard, 0, 0.5, 1), strict=True)]
    route, waited = {}, set()

    def rows_at(ref, span):
        return ref.at[:, span, :] if len(ref.shape) == 3 else ref.at[span, :]

    def spot(weight, k, first, count):
        start = pl.multiple_of((dp ^ k) * shard + first, 16)
        return rows_at(targets[weight], pl.ds(start, count))

    def pass_on(index, k, steps):
        weight, kind, first, count = pieces[index]
        place = spot(weight, k, first, count)
        part = place if k else rows_at(sources[weight], pl.ds(first, count))
        for step in steps:
            route[index, k ^ step] = wire.push(part, place, dp ^ step, mp)

    def launch(index, steps=None):
        pass_on(index, 0, onward(pieces[index][1], 0, dp_size) if steps is None else steps)

    def tick(index, ks, steps=None):
        for k in ks:
            route[index, k].wait_recv()
            waited.add((index, k))
            echo(index, [k], steps)

    def echo(index, ks, steps=None):
        for k in ks:
            after = onward(pieces[index][1], k, dp_size)
            pass_on(index, k, [step for step in after if steps is None or step in steps])

    def arrived(weight):
        for index, piece in enumerate(pieces):
            if piece[0] == weight:
                for k in arrival[piece[1]]:
                    if (index, k) not in waited:
                        route[index, k].wait_recv()

    over_y = [1]
    over_z = [step for step in onward("z", 0, dp_size) if step > 1]
    arrival = {}
    for kind in "zy":
        found = [0]
        for k in found:
            found += [k ^ step for step in onward(kind, k, dp_size)]
        arrival[kind] = found[1:]
    early = [k for k in arrival["z"] if k > 1 and k & (k - 1) == 0]
    late = [k for k in arrival["z"] if k % 2 == 0 and k not in early]
    even = [k for k in arrival["y"] if k % 2 == 0 and onward("y", k, dp_size)]
    odd = [k for k in arrival["y"] if k > 1 and k % 2 and onward("y", k, dp_size)]

    launch(0)
    for copy in small:
        copy.wait_recv()
    small += [
        wire.push(r.s_small.at[dp], r.s_small.at[dp], dp ^ step, mp) for step in range(1, dp_size)
    ]
    launch(1)
    own_weights = [
        wire.move(sources[weight], rows_at(targets[weight], window(dp, shard)))
        for weight in range(4)
    ]

    token = lax.broadcasted_iota(jnp.int32, (group, 1), 0)
    first = jnp.int32(0)
    starts = jnp.zeros((group, 1), jnp.int32)
    widths = jnp.zeros((group, 1), jnp.int32)
    for seq in range(seqs):
        starts = jnp.where(token >= first, first, starts)
        widths = jnp.where(token >= first, jnp.left_shift(GRAIN, r.grains[0, seq]), widths)
        first = first + r.lengths[0, seq]
    r.s_starts[...] = starts
    r.s_widths[...] = widths

    @pl.loop(0, group // 128)
    def _(index):
        here = window(index, 128)
        tokens = index * 128 + lax.broadcasted_iota(jnp.int32, (128, 1), 0)
        position = (tokens - r.s_starts[here, :]).astype(full)
        angles = position * r.inverse[0:1, :]
        r.s_cos[here, :] = jnp.cos(angles)
        r.s_sin[here, :] = jnp.sin(angles) * r.inverse[1:2, :]

    wire.store(r.s_cos, r.cosine)
    wire.store(r.s_sin, r.sine)
    tick(0, early)
    launch(2, over_y)

    for copy in small[mp_size - 1 :]:
        copy.wait_recv()
    devices = dp_size * mp_size * 8
    for start in range(0, width, 512):
        here = pl.ds(start, 512)
        packed = r.s_small[...].reshape(devices, 128).astype(low)
        spread = dot(packed, r.spread[:, here])
        row = lax.broadcasted_iota(jnp.int32, (devices, 1), 0)
        for line in range(3):
            chosen = row == r.targets[0:1, here] + line
            r.vectors[line : line + 1, here] = jnp.sum(
                jnp.where(chosen, spread, 0.0), axis=0, keepdims=True
            )
    for start in range(0, units, 512):
        here = pl.ds(start, 512)
        packed = r.s_small[...].reshape(devices, 128).astype(low)
        spread = dot(packed, r.spread_up[:, here])
        row = lax.broadcasted_iota(jnp.int32, (devices, 1), 0)
        chosen = row == r.targets[1:2, here] + mp * 8
        r.vectors[3:4, here] = jnp.sum(jnp.where(chosen, spread, 0.0), axis=0, keepdims=True)


    tick(1, early)
    launch(2, over_z)

    hidden_far.wait_recv()
    hidden_pass = wire.push(r.s_hidden.at[far], r.s_hidden.at[far], dp, mp ^ 1)
    own_grad = wire.move(r.grad, r.s_grads.at[mine])
    grad_far = wire.push(r.grad, r.s_grads.at[mine], dp, mp ^ 2)
    tick(0, late)
    launch(3, over_z)
    hidden_core.wait_recv()
    own_hidden.wait()
    hidden_pass.wait_recv()
    grad_core = wire.push(r.grad, r.s_grads.at[mine], dp, mp ^ 1)

    @pl.loop(0, group // 64)
    def _(index):
        here = window(index, 64)
        value = r.s_hidden[here, :].astype(full)
        ratio = lax.rsqrt(jnp.mean(value * value, axis=-1, keepdims=True) + norm_eps)
        r.s_normed[here, :] = (value * ratio * r.vectors[0:1, :]).astype(low)

    wire.store(r.s_normed, r.normed)
    tick(1, late)
    tick(2, early)
    for copy in own_weights:
        copy.wait()
    arrived(0)
    launch(4, over_z)
    wire.store(r.s_qkv, r.qkv_all)

    @pl.loop(0, mp_size)
    def _(index):
        here = block(index)
        value = r.s_normed[here, :]
        cos, sin = r.s_cos[here, :], r.s_sin[here, :]
        for part, place in enumerate((r.s_q, r.s_k, r.s_v)):
            mixed = dot(value, r.s_qkv[part, :, :])
            for head in range(heads):
                span = slice(head * HEAD, (head + 1) * HEAD)
                piece = mixed[:, span]
                if part < 2:
                    piece = turn(piece, cos, sin)
                place[here, span] = piece.astype(low)

    tick(2, late)
    launch(3, over_y)
    tick(3, early)
    wire.store(r.s_q, r.queries)
    wire.store(r.s_k, r.keys)
    wire.store(r.s_v, r.values)
    for index in range(mp_size):
        here = pl.ds(index * rows, rows)
        seen = pl.ds(0, (index + 1) * rows)

        @pl.loop(0, heads)
        def _(head):
            span = window(head, HEAD)
            probs = softmax_rows(
                r.s_q[here, span], r.s_k[seen, span], r.s_starts[here, :], index * rows, scale
            )
            r.s_heads[here, span] = dot(probs.astype(low), r.s_v[seen, span]).astype(low)

        if index == mp_size // 2:
            tick(3, late)
            launch(4, over_y)

    wire.store(r.s_heads, r.heads)
    arrived(1)
    wire.store(r.s_out, r.out_all)

    def branch(index, put):
        value = r.s_heads[index, :]

        @pl.loop(0, width // 512)
        def _(tile):
            span = window(tile, 512)
            put(span, dot(value, r.s_out[span, :], by_rows))

    def put_core(slot):
        def put(span, value):
            r.s_core_out[slot, :, span] = value.astype(low)

        return put

    def put_far(span, value):
        r.s_x_out[:, span] = (value + r.s_core_in[0, :, span].astype(full)).astype(low)

    def put_mine(span, value):
        r.s_part[:, span] = value + r.s_core_in[1, :, span].astype(full)

    branch(far_core, put_core(0))
    core_first = wire.push(r.s_core_out.at[0], r.s_core_in.at[0], dp, mp ^ 1)
    branch(core, put_core(1))
    core_second = wire.push(r.s_core_out.at[1], r.s_core_in.at[1], dp, mp ^ 1)
    core_first.wait_recv()
    branch(far, put_far)
    branch_far = wire.push(r.s_x_out, r.s_x_in, dp, mp ^ 2)
    tick(4, early)
    launch(5, over_z)
    core_second.wait_recv()
    branch(mine, put_mine)
    tick(4, late)
    launch(6, over_y)
    launch(5, over_y)
    launch(6, over_z)
    grad_far.wait_recv()
    grad_pass = wire.push(r.s_grads.at[far], r.s_grads.at[far], dp, mp ^ 1)
    branch_far.wait_recv()

    @pl.loop(0, rows // 64)
    def _(index):
        here = window(index, 64)
        there = pl.ds(pl.multiple_of(mp * rows + index * 64, 64), 64)
        value = r.s_hidden[there, :].astype(full) + (
            r.s_part[here, :] + r.s_x_in[here, :].astype(full)
        )
        r.s_middle[here, :] = value
        ratio = lax.rsqrt(jnp.mean(value * value, axis=-1, keepdims=True) + norm_eps)
        r.s_two[there, :] = (value * ratio * r.vectors[1:2, :]).astype(low)

    two_far = wire.push(r.s_two.at[mine], r.s_two.at[mine], dp, mp ^ 2)
    two_core = wire.push(r.s_two.at[mine], r.s_two.at[mine], dp, mp ^ 1)
    wire.store(r.s_middle, r.middle)
    tick(5, early)
    arrived(2)
    wire.store(r.s_up, r.up_all)

    def units_of(index):
        value = r.s_two[index, :]
        limit = r.s_widths[index, :] - mp * units

        @pl.loop(0, units // 512)
        def _(tile):
            span = window(tile, 512)
            pre_act = dot(value, r.s_up[:, span]) + r.vectors[3:4, span]
            unit = tile * 512 + lax.broadcasted_iota(jnp.int32, (1, 512), 1)
            on = unit < limit
            activated, slope = gelu_both(pre_act)
            r.s_act[index, span] = jnp.where(on, activated, 0.0).astype(low)
            r.s_slope[index, span] = jnp.where(on, slope, 0.0).astype(low)

    units_of(mine)
    two_far.wait_recv()
    two_pass = wire.push(r.s_two.at[far], r.s_two.at[far], dp, mp ^ 1)
    two_core.wait_recv()
    tick(6, [1])
    tick(5, late)
    units_of(core)
    tick(6, even)
    units_of(far)
    two_pass.wait_recv()
    units_of(far_core)
    tick(6, odd)
    wire.store(r.s_two, r.normed_two)
    wire.store(r.s_act, r.activated)
    wire.store(r.s_slope, r.slope)
    grad_core.wait_recv()
    grad_pass.wait_recv()
    own_grad.wait()
    wire.store(r.s_grads, r.grads)

    @pl.loop(0, width // 256)
    def _(tile):
        span = window(tile, 256)
        r.s_down[span, :] = dot(r.s_grads[:, span], r.s_act[...], by_tokens).astype(low)

    wire.store(r.s_down, r.grad_down)
    arrived(3)
    wire.close()
    for copy in route.values():
        copy.wait_send()
    for copy in small:
        copy.wait_send()
    for copy in (
        hidden_far,
        hidden_core,
        hidden_pass,
        grad_far,
        grad_core,
        grad_pass,
        core_first,
        core_second,
        branch_far,
        two_far,
        two_core,
        two_pass,
    ):
        copy.wait_send()


def run_forward(inputs, seqs):
    hidden, w_up, w_out, w_qkv = inputs["hidden"], inputs["w_up"], inputs["w_out"], inputs["w_qkv"]
    dp_size, mp_size = lax.axis_size("dp"), lax.axis_size("mp")
    rows, width = hidden.shape
    group = rows * mp_size
    units, lanes = w_up.shape[1], w_out.shape[1]
    shapes = dict(
        qkv_all=((3, width, lanes), low),
        out_all=((width, lanes), low),
        up_all=((width, units), low),
        down_all=((width, units), low),
        normed=((group, width), low),
        queries=((group, lanes), low),
        keys=((group, lanes), low),
        values=((group, lanes), low),
        heads=((group, lanes), low),
        middle=((rows, width), full),
        normed_two=((group, width), low),
        activated=((group, units), low),
        slope=((group, units), low),
        grads=((group, width), low),
        grad_down=((width, units), low),
        cosine=((group, HEAD), full),
        sine=((group, HEAD), full),
        vectors=((8, width), full),
    )
    remote = mp_size - 1 + dp_size - 1 + 7 * (dp_size - 1) + 16
    scratch = [
        pltpu.VMEM(shape, kind)
        for shape, kind in (
            ((group, width), low),
            ((group, width), low),
            ((3, width, lanes), low),
            ((width, lanes), low),
            ((width, units), low),
            ((group, lanes), low),
            ((group, lanes), low),
            ((group, lanes), low),
            ((group, lanes), low),
            ((group, HEAD), full),
            ((group, HEAD), full),
            ((dp_size, mp_size, 8, 128), full),
            ((group, 1), jnp.int32),
            ((group, 1), jnp.int32),
            ((2, rows, width), low),
            ((2, rows, width), low),
            ((rows, width), low),
            ((rows, width), low),
            ((rows, width), full),
            ((rows, width), full),
            ((group, width), low),
            ((group, units), low),
            ((group, units), low),
            ((group, width), low),
            ((width, units), low),
        )
    ] + [
        pltpu.SemaphoreType.DMA((remote,)),
        pltpu.SemaphoreType.DMA((remote,)),
        pltpu.SemaphoreType.DMA((32,)),
    ]
    anywhere = pl.BlockSpec(memory_space=pl.ANY)
    vector = pl.BlockSpec(memory_space=pltpu.VMEM)
    scalar = pl.BlockSpec(memory_space=pltpu.SMEM)
    placed = dict(
        gain_attn=vector,
        gain_ffn=vector,
        bias_down=vector,
        bias_up=vector,
        spread=vector,
        spread_up=vector,
        targets=vector,
        inverse=vector,
        lengths=scalar,
        grains=scalar,
        vectors=vector,
    )
    outs = pl.pallas_call(
        functools.partial(forward_kernel, seqs),
        out_shape=[jax.ShapeDtypeStruct(*shapes[name]) for name in ForwardOutputs._fields],
        in_specs=[placed.get(name, anywhere) for name in ForwardInputs._fields],
        out_specs=[placed.get(name, anywhere) for name in ForwardOutputs._fields],
        scratch_shapes=scratch,
        compiler_params=pltpu.CompilerParams(
            collective_id=0, has_side_effects=True, vmem_limit_bytes=vmem_bytes
        ),
        name="forward",
    )(*[inputs[name] for name in ForwardInputs._fields])
    return dict(zip(ForwardOutputs._fields, outs))


def small_tables(width, units, dp_size, mp_size):
    piece = width // (dp_size * mp_size)
    half = units // dp_size // 2
    lane = np.arange(128)[:, None]
    column = np.arange(width)[None, :]
    unit = np.arange(units)[None, :]
    spread = (column % piece == lane).astype(np.float32)
    spread_up = (unit % half == lane).astype(np.float32)
    targets = np.zeros((8, max(width, units)), np.int32)
    targets[0, :width] = column[0] // piece * 8
    targets[1, :units] = unit[0] // (2 * half) * (8 * mp_size) + 3 + unit[0] % (2 * half) // half
    return jnp.asarray(spread, low), jnp.asarray(spread_up, low), jnp.asarray(targets)


def rope_rows():
    index = np.arange(HEAD // 2, dtype=np.float32)
    inverse = np.float32(rope_base) ** (np.float32(-2.0) * index / np.float32(HEAD))
    table = np.zeros((8, HEAD), np.float32)
    table[0] = np.concatenate([inverse, inverse])
    table[1] = np.concatenate([-np.ones(HEAD // 2), np.ones(HEAD // 2)])
    return jnp.asarray(table)


class BackwardInputs(typing.NamedTuple):
    hidden: object
    lengths: object
    vectors: object
    cosine: object
    sine: object
    qkv_all: object
    out_all: object
    up_all: object
    down_all: object
    normed: object
    queries: object
    keys: object
    values: object
    heads: object
    middle: object
    normed_two: object
    activated: object
    slope: object
    grads: object
    grad_down: object


class BackwardOutputs(typing.NamedTuple):
    output: object
    grad_in: object
    own_qkv: object
    own_out: object
    own_up: object
    totals: object
    last_qkv: object
    last_out: object
    last_up: object
    last_down: object


class BackwardScratch(typing.NamedTuple):
    s_weights: object
    s_up: object
    s_slope: object
    s_grads: object
    s_two: object
    s_act: object
    s_pre: object
    s_own: object
    got_qkv: object
    got_out: object
    got_up: object
    got_down: object
    s_gqkv: object
    s_gout: object
    s_core_in: object
    s_x_in: object
    s_core_out: object
    s_x_out: object
    s_part: object
    s_middle: object
    s_back: object
    s_gheads: object
    s_gk: object
    s_gv: object
    s_cos: object
    s_sin: object
    s_hidden: object
    s_output: object
    s_sums: object
    s_vec: object
    s_vec_mp: object
    s_vec_y: object
    s_vec_z: object
    sent: object
    got: object
    local: object


def backward_kernel(seqs, *refs):
    r = types.SimpleNamespace(
        **dict(zip(BackwardInputs._fields + BackwardOutputs._fields + BackwardScratch._fields, refs, strict=True))
    )
    dp, mp = lax.axis_index("dp"), lax.axis_index("mp")
    dp_size, mp_size = lax.axis_size("dp"), lax.axis_size("mp")
    rings = dp_size // 2
    rows, width = r.hidden.shape
    group = rows * mp_size
    shard = width // dp_size
    units = r.slope.shape[1]
    lanes = r.heads.shape[1]
    heads = lanes // HEAD
    scale = HEAD ** (-0.5)
    wire = Wire(r.sent, r.got, r.local)
    sends = []

    def block(index):
        return window(index, rows)

    def push(source, target, to_dp, to_mp):
        copy = wire.push(source, target, to_dp, to_mp)
        sends.append(copy)
        return copy

    def sent(*copies):
        for copy in copies:
            copy.wait_send()
            sends[:] = [other for other in sends if other is not copy]

    mine, core, far, far_core = block(mp), block(mp ^ 1), block(mp ^ 2), block(mp ^ 3)

    barrier = pltpu.get_barrier_semaphore()
    for step in range(1, mp_size):
        pl.semaphore_signal(barrier, inc=1, device_id=(dp, mp ^ step), device_id_type=MESH)
    pl.semaphore_signal(barrier, inc=1, device_id=(dp ^ 1, mp), device_id_type=MESH)
    for step in range(1, rings):
        pl.semaphore_signal(barrier, inc=1, device_id=(dp ^ (2 * step), mp), device_id_type=MESH)
    pl.semaphore_wait(barrier, mp_size + rings - 1)

    local = dict(down=r.grad_down, up=r.s_up, out=r.s_gout, qkv=r.s_gqkv)
    landing = dict(down=r.got_down, up=r.got_up, out=r.got_out, qkv=r.got_qkv)
    final = dict(down=r.last_down, up=r.last_up, out=r.last_out, qkv=r.last_qkv)
    pieces = [("down", kind) + span for kind, span in zip("yz", cut(shard, 0, 0.5, 1), strict=True)]
    pieces += [("up", "z") + span for span in cut(shard, 0, 0.5, 1)]
    pieces += [("out", "z", 0, shard)]
    pieces += [("qkv", "z") + span for span in cut(shard, 0, 0.5, 1)]
    inner, leaves, middle_slots, route, own = {}, {}, {}, {}, {}
    for kind in "zy":
        found = [0]
        for k in found:
            found += [k ^ step for step in onward(kind, k, dp_size)]
        inner[kind] = [k for k in found if onward(kind, k, dp_size)]
        leaves[kind] = [k for k in found[::-1] if not onward(kind, k, dp_size)]
        pairs = [(k, step) for k in inner[kind][1:] for step in onward(kind, k, dp_size)]
        middle_slots[kind] = {pair: place for place, pair in enumerate(pairs)}

    def rows_of(index, k):
        name, kind, first, count = pieces[index]
        return pl.ds(pl.multiple_of((dp ^ k) * shard + first, 16), count)

    def spot(index, k, step):
        name, kind, first, count = pieces[index]
        span = pl.ds(first, count)
        if k == 0:
            return final[name].at[onward(kind, 0, dp_size).index(step), span]
        return landing[name].at[middle_slots[kind][k, step], span]

    def climb(index, k, source):
        kind = pieces[index][1]
        step = last_step(kind, k, dp_size)
        route[index, k ^ step, step] = push(source, spot(index, k ^ step, step), dp ^ step, mp)

    def launch(index, *ks):
        for k in ks:
            climb(index, k, local[pieces[index][0]].at[rows_of(index, k)])

    def launch_both(first, second, ks):
        for k in ks:
            launch(first, k)
            launch(second, k)

    def own_load(index):
        name, kind, first, count = pieces[index]
        for place, k in enumerate(inner[kind][1:]):
            own[index, k] = wire.move(
                local[name].at[rows_of(index, k)], r.s_own.at[place, pl.ds(first, count)]
            )

    def own_part(index, k, start, count):
        name, kind, first, _ = pieces[index]
        if name == "down":
            return r.s_own[inner[kind].index(k) - 1, pl.ds(first + start, count), :].astype(full)
        place = pl.multiple_of((dp ^ k) * shard + first + start, 16)
        return local[name][pl.ds(place, count), :].astype(full)

    def tick(index, *ks):
        name, kind, first, count = pieces[index]
        part = 48 if count % 48 == 0 else 16
        for k in ks:
            steps = onward(kind, k, dp_size)
            for step in steps:
                route[index, k, step].wait_recv()
            if name == "down":
                own[index, k].wait()

            @pl.loop(0, count // part)
            def _(turn_index):
                start = pl.multiple_of(turn_index * part, 16)
                here = pl.ds(pl.multiple_of(first + start, 16), part)
                total = own_part(index, k, start, part)
                for step in steps:
                    slot_index = middle_slots[kind][k, step]
                    total = total + landing[name][slot_index, here, :].astype(full)
                landing[name][middle_slots[kind][k, steps[0]], here, :] = total.astype(low)

            climb(index, k, spot(index, k, steps[0]))

    def finish(index):
        kind = pieces[index][1]
        for step in onward(kind, 0, dp_size):
            route[index, 0, step].wait_recv()

    def reduce_start(left, right, columns, slot_in):
        def product(index, put):
            value = left[index, columns]

            @pl.loop(0, width // 512)
            def _(tile):
                span = window(tile, 512)
                put(span, dot(value, right[span, columns], by_rows))

        def put_core(place):
            def put(span, value):
                r.s_core_out[place, :, span] = value.astype(low)

            return put

        def put_far(span, value):
            value = value + r.s_core_in[slot_in, 0, :, span].astype(full)
            r.s_x_out[slot_in, :, span] = value.astype(low)

        def put_mine(span, value):
            r.s_part[:, span] = value + r.s_core_in[slot_in, 1, :, span].astype(full)

        def first():
            product(far_core, put_core(0))
            one = push(r.s_core_out.at[0], r.s_core_in.at[slot_in, 0], dp, mp ^ 1)
            product(core, put_core(1))
            two = push(r.s_core_out.at[1], r.s_core_in.at[slot_in, 1], dp, mp ^ 1)
            return one, two

        def second(one):
            one.wait_recv()
            product(far, put_far)

        def third(two):
            two.wait_recv()
            product(mine, put_mine)

        return first, second, third

    tiles = [pl.ds(start, 512) for start in range(0, units, 512)]
    load_grads = wire.move(r.grads, r.s_grads)
    load_tiles = [
        [
            wire.move(r.down_all.at[:, span], r.s_weights.at[:, span]),
            wire.move(r.slope.at[:, span], r.s_slope.at[:, span]),
        ]
        for span in tiles
    ]
    for one, two in zip(leaves["y"], leaves["z"], strict=True):
        launch(0, one)
        launch(1, two)
    load_up = wire.move(r.up_all, r.s_up)
    load_two = wire.move(r.normed_two, r.s_two)
    load_act = wire.move(r.activated, r.s_act)
    load_middle = wire.move(r.middle, r.s_middle)
    own_load(1)
    own_load(0)
    load_rest = [
        wire.move(r.cosine, r.s_cos),
        wire.move(r.sine, r.s_sin),
        wire.move(r.hidden, r.s_hidden),
    ]
    r.s_sums[...] = jnp.zeros_like(r.s_sums)
    load_grads.wait()

    for span, loads in zip(tiles, load_tiles):
        for copy in loads:
            copy.wait()
        value = dot(r.s_grads[...], r.s_weights[:, span]) * r.s_slope[:, span].astype(full)
        value = value.astype(low)
        r.s_pre[:, span] = value
        r.s_sums[3:4, span] = jnp.sum(value.astype(full), axis=0, keepdims=True)

    early = [k for k in inner["z"][:0:-1] if len(onward("z", k, dp_size)) == 1]
    late = [k for k in inner["z"][:0:-1] if k not in early]
    early_y = [k for k in inner["y"][:0:-1] if len(onward("y", k, dp_size)) == 1]
    late_y = [k for k in inner["y"][:0:-1] if k not in early_y]
    load_up.wait()
    everything = pl.ds(0, units)
    first, second, third = reduce_start(r.s_pre, r.s_up, everything, 0)
    one, two = first()
    second(one)
    two_far = push(r.s_x_out.at[0], r.s_x_in.at[0], dp, mp ^ 2)
    third(two)
    load_two.wait()

    @pl.loop(0, width // 256)
    def _(tile):
        span = window(tile, 256)
        r.s_up[span, :] = dot(r.s_two[:, span], r.s_pre[...], by_tokens).astype(low)

    launch_both(2, 3, leaves["z"])
    tick(1, *early)
    tick(0, *early_y)
    load_heads = [
        wire.move(place, r.s_two.at[:, pl.ds(index * lanes, lanes)])
        for index, place in enumerate((r.queries, r.keys, r.values, r.heads))
    ]
    load_middle.wait()
    two_far.wait_recv()

    @pl.loop(0, rows // 64)
    def _(index):
        here = window(index, 64)
        there = pl.ds(pl.multiple_of(mp * rows + index * 64, 64), 64)
        normed_grad = r.s_part[here, :] + r.s_x_in[0, here, :].astype(full)
        middle = r.s_middle[here, :]
        grad = r.s_grads[there, :].astype(full)
        ratio = lax.rsqrt(jnp.mean(middle * middle, axis=-1, keepdims=True) + norm_eps)
        weighted = normed_grad * r.vectors[1:2, :]
        back = (
            grad
            + ratio * weighted
            - middle * (ratio**3 * jnp.mean(weighted * middle, axis=-1, keepdims=True))
        )
        r.s_back[here, :] = back
        r.s_slope[there, :] = back.astype(low)
        r.s_sums[1:2, :] += jnp.sum(normed_grad * (middle * ratio), axis=0, keepdims=True)
        r.s_sums[2:3, :] += jnp.sum(grad, axis=0, keepdims=True)

    branch_far = push(r.s_slope.at[mine], r.s_slope.at[mine], dp, mp ^ 2)
    branch_core = push(r.s_slope.at[mine], r.s_slope.at[mine], dp, mp ^ 1)
    load_normed = wire.move(r.normed, r.s_grads)

    load_act.wait()
    first, second, third = reduce_start(r.s_act, r.s_weights, everything, 1)
    sent(one, two)
    one, two = first()
    second(one)
    ffn_far = push(r.s_x_out.at[1], r.s_x_in.at[1], dp, mp ^ 2)
    third(two)
    load_weights = [
        wire.move(r.qkv_all.at[part], r.s_weights.at[:, pl.ds(part * lanes, lanes)])
        for part in range(3)
    ] + [
        wire.move(r.out_all, r.s_weights.at[:, pl.ds(3 * lanes, lanes)]),
    ]
    tick(1, *late)
    tick(2, *early)
    tick(0, *late_y)
    tick(3, *early)
    branch_far.wait_recv()
    branch_pass = push(r.s_slope.at[far], r.s_slope.at[far], dp, mp ^ 1)
    branch_core.wait_recv()
    for copy in load_heads + load_weights:
        copy.wait()
    branch_pass.wait_recv()
    to_heads = pl.ds(3 * lanes, lanes)

    @pl.loop(0, width // 512)
    def _(tile):
        span = window(tile, 512)
        r.s_gout[span, :] = dot(r.s_slope[:, span], r.s_two[:, to_heads], by_tokens).astype(low)

    launch(4, *leaves["z"])

    @pl.loop(0, group // 512)
    def _(tile):
        here = window(tile, 512)
        r.s_gheads[here, :] = dot(r.s_slope[here, :], r.s_weights[:, to_heads]).astype(low)


    for copy in load_rest:
        copy.wait()
    token = lax.broadcasted_iota(jnp.int32, (group, 1), 0)
    first_token = jnp.int32(0)
    starts = jnp.zeros((group, 1), jnp.int32)
    for seq in range(seqs):
        starts = jnp.where(token >= first_token, first_token, starts)
        first_token = first_token + r.lengths[0, seq]

    @pl.loop(0, heads)
    def _(head):
        span = window(head, HEAD)
        k_span = pl.ds(pl.multiple_of(lanes + head * HEAD, HEAD), HEAD)
        v_span = pl.ds(pl.multiple_of(2 * lanes + head * HEAD, HEAD), HEAD)
        for index in reversed(range(mp_size)):
            here = pl.ds(index * rows, rows)
            seen = pl.ds(0, (index + 1) * rows)
            query, grad = r.s_two[here, span], r.s_gheads[here, span]
            begin = starts[index * rows : (index + 1) * rows]
            probs = softmax_rows(query, r.s_two[seen, k_span], begin, index * rows, scale)
            grad_probs = dot(grad, r.s_two[seen, v_span], by_rows)
            inner = jnp.sum(probs * grad_probs, axis=-1, keepdims=True)
            grad_scores = (probs * (grad_probs - inner)).astype(low)
            query_grad = dot(grad_scores, r.s_two[seen, k_span]) * scale
            r.s_act[here, span] = turn(
                query_grad, r.s_cos[here, :], -r.s_sin[here, :]
            ).astype(low)
            key_part = dot(grad_scores, query, by_tokens)
            value_part = dot(probs.astype(low), grad, by_tokens)
            if index == mp_size - 1:
                r.s_gk[...] = key_part
                r.s_gv[...] = value_part
            else:
                r.s_gk[seen, :] += key_part
                r.s_gv[seen, :] += value_part
        for index in range(mp_size):
            here = pl.ds(index * rows, rows)
            r.s_act[here, k_span] = turn(
                r.s_gk[here, :] * scale, r.s_cos[here, :], -r.s_sin[here, :]
            ).astype(low)
            r.s_act[here, v_span] = r.s_gv[here, :].astype(low)

    tick(2, *late)

    mixed = pl.ds(0, 3 * lanes)
    first, second, third = reduce_start(r.s_act, r.s_weights, mixed, 0)
    sent(one, two, two_far)
    ffn_far.wait_recv()

    @pl.loop(0, rows // 64)
    def _(index):
        here = window(index, 64)
        value = r.s_part[here, :] + r.s_x_in[1, here, :].astype(full)
        r.s_output[here, :] = (r.s_middle[here, :] + value + r.vectors[2:3, :]).astype(low)

    wire.store(r.s_output, r.output)
    one, two = first()
    second(one)
    one_far = push(r.s_x_out.at[0], r.s_x_in.at[0], dp, mp ^ 2)
    third(two)
    tick(3, *late)
    load_normed.wait()

    @pl.loop(0, width // 256)
    def _(tile):
        span = window(tile, 256)
        r.s_gqkv[span, :] = dot(r.s_grads[:, span], r.s_act[:, mixed], by_tokens).astype(low)

    first_leaves, second_leaves = leaves["z"][:-2], leaves["z"][-2:-1]
    launch(5, *first_leaves)
    launch(6, *first_leaves)
    launch_both(5, 6, second_leaves)
    own_slot = window(dp, shard)
    wire.store(r.s_gqkv.at[own_slot], r.own_qkv)
    wire.store(r.s_gout.at[own_slot], r.own_out)
    wire.store(r.s_up.at[own_slot], r.own_up)
    tick(4, *early)
    one_far.wait_recv()

    @pl.loop(0, rows // 64)
    def _(index):
        here = window(index, 64)
        normed_grad = r.s_part[here, :] + r.s_x_in[0, here, :].astype(full)
        hidden = r.s_hidden[here, :].astype(full)
        ratio = lax.rsqrt(jnp.mean(hidden * hidden, axis=-1, keepdims=True) + norm_eps)
        weighted = normed_grad * r.vectors[0:1, :]
        r.s_back[here, :] = (
            r.s_back[here, :]
            + ratio * weighted
            - hidden * (ratio**3 * jnp.mean(weighted * hidden, axis=-1, keepdims=True))
        )
        r.s_sums[0:1, :] += jnp.sum(normed_grad * (hidden * ratio), axis=0, keepdims=True)

    wire.store(r.s_back, r.grad_in)

    lines = width // 128
    for line in range(4):
        for index in range((units if line == 3 else width) // 128):
            r.s_vec[line * lines + index : line * lines + index + 1, :] = r.s_sums[
                line : line + 1, index * 128 : (index + 1) * 128
            ]
    shared = 3 * lines
    vec_mp = [
        push(r.s_vec.at[pl.ds(0, shared)], r.s_vec_mp.at[step - 1], dp, mp ^ step)
        for step in range(1, mp_size)
    ]
    tick(4, *late)
    for copy in vec_mp:
        copy.wait_recv()
    sent(*vec_mp)
    for step in range(1, mp_size):
        r.s_vec[0:shared, :] += r.s_vec_mp[step - 1]
    vec_y = push(r.s_vec, r.s_vec_y, dp ^ 1, mp)
    launch_both(5, 6, leaves["z"][-1:])
    tick(5, *early)
    tick(6, *early)
    tick(5, *late)
    vec_y.wait_recv()
    sent(vec_y)
    r.s_vec[...] += r.s_vec_y[...]
    vec_z = [
        push(r.s_vec, r.s_vec_z.at[step - 1], dp ^ (2 * step), mp) for step in range(1, rings)
    ]
    tick(6, *late)
    for copy in vec_z:
        copy.wait_recv()
    total = r.s_vec[...]
    for step in range(1, rings):
        total = total + r.s_vec_z[step - 1]
    r.totals[...] = total
    for index in range(len(pieces)):
        finish(index)
    wire.close()
    for copy in sends:
        copy.wait_send()


def run_backward(inputs, seqs):
    dp_size, mp_size = lax.axis_size("dp"), lax.axis_size("mp")
    rings = dp_size // 2
    rows, width = inputs["hidden"].shape
    group, units = inputs["slope"].shape
    lanes = inputs["heads"].shape[1]
    shard = width // dp_size
    vec_rows = (3 * width + units) // 128
    steps = len(onward("z", 0, dp_size))
    between = dp_size - 1 - steps
    shapes = dict(
        output=((rows, width), low),
        grad_in=((rows, width), full),
        own_qkv=((shard, 3 * lanes), low),
        own_out=((shard, lanes), low),
        own_up=((shard, units), low),
        totals=((vec_rows, 128), full),
        last_qkv=((steps, shard, 3 * lanes), low),
        last_out=((steps, shard, lanes), low),
        last_up=((steps, shard, units), low),
        last_down=((steps, shard, units), low),
    )
    scratch = [
        pltpu.VMEM(shape, kind)
        for shape, kind in (
            ((width, max(units, 4 * lanes)), low),
            ((width, units), low),
            ((group, max(units, width)), low),
            ((group, width), low),
            ((group, max(width, 4 * lanes)), low),
            ((group, max(units, 3 * lanes)), low),
            ((group, units), low),
            ((rings - 1, shard, units), low),
            ((between, shard, 3 * lanes), low),
            ((between, shard, lanes), low),
            ((between, shard, units), low),
            ((between, shard, units), low),
            ((width, 3 * lanes), low),
            ((width, lanes), low),
            ((2, 2, rows, width), low),
            ((2, rows, width), low),
            ((2, rows, width), low),
            ((2, rows, width), low),
            ((rows, width), full),
            ((rows, width), full),
            ((rows, width), full),
            ((group, lanes), low),
            ((group, HEAD), full),
            ((group, HEAD), full),
            ((group, HEAD), full),
            ((group, HEAD), full),
            ((rows, width), low),
            ((rows, width), low),
            ((8, max(width, units)), full),
            ((vec_rows, 128), full),
            ((mp_size - 1, 3 * width // 128, 128), full),
            ((vec_rows, 128), full),
            ((rings - 1, vec_rows, 128), full),
        )
    ]
    remote = 7 * (dp_size - 1) + 9 + 3 + mp_size + rings
    scratch += [
        pltpu.SemaphoreType.DMA((remote,)),
        pltpu.SemaphoreType.DMA((remote,)),
        pltpu.SemaphoreType.DMA((40 + 2 * rings + 7 * steps,)),
    ]
    anywhere = pl.BlockSpec(memory_space=pl.ANY)
    vector = pl.BlockSpec(memory_space=pltpu.VMEM)
    placed = dict(
        lengths=pl.BlockSpec(memory_space=pltpu.SMEM), vectors=vector, totals=vector
    )
    outs = pl.pallas_call(
        functools.partial(backward_kernel, seqs),
        out_shape=[jax.ShapeDtypeStruct(*shapes[name]) for name in BackwardOutputs._fields],
        in_specs=[placed.get(name, anywhere) for name in BackwardInputs._fields],
        out_specs=[placed.get(name, anywhere) for name in BackwardOutputs._fields],
        scratch_shapes=scratch,
        compiler_params=pltpu.CompilerParams(
            collective_id=1, has_side_effects=True, vmem_limit_bytes=vmem_bytes
        ),
        name="backward",
    )(*[inputs[name] for name in BackwardInputs._fields])
    return dict(zip(BackwardOutputs._fields, outs))


class CollectInputs(typing.NamedTuple):
    output: object
    grad_in: object
    grad_down: object
    own_qkv: object
    own_out: object
    own_up: object
    last_qkv: object
    last_out: object
    last_up: object
    last_down: object
    totals: object


class CollectOutputs(typing.NamedTuple):
    output: object
    grad_in: object
    sum_qkv: object
    sum_out: object
    sum_up: object
    sum_down: object
    gain_one: object
    gain_two: object
    down_bias: object
    up_bias: object


def collect_kernel(piece, pieces, *refs):
    names = [name + "_in" for name in CollectInputs._fields] + list(CollectOutputs._fields)
    names += [
        "s_qkv", "s_out", "s_up", "s_down", "t_qkv", "t_out", "t_up", "t_down", "s_output",
        "s_grad_in", "local",
    ]
    r = types.SimpleNamespace(**dict(zip(names, refs, strict=True)))
    dp, mp = lax.axis_index("dp"), lax.axis_index("mp")
    shard = r.s_up.shape[1]
    wire = Wire(None, None, r.local)
    own = [r.grad_down_in.at[window(dp, shard)], r.own_up_in, r.own_qkv_in, r.own_out_in]
    last = [r.last_down_in, r.last_up_in, r.last_qkv_in, r.last_out_in]
    parts = [r.s_down, r.s_up, r.s_qkv, r.s_out]
    sums = [r.t_down, r.t_up, r.t_qkv, r.t_out]
    results = [r.sum_down, r.sum_up, r.sum_qkv, r.sum_out]
    loads = []
    for index in range(4):
        count = last[index].shape[0]
        loads.append(
            [
                wire.move(last[index], parts[index].at[pl.ds(0, count)]),
                wire.move(own[index], parts[index].at[count]),
            ]
        )
    through = [
        (wire.move(r.output_in, r.s_output), r.s_output, r.output),
        (wire.move(r.grad_in_in, r.s_grad_in), r.s_grad_in, r.grad_in),
    ]
    for line, place in enumerate((r.gain_one, r.gain_two, r.down_bias)):
        start = (dp * lax.axis_size("mp") + mp) * piece
        row = start // 128 + line * (r.output.shape[1] // 128)
        lane = start % 128
        pair = jnp.concatenate(
            [r.totals_in[pl.ds(row, 1), :], r.totals_in[pl.ds(row + 1, 1), :]], axis=1
        )
        pair = pltpu.roll(jnp.broadcast_to(pair, (8, 256)), (256 - lane) % 256, 1)
        place[...] = pair[0:1, :piece].reshape(piece)
    start = dp * pieces
    row = start // 128 + 3 * (r.output.shape[1] // 128)
    lane = start % 128
    last_row = r.totals_in.shape[0] - 1
    pair = jnp.concatenate(
        [
            r.totals_in[pl.ds(row, 1), :],
            r.totals_in[pl.ds(jnp.minimum(row + 1, last_row), 1), :],
        ],
        axis=1,
    )
    pair = pltpu.roll(jnp.broadcast_to(pair, (8, 256)), (256 - lane) % 256, 1)
    r.up_bias[...] = pair[0:1, :pieces].reshape(pieces)
    for copy, source, target in through:
        copy.wait()
        wire.store(source, target)
    for index in range(4):
        for copy in loads[index]:
            copy.wait()
        count = parts[index].shape[0]

        @pl.loop(0, shard // 16)
        def _(step):
            here = window(step, 16)
            total = parts[index][0, here, :].astype(full)
            for place in range(1, count):
                total = total + parts[index][place, here, :].astype(full)
            sums[index][here, :] = total

        if index == 2:
            lanes = results[index].shape[2]
            for part in range(3):
                wire.store(
                    sums[index].at[:, pl.ds(part * lanes, lanes)], results[index].at[part]
                )
        else:
            wire.store(sums[index], results[index])
    wire.close()


def collect(inputs, piece, pieces):
    rows, width = inputs["output"].shape
    steps, shard, units = inputs["last_up"].shape
    lanes = inputs["last_out"].shape[2]
    shapes = dict(
        output=((rows, width), low),
        grad_in=((rows, width), full),
        sum_qkv=((3, shard, lanes), full),
        sum_out=((shard, lanes), full),
        sum_up=((shard, units), full),
        sum_down=((shard, units), full),
        gain_one=((piece,), full),
        gain_two=((piece,), full),
        down_bias=((piece,), full),
        up_bias=((pieces,), full),
    )
    scratch = [
        pltpu.VMEM(shape, kind)
        for shape, kind in (
            ((steps + 1, shard, 3 * lanes), low),
            ((steps + 1, shard, lanes), low),
            ((steps + 1, shard, units), low),
            ((steps + 1, shard, units), low),
            ((shard, 3 * lanes), full),
            ((shard, lanes), full),
            ((shard, units), full),
            ((shard, units), full),
            ((rows, width), low),
            ((rows, width), full),
        )
    ] + [pltpu.SemaphoreType.DMA((20,))]
    anywhere = pl.BlockSpec(memory_space=pl.ANY)
    vector = pl.BlockSpec(memory_space=pltpu.VMEM)
    placed = dict(
        totals=vector, gain_one=vector, gain_two=vector, down_bias=vector, up_bias=vector
    )
    outs = pl.pallas_call(
        functools.partial(collect_kernel, piece, pieces),
        out_shape=[jax.ShapeDtypeStruct(*shapes[name]) for name in CollectOutputs._fields],
        in_specs=[placed.get(name, anywhere) for name in CollectInputs._fields],
        out_specs=[placed.get(name, anywhere) for name in CollectOutputs._fields],
        scratch_shapes=scratch,
        compiler_params=pltpu.CompilerParams(vmem_limit_bytes=vmem_bytes),
        name="collect",
    )(*[inputs[name] for name in CollectInputs._fields])
    return dict(zip(CollectOutputs._fields, outs))


def shards(
    hidden_in,
    out_grad,
    seq_lengths,
    seq_grains,
    gain_attn,
    w_qkv,
    w_out,
    gain_ffn,
    w_up,
    bias_up,
    w_down,
    bias_down,
):
    dp, mp = lax.axis_index("dp"), lax.axis_index("mp")
    dp_size, mp_size = lax.axis_size("dp"), lax.axis_size("mp")
    width = hidden_in.shape[1]
    units = w_up.shape[1]
    seqs = seq_lengths.shape[1]
    spread, spread_up, targets = small_tables(width, units, dp_size, mp_size)
    done = run_forward(
        dict(
            hidden=hidden_in,
            grad=out_grad,
            w_qkv=w_qkv.transpose(1, 0, 2),
            w_out=w_out.T,
            w_up=w_up,
            w_down=w_down.T,
            gain_attn=gain_attn,
            gain_ffn=gain_ffn,
            bias_down=bias_down,
            bias_up=bias_up,
            spread=spread,
            spread_up=spread_up,
            targets=targets,
            inverse=rope_rows(),
            lengths=seq_lengths,
            grains=seq_grains,
        ),
        seqs,
    )
    back = run_backward(dict(done, hidden=hidden_in, lengths=seq_lengths), seqs)
    piece, pieces = gain_attn.shape[0], bias_up.shape[0]
    ends = collect(dict(back, grad_down=done["grad_down"]), piece, pieces)
    return (
        ends["output"],
        ends["grad_in"],
        ends["gain_one"],
        ends["sum_qkv"].transpose(1, 0, 2),
        ends["sum_out"].T,
        ends["gain_two"],
        ends["sum_up"],
        ends["up_bias"],
        ends["sum_down"].T,
        ends["down_bias"],
    )


def solution(mesh):
    return jax.shard_map(
        shards,
        mesh=mesh,
        in_specs=(
            P(("dp", "mp"), None),
            P(("dp", "mp"), None),
            P("dp", None),
            P("dp", None),
            P(("dp", "mp")),
            P("dp", None, "mp"),
            P("mp", "dp"),
            P(("dp", "mp")),
            P("dp", "mp"),
            P(("mp", "dp")),
            P("mp", "dp"),
            P(("dp", "mp")),
        ),
        out_specs=(
            P(("dp", "mp"), None),
            P(("dp", "mp"), None),
            P(("dp", "mp")),
            P("dp", None, "mp"),
            P("mp", "dp"),
            P(("dp", "mp")),
            P("dp", "mp"),
            P(("mp", "dp")),
            P("mp", "dp"),
            P(("dp", "mp")),
        ),
        check_vma=False,
    )
```
